256 devices in a mesh: seq: 32 (over z_lo, x, core), samp: 8 (over y, z_hi).
Axes of the slice: x: 4, y: 4, z: 8 (z_hi: 2, z_lo: 4; z = z_hi * 4 + z_lo), core: 2. Of those that a mesh axis runs over, the one named last changes fastest.
Arguments:
- atoms_in: bfloat16 [8, 8192, 128], P('samp', 'seq'), may hold values from -6 to 6
- pair_feats: bfloat16 [256, 16, 32, 128], P('seq'), may hold values from -3 to 3
- window_shift: int32 [256], P('seq'), may hold values from -64 to -32
- atom_token: int32 [8192], P('seq'), may hold values from 0 to 1023, as said below
- token_counts: int32 [1024], P('seq'), may hold values from 1 to 15, as said below
- token_grad: bfloat16 [8, 1024, 384], P('samp', 'seq'), may hold values from -6 to 6
- norm_gain: float32 [2, 128], replicated, may hold values from 0.1 to 1.9
- weight_in: bfloat16 [2, 128, 512], replicated, may hold values from -0.5 to 0.5
- weight_out: bfloat16 [2, 128, 128], replicated, may hold values from -0.5 to 0.5
- weight_bias: float32 [2, 16, 4], replicated, may hold values from -1.5 to 1.5
- weight_token: bfloat16 [128, 384], replicated, may hold values from -0.5 to 0.5
Outputs:
- grad_atoms: bfloat16 [8, 8192, 128], P('samp', 'seq')
- grad_pair: bfloat16 [256, 16, 32, 128], P(('seq', 'samp'))
- grad_gain: float32 [2, 128], replicated
- grad_weight_in: float32 [2, 128, 512], replicated
- grad_weight_out: float32 [2, 128, 128], replicated
- grad_weight_bias: float32 [2, 16, 4], replicated
- grad_weight_token: float32 [128, 384], replicated
The draws below stay inside these ranges and needn't reach their ends.
Inputs may be any that keep to these rules, and one draw needn't show every extreme that they name: atom_token never falls and names for each atom the token whose atoms include it; token t has token_counts[t] atoms, all of them together. Atoms k*256 to (k+1)*256 - 1 belong to tokens k*32 - 1 to (k+1)*32 - 1, and for k > 0 the first of them to token k*32 - 1. `token_counts`: the counts add up to 8192.
All inputs are finite; a program needn't handle non-finite values.
Results may differ from the reference program's by a relative error of at most 0.02.
Values may be sent and summed in bfloat16 or wider, within the bound.
No kernel may reach another device: no remote copies, remote signals or barrier semaphores. Data moves between devices by JAX's collectives and lax.ppermute only.
A program may use at most 64 MiB of HBM per device.

```python
import jax
import jax.numpy as jnp
from jax import lax

C = 128
HEADS = 4
PC = 16
TC = 384
QBLK = 32
KWIN = 128
HALO = 64
BLOCKS = 2
TOK_DEV = 32
SAMPLES = 8
ATOMS = 8192
TOKENS = 1024
QBLOCKS = 256


def token_layout(key):
    count_pairs = (TOKENS - 2) // 2
    size_key, sign_key = jax.random.split(key)
    sizes = jax.random.randint(size_key, (count_pairs,), 1, 8, dtype=jnp.int32)
    signs = jax.random.randint(sign_key, (count_pairs,), 0, 2, dtype=jnp.int32) * 2 - 1
    second = 2 * jnp.arange(count_pairs, dtype=jnp.int32) + 2
    signs = jnp.where(second % TOK_DEV == 0, 1, signs)
    sizes = sizes.at[0].set(7)
    signs = signs.at[0].set(1)
    change = sizes * signs
    counts = jnp.full((TOKENS,), 8, jnp.int32)
    counts = counts.at[1:TOKENS - 2:2].add(change)
    counts = counts.at[2:TOKENS - 1:2].add(-change)
    return counts


def draw_token_counts(key, part):
    counts = token_layout(key)
    return counts


def draw_atom_token(key, part):
    counts = token_layout(key)
    ends = jnp.cumsum(counts)
    positions = jnp.arange(ATOMS, dtype=jnp.int32)
    return jnp.searchsorted(ends, positions, side='right').astype(jnp.int32)


def plant(result, rng, smallest, largest):
    dims = result.shape
    place = [jax.random.randint(jax.random.fold_in(rng, axis), (), 0, dims[axis]) for axis in range(len(dims))]
    result = result.at[tuple(place)].set(smallest)
    longest = dims.index(max(dims))
    place[longest] = (place[longest] + 1) % dims[longest]
    return result.at[tuple(place)].set(largest)


def level_of(key, shape, shards, smallest, largest):
    level, own = 1.0, jax.random.fold_in(key, 6)
    for position, parts in shards:
        heights = jnp.exp(jax.random.uniform(jax.random.fold_in(own, position), (parts,), jnp.float32, smallest / len(shards), largest / len(shards)))
        level = level * jnp.repeat(heights, shape[position] // parts).reshape([-1 if axis == position else 1 for axis in range(len(shape))])
    return level


def normal_values(stream_key, dims, scale, limit, cuts=(), kind=jnp.bfloat16):
    factor_of = level_of(stream_key, dims, cuts, -0.22, 0.18) if cuts else 1.0
    entries = jax.random.normal(stream_key, dims, jnp.float32) * scale * factor_of
    return jnp.minimum(jnp.maximum(entries, -limit), limit).astype(kind)


def setup_inputs(seed: int = 0) -> dict:
    splits = jax.random.split(jax.random.key(seed), 12)
    return {
        "atoms_in": normal_values(splits[0], (SAMPLES, ATOMS, C), 1.0, 6.0, ((0, 8), (1, 32))),
        "pair_feats": normal_values(splits[1], (QBLOCKS, PC, QBLK, KWIN), 1.0, 3.0, ((0, 32),)),
        "window_shift": plant(jax.random.randint(splits[2], (QBLOCKS,), -HALO, QBLK + HALO - KWIN + 1), jax.random.fold_in(splits[2], 1), -HALO, QBLK + HALO - KWIN).astype(jnp.int32),
        "atom_token": draw_atom_token(jax.random.fold_in(splits[11], 71), 0),
        "token_counts": draw_token_counts(jax.random.fold_in(splits[11], 71), 0),
        "token_grad": normal_values(splits[5], (SAMPLES, TOKENS, TC), 1.0, 6.0, ((0, 8), (1, 32))),
        "norm_gain": jnp.clip(1.0 + 0.18 * jax.random.normal(splits[6], (BLOCKS, C), jnp.float32), 0.1, 1.9),
        "weight_in": normal_values(splits[7], (BLOCKS, C, 4 * C), C ** -0.5, 0.5),
        "weight_out": normal_values(splits[8], (BLOCKS, C, C), C ** -0.5, 0.5),
        "weight_bias": normal_values(splits[9], (BLOCKS, PC, HEADS), PC ** -0.5, 1.5, (), jnp.float32),
        "weight_token": normal_values(splits[10], (C, TC), C ** -0.5, 0.5),
    }


EPSILON = 1e-05
highest = lax.Precision.HIGHEST

def narrow(value):
    return lax.optimization_barrier(value.astype(jnp.bfloat16)).astype(jnp.float32)

def normalize(state, gain):
    centred = state - lax.optimization_barrier(jnp.mean(state, -1, keepdims=True))
    variance = lax.optimization_barrier(jnp.mean(centred * centred, -1, keepdims=True))
    return narrow(centred * lax.rsqrt(variance + EPSILON) * gain)

def project(normed, weight):
    return jnp.dot(normed, weight, precision=highest)

def pair_bias(pair_float, bias_weight):
    return jnp.einsum('jcik,ch->jhik', pair_float, bias_weight, precision=highest)

def attend(queries, keys_ext, values_ext, bias, window_shift, first_query, first_key, atom_total):
    block_count, head_count, query_rows, key_count = bias.shape
    channels = queries.shape[1]
    head_size = channels // head_count
    offsets = jnp.arange(key_count, dtype=jnp.int32)
    starts = first_query + jnp.arange(block_count, dtype=jnp.int32) * query_rows + window_shift
    key_index = (starts - first_key)[:, None] + offsets[None, :]
    key_position = starts[:, None] + offsets[None, :]
    inside = jnp.logical_and(key_position >= 0, key_position < atom_total).astype(jnp.float32)
    key_rows = narrow(keys_ext[key_index]).reshape(block_count, key_count, head_count, head_size)
    value_rows = narrow(values_ext[key_index]).reshape(block_count, key_count, head_count, head_size)
    query_block = narrow(queries).reshape(block_count, query_rows, head_count, head_size)
    scores = jnp.einsum('jihd,jkhd->jhik', query_block, key_rows, precision=highest) / jnp.sqrt(jnp.float32(head_size)) + bias
    weights = jnp.exp(scores) * inside[:, None, None, :]
    attention = narrow(weights / lax.optimization_barrier(jnp.sum(weights, -1, keepdims=True)))
    attended = jnp.einsum('jhik,jkhd->jihd', attention, value_rows, precision=highest)
    return attended.reshape(block_count * query_rows, channels)

def forward(state, pair_float, norm_gain, in_float, out_float, weight_bias, token_float, window_shift, atom_token, token_counts):
    channels = state.shape[1]
    padding = ((HALO, HALO), (0, 0))
    for layer in range(BLOCKS):
        bias = pair_bias(pair_float, weight_bias[layer])
        normed = normalize(state, norm_gain[layer])
        projected = project(normed, in_float[layer])
        queries = projected[:, :channels]
        keys = jnp.pad(projected[:, channels:2 * channels], padding)
        values = jnp.pad(projected[:, 2 * channels:3 * channels], padding)
        gates = projected[:, 3 * channels:]
        attended = attend(queries, keys, values, bias, window_shift, 0, -HALO, state.shape[0])
        update = jnp.dot(narrow(attended), out_float[layer], precision=highest)
        state = state + jax.nn.sigmoid(gates) * update
    hidden = jax.nn.silu(jnp.dot(narrow(state), token_float, precision=highest))
    summed = jax.ops.segment_sum(hidden, atom_token, num_segments=TOKENS)
    return summed / token_counts.astype(jnp.float32)[:, None]

def reference(atoms_in, pair_feats, window_shift, atom_token, token_counts, token_grad, norm_gain, weight_in, weight_out, weight_bias, weight_token):
    shared = (pair_feats.astype(jnp.float32), norm_gain, weight_in.astype(jnp.float32), weight_out.astype(jnp.float32), weight_bias, weight_token.astype(jnp.float32))

    def one_sample(carry, inputs):
        state, cotangent = inputs

        def local(state, shared):
            return forward(state, *shared, window_shift, atom_token, token_counts)
        _, pullback = jax.vjp(local, state, shared)
        grad_state, grad_shared = pullback(cotangent)
        return (jax.tree.map(jnp.add, carry, grad_shared), grad_state)
    zeros = jax.tree.map(jnp.zeros_like, shared)
    totals, grad_states = lax.scan(one_sample, zeros, (atoms_in.astype(jnp.float32), token_grad.astype(jnp.float32)))
    return (grad_states.astype(jnp.bfloat16), totals[0].astype(jnp.bfloat16), totals[1], totals[2], totals[3], totals[4], totals[5])
```

```python
from functools import partial

import jax
import jax.numpy as jnp
from jax import lax
from jax.sharding import PartitionSpec as P

HALO = 64


EPSILON = 1e-05
highest = lax.Precision.HIGHEST


def moves(part, step):
    dims = (4, 4, 2, 4, 2)
    pairs = []
    for source in range(256):
        place = []
        rest = source
        for size in reversed(dims):
            place.append(rest % size)
            rest //= size
        place.reverse()
        place[part] = (place[part] + step) % dims[part]
        target = 0
        for size, value in zip(dims, place):
            target = target * size + value
        pairs.append((source, target))
    return pairs


def hop(value, part, step):
    return lax.ppermute(value, ("seq", "samp"), moves(part, step))


def places():
    seq, samp = lax.axis_index("seq"), lax.axis_index("samp")
    return seq // 8, (seq // 2) % 4, seq % 2, samp // 2, samp % 2


def chunk(value, index):
    return lax.dynamic_index_in_dim(value, index, 0, False)


def spread(value, part, size, index, wire):
    own = chunk(value, index)
    got = [hop(chunk(value, (index + k) % size).astype(wire), part, k).astype(jnp.float32) for k in range(1, size)]
    return pair_up(own, got)


def pair_up(own, got):
    if len(got) == 1:
        return own + got[0]
    return (own + got[1]) + (got[0] + got[2])


def everyone(value, part, size):
    return pair_up(value, [hop(value, part, k) for k in range(1, size)])


def gathered(value, part, size, index):
    got = [value] + [hop(value, part, k) for k in range(1, size)]
    stacked = jnp.stack(got)
    order = jnp.mod(index - jnp.arange(size), size)
    return jnp.take(stacked, order, axis=0)


def total(value):
    z, x, core, y, far = places()
    rows = value.shape[0]
    value = spread(value.reshape(2, rows // 2, 128), 2, 2, core, jnp.bfloat16)
    value = spread(value.reshape(4, rows // 8, 128), 3, 4, y, jnp.bfloat16)
    value = everyone(value, 1, 4)
    value = everyone(value, 0, 4)
    value = everyone(value, 4, 2)
    value = gathered(value, 3, 4, y).reshape(rows // 2, 128)
    return gathered(value, 2, 2, core).reshape(rows, 128)


def padded(cells, sides, width):
    for axis, dim in sides:
        count = lax.axis_size(axis)
        ends = count - 1
        head = lax.slice_in_dim(cells, 0, width, axis=dim)
        tail = lax.slice_in_dim(cells, cells.shape[dim] - width, cells.shape[dim], axis=dim)
        cells = jnp.concatenate(
            [
                lax.ppermute(tail, axis, [(i, (i + 1) % count) for i in range(ends)]),
                cells,
                lax.ppermute(head, axis, [((i + 1) % count, i) for i in range(ends)]),
            ],
            axis=dim,
        )
    return cells


def shifted(array, axis, by):
    length = lax.axis_size(axis)
    pairs = [(i, i + by) for i in range(length) if 0 <= i + by < length]
    return lax.ppermute(array, axis, pairs)


def narrow(value):
    return lax.optimization_barrier(value.astype(jnp.bfloat16)).astype(jnp.float32)


def normalize(state, gain):
    centred = state - jnp.mean(state, -1, keepdims=True)
    variance = jnp.mean(centred * centred, -1, keepdims=True)
    return narrow(centred * lax.rsqrt(variance + EPSILON) * gain)


def project(normed, weight):
    return jnp.dot(normed, weight, precision=highest)


def pair_bias(pair_float, bias_weight):
    return jnp.einsum("jcik,ch->jhik", pair_float, bias_weight, precision=highest)


def reach_blocks(rows, block_count, query_rows, pieces):
    channels = rows.shape[-1]
    parts = [
        rows[m * query_rows : m * query_rows + block_count * query_rows].reshape(
            block_count, query_rows, channels
        )
        for m in range(pieces)
    ]
    return jnp.concatenate(parts, 1)


def attend(queries, keys_ext, values_ext, bias, window_shift, first_query, first_key, atom_total):
    block_count, head_count, query_rows, key_count = bias.shape
    channels = queries.shape[1]
    head_size = channels // head_count
    margin = first_query - first_key
    span = keys_ext.shape[0] - block_count * query_rows + query_rows
    pieces = span // query_rows
    offsets = jnp.arange(span, dtype=jnp.int32)
    relative = offsets[None, :] - margin - window_shift[:, None]
    position = (
        first_key
        + jnp.arange(block_count, dtype=jnp.int32)[:, None] * query_rows
        + offsets[None, :]
    )
    inside = (relative >= 0) & (relative < key_count) & (position >= 0) & (position < atom_total)
    window_keys = jnp.arange(key_count, dtype=jnp.int32)
    placement = (relative[:, None, :] == window_keys[None, :, None]).astype(jnp.float32)
    bias_wide = jnp.einsum("jhik,jkl->jhil", bias, placement, precision=highest)
    key_rows = narrow(reach_blocks(keys_ext, block_count, query_rows, pieces)).reshape(
        block_count, span, head_count, head_size
    )
    value_rows = narrow(reach_blocks(values_ext, block_count, query_rows, pieces)).reshape(
        block_count, span, head_count, head_size
    )
    query_block = narrow(queries).reshape(block_count, query_rows, head_count, head_size)
    scores = (
        jnp.einsum("jihd,jkhd->jhik", query_block, key_rows, precision=highest)
        / jnp.sqrt(jnp.float32(head_size))
        + bias_wide
    )
    masked = jnp.where(inside[:, None, None, :], scores, -jnp.inf)
    weights = jnp.exp(masked)
    attention = narrow(weights / jnp.sum(weights, -1, keepdims=True))
    attended = jnp.einsum("jhik,jkhd->jihd", attention, value_rows, precision=highest)
    return attended.reshape(block_count * query_rows, channels)


def finish(
    projected,
    lower,
    upper,
    state,
    bias,
    out_weight,
    kv_weight,
    window_shift,
    first_atom,
    atom_total,
    from_inputs,
):
    channels = state.shape[-1]
    rim_rows = lower.shape[0]
    rows = jnp.concatenate([lower, projected[:, channels : 3 * channels], upper], 0)
    attended = attend(
        projected[:, :channels],
        rows[:, :channels],
        rows[:, channels:],
        bias,
        window_shift,
        first_atom,
        first_atom - rim_rows,
        atom_total,
    )
    update = jnp.dot(narrow(attended), out_weight, precision=highest)
    return state + jax.nn.sigmoid(projected[:, 3 * channels :]) * update


def token_head(state, weight):
    return jax.nn.silu(jnp.dot(narrow(state), weight, precision=highest))


def body(
    atoms_in,
    pair_feats,
    window_shift,
    atom_token,
    token_counts,
    token_grad,
    norm_gain,
    weight_in,
    weight_out,
    weight_bias,
    weight_token,
):
    shard = lax.axis_index("seq")
    atom_rows = atoms_in.shape[1]
    token_rows = token_grad.shape[1]
    channels = atoms_in.shape[2]
    layers = weight_in.shape[0]
    atom_total = atom_rows * lax.axis_size("seq")
    first_atom = shard * atom_rows
    pair_float = pair_feats.astype(jnp.float32)
    in_float = weight_in.astype(jnp.float32)
    out_float = weight_out.astype(jnp.float32)
    token_float = weight_token.astype(jnp.float32)
    layer_apply = jax.vmap(
        partial(
            finish,
            window_shift=window_shift,
            first_atom=first_atom,
            atom_total=atom_total,
            from_inputs=False,
        ),
        in_axes=(0, 0, 0, 0, None, None, None),
    )
    state = atoms_in.astype(jnp.float32)
    saved = []
    for layer in range(layers):
        bias = pair_bias(pair_float, weight_bias[layer])
        normed = normalize(state, norm_gain[layer])
        projected = jnp.dot(
            normed.astype(jnp.bfloat16), weight_in[layer], preferred_element_type=jnp.float32
        )
        outgoing = projected[:, :, channels : 3 * channels].astype(jnp.bfloat16)
        extended = padded(outgoing, (("seq", 1),), HALO)
        lower = extended[:, :HALO].astype(jnp.float32)
        upper = extended[:, HALO + atom_rows :].astype(jnp.float32)
        kv_weight = in_float[layer][:, channels : 3 * channels]
        saved.append((state, normed, projected, bias, lower, upper, kv_weight))
        state = layer_apply(projected, lower, upper, state, bias, out_float[layer], kv_weight)
    scaled = token_grad.astype(jnp.float32) / token_counts.astype(jnp.float32)[None, :, None]
    below = shifted(scaled[:, token_rows - 1 :], "seq", 1)
    token_table = jnp.concatenate([below, scaled], 1)
    local_index = atom_token - (shard * token_rows - 1)
    cotangent = jnp.take(token_table, local_index, axis=1)
    _, token_back = jax.vjp(token_head, state, token_float)
    grad_state, grad_token = token_back(cotangent)
    grad_gains = [None] * layers
    grad_inputs = [None] * layers
    grad_outputs = [None] * layers
    grad_biases = [None] * layers
    score_grads = [None] * layers
    for layer in reversed(range(layers)):
        state_in, normed, projected, bias, lower, upper, kv_weight = saved[layer]
        _, layer_back = jax.vjp(
            layer_apply, projected, lower, upper, state_in, bias, out_float[layer], kv_weight
        )
        grad_proj, grad_lower, grad_upper, grad_residual, grad_bias, grad_out, grad_kv = layer_back(
            grad_state
        )
        _, project_back = jax.vjp(project, normed, in_float[layer])
        from_below = shifted(grad_upper.astype(jnp.bfloat16), "seq", 1).astype(grad_upper.dtype)
        from_above = shifted(grad_lower.astype(jnp.bfloat16), "seq", -1).astype(grad_lower.dtype)
        grad_proj = grad_proj.at[:, :HALO, channels : 3 * channels].add(from_below)
        grad_proj = grad_proj.at[:, atom_rows - HALO :, channels : 3 * channels].add(from_above)
        grad_normed, grad_in = project_back(grad_proj)
        _, norm_back = jax.vjp(normalize, state_in, norm_gain[layer])
        grad_norm, grad_gain = norm_back(grad_normed)
        grad_state = grad_residual + grad_norm
        grad_gains[layer] = grad_gain
        grad_inputs[layer] = grad_in
        grad_outputs[layer] = grad_out
        grad_biases[layer] = jnp.einsum("jcik,jhik->ch", pair_float, grad_bias, precision=highest)
        score_grads[layer] = grad_bias
    scores = jnp.stack(score_grads, 1)
    scores = scores.reshape(4, 2, layers, *scores.shape[2:])
    _, _, _, y, far = places()
    scores = spread(scores.astype(jnp.bfloat16), 3, 4, y, jnp.bfloat16)
    scores = spread(scores.astype(jnp.float32), 4, 2, far, jnp.bfloat16)
    pair_sum = jnp.einsum("lhik,lch->cik", scores, weight_bias, precision=highest)[None].astype(jnp.bfloat16)
    leaves = (
        jnp.stack(grad_gains),
        jnp.stack(grad_inputs),
        jnp.stack(grad_outputs),
        jnp.stack(grad_biases),
        grad_token,
    )
    flat = jnp.concatenate([leaf.reshape(-1, 128) for leaf in leaves], 0)
    used = flat.shape[0]
    flat = total(jnp.pad(flat, ((0, -used % 64), (0, 0))))
    totals, at = [], 0
    for leaf in leaves:
        height = leaf.size // 128
        totals.append(flat[at : at + height].reshape(leaf.shape))
        at += height
    return (
        grad_state.astype(jnp.bfloat16),
        pair_sum,
        totals[0],
        totals[1],
        totals[2],
        totals[3],
        totals[4],
    )


def solution(mesh):
    return jax.shard_map(
        body,
        mesh=mesh,
        in_specs=(
            P("samp", "seq", None),
            P("seq", None, None, None),
            P("seq"),
            P("seq"),
            P("seq"),
            P("samp", "seq", None),
            P(),
            P(),
            P(),
            P(),
            P(),
        ),
        out_specs=(
            P("samp", "seq", None),
            P(("seq", "samp"), None, None, None),
            P(),
            P(),
            P(),
            P(),
            P(),
        ),
        check_vma=False,
    )
```

```python
from functools import partial

import jax
import jax.numpy as jnp
from jax import lax
from jax.experimental import pallas as pl
from jax.experimental.pallas import tpu as pltpu
from jax.sharding import PartitionSpec as P

HALO = 64
KWIN = 128
QBLK = 32
HEADS = 4
EPSILON = 1e-05
F32 = jnp.float32
BF16 = jnp.bfloat16
DIMS = (4, 4, 2, 4, 2)
WORLD = ("seq", "samp")


def moves(part, step):
    pairs = []
    for source in range(256):
        place, rest = [], source
        for size in reversed(DIMS):
            place.append(rest % size)
            rest //= size
        place.reverse()
        place[part] = (place[part] + step) % DIMS[part]
        target = 0
        for size, value in zip(DIMS, place):
            target = target * size + value
        pairs.append((source, target))
    return pairs


def hop(value, part, step):
    return lax.ppermute(value, WORLD, moves(part, step))


def shifted(array, by):
    length = lax.axis_size("seq")
    pairs = [(i, i + by) for i in range(length) if 0 <= i + by < length]
    return lax.ppermute(array, "seq", pairs)


def pair_up(own, got):
    if len(got) == 1:
        return own + got[0]
    return (own + got[1]) + (got[0] + got[2])


def everyone(value, part):
    return pair_up(value, [hop(value, part, k) for k in range(1, DIMS[part])])


def run(body, outs, args, smem=(), scratch=(), flops=10**8, nbytes=10**6):
    specs = [
        pl.BlockSpec(memory_space=pltpu.SMEM if i in smem else pltpu.VMEM) for i in range(len(args))
    ]
    return pl.pallas_call(
        body,
        out_shape=[jax.ShapeDtypeStruct(s, d) for s, d in outs],
        in_specs=specs,
        out_specs=[pl.BlockSpec(memory_space=pltpu.VMEM) for _ in outs],
        scratch_shapes=list(scratch),
        compiler_params=pltpu.CompilerParams(vmem_limit_bytes=24 * 2**20),
        cost_estimate=pl.CostEstimate(flops=flops, bytes_accessed=nbytes, transcendentals=0),
    )(*args)


def nn(a, b):
    return jnp.dot(a, b, preferred_element_type=F32)


def nt(a, b):
    return lax.dot_general(a, b, (((1,), (1,)), ((), ())), preferred_element_type=F32)


def tn(a, b):
    return lax.dot_general(a, b, (((0,), (0,)), ((), ())), preferred_element_type=F32)


def stats(state):
    centred = state - jnp.mean(state, -1, keepdims=True)
    scale = lax.rsqrt(jnp.mean(centred * centred, -1, keepdims=True) + EPSILON)
    return centred * scale, scale


def sigmoid(value):
    return 1.0 / (1.0 + jnp.exp(-value))


def head_mask(rows):
    row = lax.broadcasted_iota(jnp.int32, (rows, 128), 0) // QBLK
    lane = lax.broadcasted_iota(jnp.int32, (rows, 128), 1) // 32
    return row == lane


def stacked(block, mask):
    return jnp.where(mask, jnp.concatenate([block.astype(F32)] * HEADS, 0), 0.0).astype(BF16)


def picked(wide, mask):
    wide = jnp.where(mask, wide, 0.0)
    return (wide[0:32] + wide[32:64]) + (wide[64:96] + wide[96:128])


def project_into(state, gain, weight, normed_ref, q_ref, kv_ref, gate_ref, head_ref, tail_ref):
    unit, _ = stats(state)
    normed = (unit * gain).astype(BF16)
    normed_ref[...] = normed
    projected = nn(normed, weight)
    q_ref[...] = projected[:, 0:128].astype(BF16)
    kv = projected[:, 128:384].astype(BF16)
    kv_ref[...] = kv
    gate_ref[...] = sigmoid(projected[:, 384:512])
    rows = kv.shape[0]
    head_ref[...] = kv[0:HALO]
    tail_ref[0:HALO, :] = kv[rows - HALO : rows]


def count_rows(counts):
    size = counts.shape[1]
    row = lax.broadcasted_iota(jnp.int32, (size, size), 0)
    lane = lax.broadcasted_iota(jnp.int32, (size, size), 1)
    column = jnp.sum(jnp.where(row == lane, counts.astype(F32), 0.0), -1, keepdims=True)
    return jnp.broadcast_to(column, (size, 128))


def first_kernel(atoms, gain, weight, grad, counts, normed, q, kv, gate, head, tail):
    project_into(
        atoms[...].astype(F32), gain[0:1, :], weight[0], normed, q, kv, gate, head, tail
    )
    last = lax.broadcasted_iota(jnp.int32, (16, 384), 0) == 15
    row = jnp.where(last, grad[16:32, :].astype(F32), 0.0).astype(BF16)
    many = jnp.where(last[:, :128], count_rows(counts[...])[16:32], 0.0).astype(BF16)
    tail[HALO : HALO + 16, :] = row[:, 0:256]
    tail[HALO + 16 : HALO + 32, 0:128] = row[:, 256:384]
    tail[HALO + 16 : HALO + 32, 128:256] = many


def bias_kernel(weight, pair, bias):
    def block(j, carry):
        totals = [None] * 8
        for c in range(16):
            part = pair[j, c * 32 : (c + 1) * 32, :].astype(F32)
            for m in range(8):
                term = part * weight[m // 4, c, m % 4]
                totals[m] = term if c == 0 else totals[m] + term
        for m in range(8):
            bias[m // 4, j, (m % 4) * 32 : (m % 4 + 1) * 32, :] = totals[m]
        return carry

    lax.fori_loop(0, pair.shape[0], block, 0)


def load_window(kv, lower, upper, keys, values):
    rows = kv.shape[0]
    for ref, at in ((keys, 0), (values, 128)):
        ref[0:HALO, :] = lower[0:HALO, at : at + 128].astype(F32)
        ref[HALO : HALO + rows, :] = kv[:, at : at + 128].astype(F32)
        ref[HALO + rows : HALO + rows + HALO, :] = upper[:, at : at + 128].astype(F32)


def attention_forward(shift, q, bias, layer, keys, values, chances, att, atom_total):
    blocks = q.shape[0] // QBLK
    mask = head_mask(128)
    first = lax.axis_index("seq") * q.shape[0]
    lane = lax.broadcasted_iota(jnp.int32, (1, KWIN), 1)
    for j in range(blocks):
        begin = j * QBLK + shift[j]
        window = pl.ds(begin + HALO, KWIN)
        key = keys[window, :].astype(BF16)
        value = values[window, :].astype(BF16)
        wide = stacked(q[j * QBLK : (j + 1) * QBLK, :], mask)
        scores = nt(wide, key) * (32.0**-0.5) + bias[layer, j]
        place = first + begin + lane
        inside = jnp.logical_and(place >= 0, place < atom_total)
        weights = jnp.where(inside, jnp.exp(scores), 0.0)
        chance = weights * (1.0 / jnp.sum(weights, -1, keepdims=True))
        chances[j] = chance
        out = nn(chance.astype(BF16), value)
        att[j * QBLK : (j + 1) * QBLK, :] = picked(out, mask).astype(BF16)


def attention_backward(
    shift, q, keys, values, chances, grad_att, grad_q, grad_keys, grad_values, score_grad
):
    blocks = q.shape[0] // QBLK
    mask = head_mask(128)
    grad_keys[...] = jnp.zeros_like(grad_keys)
    grad_values[...] = jnp.zeros_like(grad_values)
    for j in range(blocks):
        window = pl.ds(j * QBLK + shift[j] + HALO, KWIN)
        rows = slice(j * QBLK, (j + 1) * QBLK)
        key = keys[window, :].astype(BF16)
        value = values[window, :].astype(BF16)
        wide = stacked(q[rows, :], mask)
        out = stacked(grad_att[rows, :], mask)
        chance = chances[j]
        grad_chance = nt(out, value).astype(BF16).astype(F32)
        term = chance * grad_chance
        grad_score = term - chance * jnp.sum(term, -1, keepdims=True)
        score_grad[j] = grad_score.astype(BF16)
        scaled = (grad_score * (32.0**-0.5)).astype(BF16)
        grad_q[rows, :] = picked(nn(scaled, key), mask).astype(BF16)
        grad_keys[window, :] += tn(scaled, wide).astype(BF16).astype(F32)
        grad_values[window, :] += tn(chance.astype(BF16), out).astype(BF16).astype(F32)


def share_scores(score_grad, own, one, two, three):
    y = lax.axis_index("samp") // 2
    for k, ref in enumerate((own, one, two, three)):
        ref[...] = score_grad[pl.ds(lax.rem(y + k, 4) * 2, 2)]


def forward_kernel(
    atom_total,
    shift,
    q,
    kv,
    lower,
    upper,
    bias,
    gate,
    atoms,
    weight_out,
    gain,
    weight_in,
    state,
    chances,
    att,
    normed,
    q_next,
    kv_next,
    gate_next,
    head,
    tail,
    keys,
    values,
):
    load_window(kv, lower, upper, keys, values)
    attention_forward(shift, q, bias, 0, keys, values, chances, att, atom_total)
    after = atoms[...].astype(F32) + gate[...] * nn(att[...], weight_out[0])
    state[...] = after
    project_into(
        after, gain[1:2, :], weight_in[1], normed, q_next, kv_next, gate_next, head, tail
    )


def layer_back(
    grad_state, gate, att, weight_out, layer, grad_gate, grad_update, grad_att, update=None
):
    if update is None:
        update = nn(att[...], weight_out[layer])
    gates = gate[...]
    grad_gate[...] = (grad_state * update * gates * (1.0 - gates)).astype(BF16)
    change = (grad_state * gates).astype(BF16)
    grad_update[...] = change
    grad_att[...] = nt(change, weight_out[layer]).astype(BF16)


def send_halo(grad_keys, grad_values, center, lower, upper):
    rows = center.shape[0]
    for ref, at in ((grad_keys, 0), (grad_values, 128)):
        lower[:, at : at + 128] = ref[0:HALO, :].astype(BF16)
        center[:, at : at + 128] = ref[HALO : HALO + rows, :]
        upper[:, at : at + 128] = ref[HALO + rows : HALO + rows + HALO, :].astype(BF16)


def middle_kernel(
    atom_total,
    shift,
    q,
    kv,
    lower,
    upper,
    bias,
    gate,
    state,
    weight_out,
    weight_token,
    grad,
    counts,
    atom_token,
    below,
    att,
    grad_update,
    narrow_state,
    grad_hidden,
    grad_state,
    grad_gate,
    grad_q,
    center,
    grad_lower,
    grad_upper,
    score_own,
    score_one,
    score_two,
    score_three,
    keys,
    values,
    chances,
    grad_att,
    grad_keys,
    grad_values,
    score_grad,
):
    load_window(kv, lower, upper, keys, values)
    attention_forward(shift, q, bias, 1, keys, values, chances, att, atom_total)
    update = nn(att[...], weight_out[1])
    after = (state[...] + gate[...] * update).astype(BF16)
    narrow_state[...] = after
    tokens = grad.shape[0]
    atoms = q.shape[0]
    place = atom_token[...] - lax.axis_index("seq") * tokens
    place = jnp.where(place < 0, tokens + 15, place)
    chosen = lax.broadcasted_iota(jnp.int32, (tokens + 16, atoms), 0) == place
    chosen = jnp.where(chosen, 1.0, 0.0).astype(BF16)
    own = jnp.concatenate([grad[...], count_rows(counts[...]).astype(BF16)], 1)
    before = jnp.concatenate([below[HALO : HALO + 16, :], below[HALO + 16 : HALO + 32, :]], 1)
    found = tn(chosen, jnp.concatenate([own, before], 0))
    many = found[:, 384:512]
    cotangent = found[:, 0:384] / jnp.concatenate([many] * 3, 1)
    hidden = nn(after, weight_token[...])
    open_ = sigmoid(hidden)
    back = (cotangent * (open_ * (1.0 + hidden * (1.0 - open_)))).astype(BF16)
    grad_hidden[...] = back
    rising = nt(back, weight_token[...]).astype(BF16).astype(F32)
    grad_state[...] = rising
    layer_back(rising, gate, att, weight_out, 1, grad_gate, grad_update, grad_att, update)
    attention_backward(
        shift, q, keys, values, chances, grad_att, grad_q, grad_keys, grad_values, score_grad
    )
    send_halo(grad_keys, grad_values, center, grad_lower, grad_upper)
    share_scores(score_grad, score_own, score_one, score_two, score_three)


def pair_weight_grad(pair, scores, out):
    y = lax.axis_index("samp") // 2
    left, right = [], []
    for k, ref in enumerate(scores):
        base = lax.rem(y + k, 4) * 2
        for m in range(2):
            left.append(pair[base + m])
            right.append(ref[m])
    product = nt(jnp.concatenate(left, 1), jnp.concatenate(right, 1))
    row = lax.rem(lax.broadcasted_iota(jnp.int32, product.shape, 0), QBLK)
    lane = lax.rem(lax.broadcasted_iota(jnp.int32, product.shape, 1), QBLK)
    product = jnp.where(row == lane, product, 0.0)
    for c in range(16):
        out[c : c + 1, :] = jnp.sum(product[c * 32 : (c + 1) * 32], 0, keepdims=True)


def middle_weights_kernel(
    pair, own, one, two, three, narrow_state, grad_hidden, att, grad_update, token, out, bias
):
    pair_weight_grad(pair, (own, one, two, three), bias)
    product = tn(narrow_state[...], grad_hidden[...])
    for m in range(3):
        token[m * 128 : (m + 1) * 128, :] = product[:, m * 128 : (m + 1) * 128]
    out[...] = tn(att[...], grad_update[...])


def join_projected(grad_q, center, from_below, from_above, grad_gate, joined):
    rows = center.shape[0]
    joined[:, 0:128] = grad_q[...]
    joined[:, 384:512] = grad_gate[...]
    joined[0:HALO, 128:384] = (center[0:HALO, :] + from_below[...].astype(F32)).astype(BF16)
    joined[HALO : rows - HALO, 128:384] = center[HALO : rows - HALO, :].astype(BF16)
    joined[rows - HALO : rows, 128:384] = (
        center[rows - HALO : rows, :] + from_above[...].astype(F32)
    ).astype(BF16)


def norm_back(grad_normed, state, gain):
    unit, scale = stats(state)
    grad_gain = jnp.sum(grad_normed * unit, 0, keepdims=True)
    back = grad_normed * gain
    back = scale * (
        back - jnp.mean(back, -1, keepdims=True) - unit * jnp.mean(back * unit, -1, keepdims=True)
    )
    return back, grad_gain


def backward_kernel(
    shift,
    grad_q_later,
    center_later,
    from_below,
    from_above,
    grad_gate_later,
    state,
    gain,
    weight_in,
    grad_state_later,
    q,
    kv,
    lower,
    upper,
    gate,
    att,
    weight_out,
    chances,
    joined,
    grad_gain,
    grad_update,
    grad_state,
    grad_gate,
    grad_q,
    center,
    grad_lower,
    grad_upper,
    score_own,
    score_one,
    score_two,
    score_three,
    keys,
    values,
    grad_att,
    grad_keys,
    grad_values,
    score_grad,
):
    load_window(kv, lower, upper, keys, values)
    join_projected(grad_q_later, center_later, from_below, from_above, grad_gate_later, joined)
    grad_normed = nt(joined[...], weight_in[1]).astype(BF16).astype(F32)
    back, gained = norm_back(grad_normed, state[...], gain[1:2, :])
    grad_gain[...] = gained
    rising = grad_state_later[...] + back
    grad_state[...] = rising
    layer_back(rising, gate, att, weight_out, 0, grad_gate, grad_update, grad_att)
    attention_backward(
        shift, q, keys, values, chances, grad_att, grad_q, grad_keys, grad_values, score_grad
    )
    send_halo(grad_keys, grad_values, center, grad_lower, grad_upper)
    share_scores(score_grad, score_own, score_one, score_two, score_three)


def backward_weights_kernel(
    pair, own, one, two, three, normed, joined, att, grad_update, inner, out, bias
):
    pair_weight_grad(pair, (own, one, two, three), bias)
    product = tn(normed[...], joined[...])
    for m in range(4):
        inner[m * 128 : (m + 1) * 128, :] = product[:, m * 128 : (m + 1) * 128]
    out[...] = tn(att[...], grad_update[...])


BIG = 208
SPAN = 224


def last_kernel(
    grad_q,
    center,
    from_below,
    from_above,
    grad_gate,
    atoms,
    gain,
    weight_in,
    grad_state,
    normed,
    token,
    out_later,
    inner_later,
    out_first,
    gain_later,
    bias_later,
    bias_first,
    grad_atoms,
    keep,
    send,
    joined,
    whole,
):
    join_projected(grad_q, center, from_below, from_above, grad_gate, joined)
    grad_normed = nt(joined[...], weight_in[0]).astype(BF16).astype(F32)
    back, gained = norm_back(grad_normed, atoms[...].astype(F32), gain[0:1, :])
    grad_atoms[...] = (grad_state[...] + back).astype(BF16)
    product = tn(normed[...], joined[...])
    sources = [(token, r) for r in range(0, 384, 16)]
    sources += [(out_later, r) for r in range(0, 128, 16)]
    sources += [(inner_later, r) for r in range(0, 512, 16)]
    sources += [(out_first, r) for r in range(0, 128, 16)]
    for index, (ref, r) in enumerate(sources):
        row = index * 16
        whole[row // BIG, row % BIG : row % BIG + 16, :] = ref[r : r + 16, :]
    for m in range(4):
        for r in range(0, 128, 16):
            row = 1152 + m * 128 + r
            whole[row // BIG, row % BIG : row % BIG + 16, :] = product[
                r : r + 16, m * 128 : (m + 1) * 128
            ]
    whole[0, BIG:SPAN, :] = bias_first[...]
    whole[1, BIG:SPAN, :] = bias_later[...]
    first = lax.broadcasted_iota(jnp.int32, (16, 128), 0) == 0
    whole[2, BIG:SPAN, :] = jnp.where(first, gained, gain_later[...])
    for m in range(3, 8):
        whole[m, BIG:SPAN, :] = jnp.zeros((16, 128), F32)
    core = lax.rem(lax.axis_index("seq"), 2)
    keep[...] = whole[pl.ds(core * 4, 4)]
    send[...] = whole[pl.ds((1 - core) * 4, 4)].astype(BF16)


def core_kernel(keep, got, own, one, two, three, whole):
    whole[...] = keep[...] + got[...].astype(F32)
    y = lax.axis_index("samp") // 2
    own[...] = whole[y]
    for k, ref in enumerate((one, two, three)):
        ref[...] = whole[lax.rem(y + k + 1, 4)].astype(BF16)


def quarter_kernel(own, one, two, three, half):
    y = lax.axis_index("samp") // 2
    half[y] = own[...]
    for k, ref in enumerate((one, two, three)):
        half[lax.rem(y + 3 - k, 4)] = ref[...]


def finish_kernel(half, got, grad_gain, inner, out, bias, token, whole):
    core = lax.rem(lax.axis_index("seq"), 2)
    whole[pl.ds(core * 4, 4)] = half[...]
    whole[pl.ds((1 - core) * 4, 4)] = got[...]

    def take(ref, base, blocks):
        for m in range(blocks):
            for r in range(0, 128, 16):
                row = base + m * 128 + r
                ref[r : r + 16, m * 128 : (m + 1) * 128] = whole[
                    row // BIG, row % BIG : row % BIG + 16, :
                ]

    take(token, 0, 3)
    take(out.at[1], 384, 1)
    take(inner.at[1], 512, 4)
    take(out.at[0], 1024, 1)
    take(inner.at[0], 1152, 4)
    grad_gain[...] = whole[2, BIG : BIG + 2, :]
    for layer in range(2):
        spread = whole[layer, BIG:SPAN, :]
        lane = lax.broadcasted_iota(jnp.int32, spread.shape, 1) // QBLK
        for h in range(HEADS):
            bias[layer, :, h : h + 1] = jnp.sum(
                jnp.where(lane == h, spread, 0.0), -1, keepdims=True
            )


def expand_kernel(weight, first, later, pair):
    refs = (first, later)
    for c in range(16):
        value = None
        for layer in range(2):
            for h in range(HEADS):
                term = refs[layer][h * 32 : (h + 1) * 32, :] * weight[layer, c, h]
                value = term if value is None else value + term
        pair[c * 32 : (c + 1) * 32, :] = value.astype(BF16)


def sum_scores(own, one, two, three):
    got = [hop(v, 3, k + 1).astype(F32) for k, v in enumerate((one, two, three))]
    both = pair_up(own.astype(F32), got)
    far = lax.rem(lax.axis_index("samp"), 2)
    away = lax.dynamic_index_in_dim(both, 1 - far, 0, False).astype(BF16)
    return lax.dynamic_index_in_dim(both, far, 0, False) + hop(away, 4, 1).astype(F32)


def body(
    atoms_in,
    pair_feats,
    window_shift,
    atom_token,
    token_counts,
    token_grad,
    norm_gain,
    weight_in,
    weight_out,
    weight_bias,
    weight_token,
):
    rows = atoms_in.shape[1]
    blocks = pair_feats.shape[0]
    atom_total = rows * lax.axis_size("seq")
    atoms = atoms_in[0]
    grad = token_grad[0]
    pair = pair_feats.reshape(blocks, 512, 128)
    counts = token_counts.reshape(1, -1)
    token_row = atom_token.reshape(1, -1)
    ext = rows + 2 * HALO
    window = [pltpu.VMEM((ext, 128), F32), pltpu.VMEM((ext, 128), F32)]
    square = ((blocks, 128, 128), F32)
    wide = ((rows, 128), BF16)
    full = ((rows, 128), F32)
    kv_shape = ((rows, 256), BF16)
    rim = ((HALO, 256), BF16)
    score_piece = ((2, 128, 128), BF16)

    normed0, q0, kv0, gate0, head0, tail0 = run(
        first_kernel,
        [wide, wide, kv_shape, full, rim, ((HALO + 32, 256), BF16)],
        (atoms, norm_gain, weight_in, grad, counts),
    )
    lower0 = shifted(tail0, 1)
    upper0 = shifted(head0, -1)
    (bias,) = run(
        bias_kernel,
        [((2, blocks, 128, 128), F32)],
        (weight_bias, pair),
        smem=(0,),
        nbytes=2 * 10**6,
    )
    state1, chances0, att0, normed1, q1, kv1, gate1, head1, tail1 = run(
        partial(forward_kernel, atom_total),
        [full, square, wide, wide, wide, kv_shape, full, rim, rim],
        (
            window_shift,
            q0,
            kv0,
            lower0,
            upper0,
            bias,
            gate0,
            atoms,
            weight_out,
            norm_gain,
            weight_in,
        ),
        smem=(0,),
        scratch=window,
    )
    lower1 = shifted(tail1, 1)
    upper1 = shifted(head1, -1)
    back_scratch = [
        pltpu.VMEM((rows, 128), BF16),
        pltpu.VMEM((ext, 128), F32),
        pltpu.VMEM((ext, 128), F32),
        pltpu.VMEM((blocks, 128, 128), BF16),
    ]
    (
        att1,
        grad_update1,
        narrow_state,
        grad_hidden,
        grad_state2,
        grad_gate1,
        grad_q1,
        center1,
        grad_lower1,
        grad_upper1,
        *scores1,
    ) = run(
        partial(middle_kernel, atom_total),
        [
            wide,
            wide,
            wide,
            ((rows, 384), BF16),
            full,
            wide,
            wide,
            ((rows, 256), F32),
            rim,
            rim,
            score_piece,
            score_piece,
            score_piece,
            score_piece,
        ],
        (
            window_shift,
            q1,
            kv1,
            lower1,
            upper1,
            bias,
            gate1,
            state1,
            weight_out,
            weight_token,
            grad,
            counts,
            token_row,
            lower0,
        ),
        smem=(0,),
        scratch=window + [pltpu.VMEM((blocks, 128, 128), F32)] + back_scratch,
    )
    from_below1 = shifted(grad_upper1, 1)
    from_above1 = shifted(grad_lower1, -1)
    grad_token, grad_out1, grad_bias1 = run(
        middle_weights_kernel,
        [((384, 128), F32), ((128, 128), F32), ((16, 128), F32)],
        (pair, *scores1, narrow_state, grad_hidden, att1, grad_update1),
    )
    (
        joined1,
        grad_gain1,
        grad_update0,
        grad_state1,
        grad_gate0,
        grad_q0,
        center0,
        grad_lower0,
        grad_upper0,
        *scores0,
    ) = run(
        backward_kernel,
        [
            ((rows, 512), BF16),
            ((1, 128), F32),
            wide,
            full,
            wide,
            wide,
            ((rows, 256), F32),
            rim,
            rim,
            score_piece,
            score_piece,
            score_piece,
            score_piece,
        ],
        (
            window_shift,
            grad_q1,
            center1,
            from_below1,
            from_above1,
            grad_gate1,
            state1,
            norm_gain,
            weight_in,
            grad_state2,
            q0,
            kv0,
            lower0,
            upper0,
            gate0,
            att0,
            weight_out,
            chances0,
        ),
        smem=(0,),
        scratch=window + back_scratch,
    )
    from_below0 = shifted(grad_upper0, 1)
    from_above0 = shifted(grad_lower0, -1)
    grad_in1, grad_out0, grad_bias0 = run(
        backward_weights_kernel,
        [((512, 128), F32), ((128, 128), F32), ((16, 128), F32)],
        (pair, *scores0, normed1, joined1, att0, grad_update0),
    )
    grad_atoms, keep, send = run(
        last_kernel,
        [wide, ((4, SPAN, 128), F32), ((4, SPAN, 128), BF16)],
        (
            grad_q0,
            center0,
            from_below0,
            from_above0,
            grad_gate0,
            atoms,
            norm_gain,
            weight_in,
            grad_state1,
            normed0,
            grad_token,
            grad_out1,
            grad_in1,
            grad_out0,
            grad_gain1,
            grad_bias1,
            grad_bias0,
        ),
        scratch=[pltpu.VMEM((rows, 512), BF16), pltpu.VMEM((8, SPAN, 128), F32)],
    )
    own, one, two, three = run(
        core_kernel,
        [((SPAN, 128), F32)] + [((SPAN, 128), BF16)] * 3,
        (keep, hop(send, 2, 1)),
        scratch=[pltpu.VMEM((4, SPAN, 128), F32)],
    )
    got = [hop(v, 3, k + 1).astype(F32) for k, v in enumerate((one, two, three))]
    total = pair_up(own, got)
    total = everyone(total, 1)
    total = everyone(total, 0)
    total = everyone(total, 4)
    (half,) = run(
        quarter_kernel,
        [((4, SPAN, 128), F32)],
        (total, *[hop(total, 3, k) for k in range(1, 4)]),
    )
    grad_gain, grad_in, grad_out, grad_bias, grad_token = run(
        finish_kernel,
        [
            ((2, 128), F32),
            ((2, 128, 512), F32),
            ((2, 128, 128), F32),
            ((2, 16, 4), F32),
            ((128, 384), F32),
        ],
        (half, hop(half, 2, 1)),
        scratch=[pltpu.VMEM((8, SPAN, 128), F32)],
    )
    (pair_sum,) = run(
        expand_kernel,
        [((512, 128), BF16)],
        (weight_bias, sum_scores(*scores0), sum_scores(*scores1)),
        smem=(0,),
    )
    return (
        grad_atoms[None],
        pair_sum.reshape(1, 16, 32, 128),
        grad_gain,
        grad_in,
        grad_out,
        grad_bias,
        grad_token,
    )


def solution(mesh):
    return jax.shard_map(
        body,
        mesh=mesh,
        in_specs=(
            P("samp", "seq", None),
            P("seq", None, None, None),
            P("seq"),
            P("seq"),
            P("seq"),
            P("samp", "seq", None),
            P(),
            P(),
            P(),
            P(),
            P(),
        ),
        out_specs=(
            P("samp", "seq", None),
            P(("seq", "samp"), None, None, None),
            P(),
            P(),
            P(),
            P(),
            P(),
        ),
        check_vma=False,
    )
```

```python
from functools import partial

import jax
import jax.numpy as jnp
from jax import lax
from jax.experimental import pallas as pl
from jax.experimental.pallas import tpu as pltpu
from jax.sharding import PartitionSpec as P

HALO = 64
KWIN = 128
QBLK = 32
HEADS = 4
EPSILON = 1e-05
F32 = jnp.float32
BF16 = jnp.bfloat16
DIMS = (4, 4, 2, 4, 2)
WORLD = ("seq", "samp")


def moves(part, step):
    pairs = []
    for source in range(256):
        place, rest = [], source
        for size in reversed(DIMS):
            place.append(rest % size)
            rest //= size
        place.reverse()
        place[part] = (place[part] + step) % DIMS[part]
        target = 0
        for size, value in zip(DIMS, place):
            target = target * size + value
        pairs.append((source, target))
    return pairs


def hop(value, part, step):
    return lax.ppermute(value, WORLD, moves(part, step))


def swapped(near, far):
    length = lax.axis_size("seq")
    chip = [(i, i ^ 1) for i in range(length)]
    across = [(i, i - 1 + 2 * (i % 2)) for i in range(length)]
    across = [(i, j) for i, j in across if 0 <= j < length]
    far = lax.ppermute(far, "seq", across)
    return lax.ppermute(near, "seq", chip), far


def pair_up(own, got):
    if len(got) == 1:
        return own + got[0]
    return (own + got[1]) + (got[0] + got[2])


def everyone(value, part):
    got = [hop(value, part, k).astype(F32) for k in range(1, DIMS[part])]
    return pair_up(value.astype(F32), got).astype(BF16)


def run(body, outs, args, smem=(), hbm=(), scratch=(), flops=10**8, nbytes=10**6):
    spaces = [pltpu.VMEM] * len(args)
    for i in smem:
        spaces[i] = pltpu.SMEM
    for i in hbm:
        spaces[i] = pltpu.HBM
    specs = [pl.BlockSpec(memory_space=space) for space in spaces]
    return pl.pallas_call(
        body,
        out_shape=[jax.ShapeDtypeStruct(s, d) for s, d in outs],
        in_specs=specs,
        out_specs=[pl.BlockSpec(memory_space=pltpu.VMEM) for _ in outs],
        scratch_shapes=list(scratch),
        compiler_params=pltpu.CompilerParams(vmem_limit_bytes=24 * 2**20),
        cost_estimate=pl.CostEstimate(flops=flops, bytes_accessed=nbytes, transcendentals=0),
    )(*args)


def nn(a, b):
    return jnp.dot(a, b, preferred_element_type=F32)


def nt(a, b):
    return lax.dot_general(a, b, (((1,), (1,)), ((), ())), preferred_element_type=F32)


def tn(a, b):
    return lax.dot_general(a, b, (((0,), (0,)), ((), ())), preferred_element_type=F32)


def stats(state):
    centred = state - jnp.mean(state, -1, keepdims=True)
    scale = lax.rsqrt(jnp.mean(centred * centred, -1, keepdims=True) + EPSILON)
    return centred * scale, scale


def sigmoid(value):
    return 1.0 / (1.0 + jnp.exp(-value))


def head_mask(rows):
    row = lax.broadcasted_iota(jnp.int32, (rows, 128), 0) // QBLK
    lane = lax.broadcasted_iota(jnp.int32, (rows, 128), 1) // 32
    return row == lane


def stacked(block, mask):
    return jnp.where(mask, jnp.concatenate([block.astype(F32)] * HEADS, 0), 0.0).astype(BF16)


def picked(wide, mask):
    wide = jnp.where(mask, wide, 0.0)
    return (wide[0:32] + wide[32:64]) + (wide[64:96] + wide[96:128])


def odd_core():
    return lax.rem(lax.axis_index("seq"), 2) == 1


def project_into(state, gain, weight, normed_ref, q_ref, kv_ref, gate_ref, near_ref, far_ref):
    unit, _ = stats(state)
    normed = (unit * gain).astype(BF16)
    normed_ref[...] = normed
    projected = nn(normed, weight)
    q_ref[...] = projected[:, 0:128].astype(BF16)
    kv = projected[:, 128:384]
    kv_ref[...] = kv.astype(BF16)
    gate_ref[...] = sigmoid(projected[:, 384:512])
    rows = kv.shape[0]
    head, tail = kv[0:HALO], kv[rows - HALO : rows]
    near_ref[0:HALO, :] = jnp.where(odd_core(), head, tail).astype(BF16)
    far_ref[0:HALO, :] = jnp.where(odd_core(), tail, head).astype(BF16)


def from_before(near, far):
    return jnp.where(odd_core(), near.astype(F32), far.astype(F32))


def from_after(near, far):
    return jnp.where(odd_core(), far.astype(F32), near.astype(F32))


def count_rows(counts):
    size = counts.shape[1]
    row = lax.broadcasted_iota(jnp.int32, (size, size), 0)
    lane = lax.broadcasted_iota(jnp.int32, (size, size), 1)
    column = jnp.sum(jnp.where(row == lane, counts.astype(F32), 0.0), -1, keepdims=True)
    return jnp.broadcast_to(column, (size, 128))


def first_kernel(
    atoms_far,
    gain_far,
    weight_far,
    grad_far,
    counts_far,
    normed,
    q,
    kv,
    gate,
    near,
    far,
    atoms,
    gain,
    weight,
    grad,
    counts,
    sems,
):
    pairs = (
        (atoms_far, atoms),
        (weight_far, weight),
        (gain_far, gain),
        (grad_far, grad),
        (counts_far, counts),
    )
    copies = [pltpu.make_async_copy(a, b, sems.at[i]) for i, (a, b) in enumerate(pairs)]
    for copy in copies:
        copy.start()
    for copy in copies:
        copy.wait()
    project_into(atoms[...].astype(F32), gain[0:1, :], weight[0], normed, q, kv, gate, near, far)
    last = lax.broadcasted_iota(jnp.int32, (16, 384), 0) == 15
    row = jnp.where(last, grad[16:32, :].astype(F32), 0.0).astype(BF16)
    many = jnp.where(last[:, :128], count_rows(counts[...])[16:32], 0.0).astype(BF16)
    for ref in (near, far):
        ref[HALO : HALO + 16, :] = row[:, 0:256]
        ref[HALO + 16 : HALO + 32, 0:128] = row[:, 256:384]
        ref[HALO + 16 : HALO + 32, 128:256] = many


def bias_kernel(layer, weight, pair_far, *rest):
    bias, pair, sems = rest[-3:]
    blocks = pair.shape[0]

    def fetch(j):
        return pltpu.make_async_copy(pair_far.at[j], pair.at[j], sems.at[j])

    for j in range(blocks):
        fetch(j).start()

    def block(j, carry):
        fetch(j).wait()
        totals = [None] * HEADS
        for c in range(16):
            part = pair[j, c * 32 : (c + 1) * 32, :].astype(F32)
            for h in range(HEADS):
                term = part * weight[layer, h, c]
                totals[h] = term if c == 0 else totals[h] + term
        for h in range(HEADS):
            bias[j, h * 32 : (h + 1) * 32, :] = totals[h]
        return carry

    lax.fori_loop(0, blocks, block, 0)


def load_window(kv, near, far, keys, values):
    rows = kv.shape[0]
    for ref, at in ((keys, 0), (values, 128)):
        beside, across = near[0:HALO, at : at + 128], far[0:HALO, at : at + 128]
        ref[0:HALO, :] = from_before(beside, across)
        ref[HALO : HALO + rows, :] = kv[:, at : at + 128].astype(F32)
        ref[HALO + rows : HALO + rows + HALO, :] = from_after(beside, across)


def windows(shift, q, keys, values):
    mask = head_mask(128)
    spans = [pl.ds(j * QBLK + shift[j] + HALO, KWIN) for j in range(q.shape[0] // QBLK)]
    wide = [stacked(q[j * QBLK : (j + 1) * QBLK, :], mask) for j in range(len(spans))]
    key = [keys[span, :].astype(BF16) for span in spans]
    value = [values[span, :].astype(BF16) for span in spans]
    return spans, wide, key, value


def attention_forward(shift, found, bias, att, rows, atom_total):
    _, wide, key, value = found
    count = len(wide)
    mask = head_mask(128)
    first = lax.axis_index("seq") * rows
    lane = lax.broadcasted_iota(jnp.int32, (1, KWIN), 1)
    scores = [nt(wide[j], key[j]) for j in range(count)]
    chances = []
    for j in range(count):
        place = first + (j * QBLK + shift[j]) + lane
        inside = jnp.logical_and(place >= 0, place < atom_total)
        weights = jnp.where(inside, jnp.exp(scores[j] * (32.0**-0.5) + bias[j]), 0.0)
        chances.append(weights * (1.0 / jnp.sum(weights, -1, keepdims=True)))
    out = [nn(chances[j].astype(BF16), value[j]) for j in range(count)]
    for j in range(count):
        att[j * QBLK : (j + 1) * QBLK, :] = picked(out[j], mask).astype(BF16)
    return chances


def attention_backward(found, chances, grad_att, grad_q, grad_keys, grad_values, score_grad):
    spans, wide, key, value = found
    count = len(wide)
    mask = head_mask(128)
    out = [stacked(grad_att[j * QBLK : (j + 1) * QBLK, :], mask) for j in range(count)]
    rising = [nt(out[j], value[j]) for j in range(count)]
    value_back = [tn(chances[j].astype(BF16), out[j]) for j in range(count)]
    scaled = []
    for j in range(count):
        term = chances[j] * rising[j].astype(BF16).astype(F32)
        grad_score = term - chances[j] * jnp.sum(term, -1, keepdims=True)
        score_grad[j] = grad_score.astype(BF16)
        scaled.append((grad_score * (32.0**-0.5)).astype(BF16))
    query_back = [nn(scaled[j], key[j]) for j in range(count)]
    key_back = [tn(scaled[j], wide[j]) for j in range(count)]
    for j in range(count):
        grad_q[j * QBLK : (j + 1) * QBLK, :] = picked(query_back[j], mask).astype(BF16)
    grad_keys[...] = jnp.zeros_like(grad_keys)
    grad_values[...] = jnp.zeros_like(grad_values)
    for j in range(count):
        grad_keys[spans[j], :] += key_back[j].astype(BF16).astype(F32)
        grad_values[spans[j], :] += value_back[j].astype(BF16).astype(F32)


def share_scores(score_grad, own, one, two, three):
    y = lax.axis_index("samp") // 2
    for k, ref in enumerate((own, one, two, three)):
        ref[...] = score_grad[pl.ds(lax.rem(y + k, 4) * 2, 2)]


def forward_kernel(
    atom_total,
    shift,
    q,
    kv,
    near,
    far,
    bias,
    gate,
    atoms,
    weight_out,
    gain,
    weight_in,
    state,
    chances,
    att,
    normed,
    q_next,
    kv_next,
    gate_next,
    near_next,
    far_next,
    keys,
    values,
):
    load_window(kv, near, far, keys, values)
    found = windows(shift, q, keys, values)
    kept = attention_forward(shift, found, bias, att, q.shape[0], atom_total)
    for j, chance in enumerate(kept):
        chances[j] = chance
    after = atoms[...].astype(F32) + gate[...] * nn(att[...], weight_out[0])
    state[...] = after
    project_into(
        after, gain[1:2, :], weight_in[1], normed, q_next, kv_next, gate_next, near_next, far_next
    )


def layer_back(
    grad_state, gate, att, weight_out, layer, grad_gate, grad_update, grad_att, update=None
):
    if update is None:
        update = nn(att[...], weight_out[layer])
    gates = gate[...]
    grad_gate[...] = (grad_state * update * gates * (1.0 - gates)).astype(BF16)
    change = (grad_state * gates).astype(BF16)
    grad_update[...] = change
    grad_att[...] = nt(change, weight_out[layer]).astype(BF16)


def send_halo(grad_keys, grad_values, center, near, far):
    rows = center.shape[0]
    odd = odd_core()
    for ref, at in ((grad_keys, 0), (grad_values, 128)):
        before, after = ref[0:HALO, :], ref[HALO + rows : HALO + rows + HALO, :]
        near[:, at : at + 128] = jnp.where(odd, before, after).astype(BF16)
        far[:, at : at + 128] = jnp.where(odd, after, before).astype(BF16)
        center[:, at : at + 128] = ref[HALO : HALO + rows, :]


def middle_kernel(
    atom_total,
    shift,
    q,
    kv,
    near,
    far,
    bias,
    gate,
    state,
    weight_out,
    weight_token,
    grad,
    counts,
    atom_token,
    near_first,
    far_first,
    att,
    grad_update,
    narrow_state,
    grad_hidden,
    grad_state,
    grad_gate,
    grad_q,
    center,
    grad_near,
    grad_far,
    score_own,
    score_one,
    score_two,
    score_three,
    keys,
    values,
    grad_att,
    grad_keys,
    grad_values,
    score_grad,
):
    load_window(kv, near, far, keys, values)
    found = windows(shift, q, keys, values)
    chances = attention_forward(shift, found, bias, att, q.shape[0], atom_total)
    update = nn(att[...], weight_out[1])
    after = (state[...] + gate[...] * update).astype(BF16)
    narrow_state[...] = after
    tokens = grad.shape[0]
    atoms = q.shape[0]
    place = atom_token[...] - lax.axis_index("seq") * tokens
    place = jnp.where(place < 0, tokens + 15, place)
    chosen = lax.broadcasted_iota(jnp.int32, (tokens + 16, atoms), 0) == place
    chosen = jnp.where(chosen, 1.0, 0.0).astype(BF16)
    own = jnp.concatenate([grad[...], count_rows(counts[...]).astype(BF16)], 1)
    before = from_before(near_first[HALO : HALO + 32, :], far_first[HALO : HALO + 32, :])
    before = jnp.concatenate([before[0:16], before[16:32]], 1).astype(BF16)
    taken = tn(chosen, jnp.concatenate([own, before], 0))
    many = taken[:, 384:512]
    cotangent = taken[:, 0:384] / jnp.concatenate([many] * 3, 1)
    hidden = nn(after, weight_token[...])
    open_ = sigmoid(hidden)
    back = (cotangent * (open_ * (1.0 + hidden * (1.0 - open_)))).astype(BF16)
    grad_hidden[...] = back
    rising = nt(back, weight_token[...]).astype(BF16).astype(F32)
    grad_state[...] = rising
    layer_back(rising, gate, att, weight_out, 1, grad_gate, grad_update, grad_att, update)
    attention_backward(found, chances, grad_att, grad_q, grad_keys, grad_values, score_grad)
    send_halo(grad_keys, grad_values, center, grad_near, grad_far)
    share_scores(score_grad, score_own, score_one, score_two, score_three)


def pair_weight_grad(pair, scores, out):
    left = [pair[block] for block, _ in scores]
    product = nt(jnp.concatenate(left, 1), jnp.concatenate([piece for _, piece in scores], 1))
    row = lax.rem(lax.broadcasted_iota(jnp.int32, product.shape, 0), QBLK)
    lane = lax.rem(lax.broadcasted_iota(jnp.int32, product.shape, 1), QBLK)
    product = jnp.where(row == lane, product, 0.0)
    for c in range(16):
        out[c : c + 1, :] = jnp.sum(product[c * 32 : (c + 1) * 32], 0, keepdims=True)


def middle_weights_kernel(
    pair, own, one, two, three, narrow_state, grad_hidden, att, grad_update, token, out, bias
):
    y = lax.axis_index("samp") // 2
    pair_weight_grad(
        pair,
        [
            (lax.rem(y + k, 4) * 2 + m, ref[m])
            for k, ref in enumerate((own, one, two, three))
            for m in range(2)
        ],
        bias,
    )
    product = tn(narrow_state[...], grad_hidden[...])
    for m in range(3):
        token[m * 128 : (m + 1) * 128, :] = product[:, m * 128 : (m + 1) * 128]
    out[...] = tn(att[...], grad_update[...])


def join_projected(grad_q, center, near, far, grad_gate, joined):
    rows = center.shape[0]
    joined[:, 0:128] = grad_q[...]
    joined[:, 384:512] = grad_gate[...]
    below, above = from_before(near[...], far[...]), from_after(near[...], far[...])
    joined[0:HALO, 128:384] = (center[0:HALO, :] + below).astype(BF16)
    joined[HALO : rows - HALO, 128:384] = center[HALO : rows - HALO, :].astype(BF16)
    joined[rows - HALO : rows, 128:384] = (center[rows - HALO : rows, :] + above).astype(BF16)


def norm_back(grad_normed, state, gain):
    unit, scale = stats(state)
    grad_gain = jnp.sum(grad_normed * unit, 0, keepdims=True)
    back = grad_normed * gain
    back = scale * (
        back - jnp.mean(back, -1, keepdims=True) - unit * jnp.mean(back * unit, -1, keepdims=True)
    )
    return back, grad_gain


def backward_kernel(
    shift,
    grad_q_later,
    center_later,
    near_later,
    far_later,
    grad_gate_later,
    state,
    gain,
    weight_in,
    grad_state_later,
    q,
    kv,
    near,
    far,
    gate,
    att,
    weight_out,
    chances,
    joined,
    grad_gain,
    grad_update,
    grad_state,
    grad_gate,
    grad_q,
    center,
    grad_near,
    grad_far,
    score_grad,
    keys,
    values,
    grad_att,
    grad_keys,
    grad_values,
):
    load_window(kv, near, far, keys, values)
    found = windows(shift, q, keys, values)
    join_projected(grad_q_later, center_later, near_later, far_later, grad_gate_later, joined)
    grad_normed = nt(joined[...], weight_in[1]).astype(BF16).astype(F32)
    back, gained = norm_back(grad_normed, state[...], gain[1:2, :])
    grad_gain[...] = gained
    rising = grad_state_later[...] + back
    grad_state[...] = rising
    layer_back(rising, gate, att, weight_out, 0, grad_gate, grad_update, grad_att)
    kept = [chances[j] for j in range(chances.shape[0])]
    attention_backward(found, kept, grad_att, grad_q, grad_keys, grad_values, score_grad)
    send_halo(grad_keys, grad_values, center, grad_near, grad_far)


EARLY = 144
EXTRA = 160
SPAN = 224


def backward_weights_kernel(
    pair,
    scores,
    normed,
    joined,
    att,
    grad_update,
    token,
    out_later,
    bias_later,
    gain_later,
    keep,
    send,
    whole,
):
    def put(row, value):
        whole[row // EARLY, row % EARLY : row % EARLY + 16, :] = value

    for r in range(0, 384, 16):
        put(r, token[r : r + 16, :])
    for r in range(0, 128, 16):
        put(384 + r, out_later[r : r + 16, :])
    inner = tn(normed[...], joined[...])
    for m in range(4):
        for r in range(0, 128, 16):
            put(512 + m * 128 + r, inner[r : r + 16, m * 128 : (m + 1) * 128])
    out = tn(att[...], grad_update[...])
    for r in range(0, 128, 16):
        put(1024 + r, out[r : r + 16, :])
    for m in range(2, 8):
        whole[m, EARLY:EXTRA, :] = jnp.zeros((16, 128), F32)
    pair_weight_grad(
        pair, [(j, scores[j]) for j in range(pair.shape[0])], whole.at[0, EARLY:EXTRA]
    )
    whole[1, EARLY:EXTRA, :] = bias_later[...]
    whole[3, EARLY : EARLY + 1, :] = gain_later[...]
    core = lax.rem(lax.axis_index("seq"), 2)
    keep[...] = whole[pl.ds(core * 4, 4)]
    send[...] = whole[pl.ds((1 - core) * 4, 4)]


def last_kernel(
    grad_q,
    center,
    near,
    far,
    grad_gate,
    atoms,
    gain,
    weight_in,
    grad_state,
    normed,
    keep_early,
    send_early,
    grad_atoms,
    keep,
    send,
    joined,
    late,
):
    join_projected(grad_q, center, near, far, grad_gate, joined)
    grad_normed = nt(joined[...], weight_in[0]).astype(BF16).astype(F32)
    product = tn(normed[...], joined[...])
    back, gained = norm_back(grad_normed, atoms[...].astype(F32), gain[0:1, :])
    grad_atoms[...] = (grad_state[...] + back).astype(BF16)
    for m in range(8):
        late[m, 0:16, :] = jnp.zeros((16, 128), F32)
        half = (m % 2) * 64
        late[m, 16:80, :] = product[half : half + 64, (m // 2) * 128 : (m // 2 + 1) * 128]
    late[2, 0:1, :] = gained
    core = lax.rem(lax.axis_index("seq"), 2)
    for ref, early, at in ((keep, keep_early, core), (send, send_early, 1 - core)):
        piece = late[pl.ds(at * 4, 4)]
        ref[:, 0:EARLY, :] = early[:, 0:EARLY, :].astype(ref.dtype)
        ref[:, EARLY:EXTRA, :] = (early[:, EARLY:EXTRA, :] + piece[:, 0:16]).astype(ref.dtype)
        ref[:, EXTRA:SPAN, :] = piece[:, 16:80].astype(ref.dtype)


def core_kernel(keep, got, scores, own, own_scores, one, two, three, whole):
    whole[...] = keep[...] + got[...].astype(F32)
    y = lax.axis_index("samp") // 2
    own[...] = whole[y]
    own_scores[...] = scores[pl.ds(y * 2, 2)]
    for k, ref in enumerate((one, two, three)):
        at = lax.rem(y + k + 1, 4)
        ref[0:SPAN, :] = whole[at].astype(BF16)
        for m in range(2):
            ref[SPAN + m * 128 : SPAN + (m + 1) * 128, :] = scores[at * 2 + m]


def far_kernel(
    own,
    own_scores,
    one,
    two,
    three,
    later,
    later_one,
    later_two,
    later_three,
    message,
    kept,
    both,
):
    got = [ref[...].astype(F32) for ref in (one, two, three)]
    message[0:SPAN, :] = pair_up(own[...], [v[0:SPAN] for v in got]).astype(BF16)
    for m in range(2):
        rows = slice(SPAN + m * 128, SPAN + (m + 1) * 128)
        both[m, 0] = pair_up(own_scores[m].astype(F32), [v[rows] for v in got])
        pieces = [ref[m].astype(F32) for ref in (later_one, later_two, later_three)]
        both[m, 1] = pair_up(later[m].astype(F32), pieces)
    side = lax.rem(lax.axis_index("samp"), 2)
    kept[...] = both[side]
    away = both[1 - side].astype(BF16)
    message[SPAN : SPAN + 128, :] = away[0]
    message[SPAN + 128 : SPAN + 256, :] = away[1]


def quarter_kernel(own, one, two, three, half):
    y = lax.axis_index("samp") // 2
    half[y] = own[...]
    for k, ref in enumerate((one, two, three)):
        half[lax.rem(y + 3 - k, 4)] = ref[...]


def finish_kernel(half, got, grad_gain, inner, out, bias, token):
    def finish(lower, upper):
        def chunk(m):
            return (lower if m < 4 else upper).at[m % 4]

        def rows(row):
            return chunk(row // EARLY)[row % EARLY : row % EARLY + 16, :].astype(F32)

        def take(ref, base, blocks):
            for m in range(blocks):
                for r in range(0, 128, 16):
                    ref[r : r + 16, m * 128 : (m + 1) * 128] = rows(base + m * 128 + r)

        take(token, 0, 3)
        take(out.at[1], 384, 1)
        take(inner.at[1], 512, 4)
        take(out.at[0], 1024, 1)
        for m in range(8):
            half_rows = (m % 2) * 64
            inner[0, half_rows : half_rows + 64, (m // 2) * 128 : (m // 2 + 1) * 128] = chunk(m)[
                EXTRA:SPAN, :
            ].astype(F32)
        for layer in range(2):
            grad_gain[layer : layer + 1, :] = chunk(2 + layer)[EARLY:EXTRA, :].astype(F32)[0:1]
            head = lax.broadcasted_iota(jnp.int32, (HEADS, 128), 0)
            lane = lax.broadcasted_iota(jnp.int32, (HEADS, 128), 1) // QBLK
            choose = jnp.where(head == lane, 1.0, 0.0).astype(BF16)
            bias[layer] = nt(choose, chunk(layer)[EARLY:EXTRA, :])

    odd = odd_core()

    @pl.when(jnp.logical_not(odd))
    def _():
        finish(half, got)

    @pl.when(odd)
    def _():
        finish(got, half)


def expand_kernel(weight, kept, got, pair):
    first = kept[0] + got[SPAN : SPAN + 128, :].astype(F32)
    later = kept[1] + got[SPAN + 128 : SPAN + 256, :].astype(F32)
    for c in range(16):
        value = None
        for layer, ref in enumerate((first, later)):
            for h in range(HEADS):
                term = ref[h * 32 : (h + 1) * 32, :] * weight[layer, h, c]
                value = term if value is None else value + term
        pair[c * 32 : (c + 1) * 32, :] = value.astype(BF16)


def body(
    atoms_in,
    pair_feats,
    window_shift,
    atom_token,
    token_counts,
    token_grad,
    norm_gain,
    weight_in,
    weight_out,
    weight_bias,
    weight_token,
):
    rows = atoms_in.shape[1]
    blocks = pair_feats.shape[0]
    atom_total = rows * lax.axis_size("seq")
    atoms = atoms_in[0]
    grad = token_grad[0]
    pair = pair_feats.reshape(blocks, 512, 128)
    counts = token_counts.reshape(1, -1)
    token_row = atom_token.reshape(1, -1)
    ext = rows + 2 * HALO
    window = [pltpu.VMEM((ext, 128), F32), pltpu.VMEM((ext, 128), F32)]
    square = ((blocks, 128, 128), F32)
    wide = ((rows, 128), BF16)
    full = ((rows, 128), F32)
    kv_shape = ((rows, 256), BF16)
    first_rim = ((HALO + 32, 256), BF16)
    rim = ((HALO, 256), BF16)
    score_piece = ((2, 128, 128), BF16)
    channel_weight = weight_bias.transpose(0, 2, 1)

    def pair_bias(layer, *after):
        (bias,) = run(
            partial(bias_kernel, layer),
            [square],
            (channel_weight, pair, *after),
            smem=(0,),
            hbm=range(1, 2 + len(after)),
            scratch=[
                pltpu.VMEM((blocks, 512, 128), BF16),
                pltpu.SemaphoreType.DMA((blocks,)),
            ],
        )
        return bias

    inputs = (atoms, norm_gain, weight_in, grad, counts)
    normed0, q0, kv0, gate0, *rims0 = run(
        first_kernel,
        [wide, wide, kv_shape, full, first_rim, first_rim],
        inputs,
        hbm=range(5),
        scratch=[pltpu.VMEM(v.shape, v.dtype) for v in inputs]
        + [pltpu.SemaphoreType.DMA((len(inputs),))],
    )
    rims0 = swapped(*rims0)
    bias0 = pair_bias(0)
    state1, chances0, att0, normed1, q1, kv1, gate1, *rims1 = run(
        partial(forward_kernel, atom_total),
        [full, square, wide, wide, wide, kv_shape, full, rim, rim],
        (window_shift, q0, kv0, *rims0, bias0, gate0, atoms, weight_out, norm_gain, weight_in),
        smem=(0,),
        scratch=window,
    )
    bias1 = pair_bias(1, att0)
    rims1 = swapped(*rims1)
    back_scratch = [
        pltpu.VMEM((rows, 128), BF16),
        pltpu.VMEM((ext, 128), F32),
        pltpu.VMEM((ext, 128), F32),
    ]
    (
        att1,
        grad_update1,
        narrow_state,
        grad_hidden,
        grad_state2,
        grad_gate1,
        grad_q1,
        center1,
        near1,
        far1,
        *scores1,
    ) = run(
        partial(middle_kernel, atom_total),
        [
            wide,
            wide,
            wide,
            ((rows, 384), BF16),
            full,
            wide,
            wide,
            ((rows, 256), F32),
            rim,
            rim,
            score_piece,
            score_piece,
            score_piece,
            score_piece,
        ],
        (
            window_shift,
            q1,
            kv1,
            *rims1,
            bias1,
            gate1,
            state1,
            weight_out,
            weight_token,
            grad,
            counts,
            token_row,
            *rims0,
        ),
        smem=(0,),
        scratch=window + back_scratch + [pltpu.VMEM((blocks, 128, 128), BF16)],
    )
    rims1 = swapped(near1, far1)
    got_one = hop(scores1[1], 3, 1)
    grad_token, grad_out1, grad_bias1 = run(
        middle_weights_kernel,
        [((384, 128), F32), ((128, 128), F32), ((16, 128), F32)],
        (pair, *scores1, narrow_state, grad_hidden, att1, grad_update1),
    )
    *rims1, got_one, grad_token = lax.optimization_barrier((*rims1, got_one, grad_token))
    (
        joined1,
        grad_gain1,
        grad_update0,
        grad_state1,
        grad_gate0,
        grad_q0,
        center0,
        near0,
        far0,
        scores0,
    ) = run(
        backward_kernel,
        [
            ((rows, 512), BF16),
            ((1, 128), F32),
            wide,
            full,
            wide,
            wide,
            ((rows, 256), F32),
            rim,
            rim,
            ((blocks, 128, 128), BF16),
        ],
        (
            window_shift,
            grad_q1,
            center1,
            *rims1,
            grad_gate1,
            state1,
            norm_gain,
            weight_in,
            grad_state2,
            q0,
            kv0,
            *rims0,
            gate0,
            att0,
            weight_out,
            chances0,
        ),
        smem=(0,),
        scratch=window + back_scratch,
    )
    last_rims = swapped(near0, far0)
    keep, send = run(
        backward_weights_kernel,
        [((4, EXTRA, 128), F32), ((4, EXTRA, 128), F32)],
        (
            pair,
            scores0,
            normed1,
            joined1,
            att0,
            grad_update0,
            grad_token,
            grad_out1,
            grad_bias1,
            grad_gain1,
        ),
        scratch=[pltpu.VMEM((8, EXTRA, 128), F32)],
    )
    got_two, got_three = hop(scores1[2], 3, 2), hop(scores1[3], 3, 3)
    *last_rims, got_two, got_three = lax.optimization_barrier((*last_rims, got_two, got_three))
    grad_atoms, keep, send = run(
        last_kernel,
        [wide, ((4, SPAN, 128), F32), ((4, SPAN, 128), BF16)],
        (
            grad_q0,
            center0,
            *last_rims,
            grad_gate0,
            atoms,
            norm_gain,
            weight_in,
            grad_state1,
            normed0,
            keep,
            send,
        ),
        scratch=[pltpu.VMEM((rows, 512), BF16), pltpu.VMEM((8, 80, 128), F32)],
    )
    message = ((SPAN + 256, 128), BF16)
    own, own_scores, *pieces = run(
        core_kernel,
        [((SPAN, 128), F32), score_piece, message, message, message],
        (keep, hop(send, 2, 1), scores0),
        scratch=[pltpu.VMEM((4, SPAN, 128), F32)],
    )
    pieces = [hop(v, 3, k + 1) for k, v in enumerate(pieces)]
    out, kept = run(
        far_kernel,
        [message, ((2, 128, 128), F32)],
        (own, own_scores, *pieces, scores1[0], got_one, got_two, got_three),
        scratch=[pltpu.VMEM((2, 2, 128, 128), F32)],
    )
    got = hop(out, 4, 1)
    total = (out[0:SPAN].astype(F32) + got[0:SPAN].astype(F32)).astype(BF16)
    total = everyone(total, 1)
    (pair_sum,) = run(expand_kernel, [((512, 128), BF16)], (channel_weight, kept, got), smem=(0,))
    total, pair_sum = lax.optimization_barrier((total, pair_sum))
    total = everyone(total, 0)
    (half,) = run(
        quarter_kernel,
        [((4, SPAN, 128), BF16)],
        (total, *[hop(total, 3, k) for k in range(1, 4)]),
    )
    grad_gain, grad_in, grad_out, grad_bias, grad_token = run(
        finish_kernel,
        [
            ((2, 128), F32),
            ((2, 128, 512), F32),
            ((2, 128, 128), F32),
            ((2, 4, 16), F32),
            ((128, 384), F32),
        ],
        (half, hop(half, 2, 1)),
    )
    return (
        grad_atoms[None],
        pair_sum.reshape(1, 16, 32, 128),
        grad_gain,
        grad_in,
        grad_out,
        grad_bias.transpose(0, 2, 1),
        grad_token,
    )


def solution(mesh):
    return jax.shard_map(
        body,
        mesh=mesh,
        in_specs=(
            P("samp", "seq", None),
            P("seq", None, None, None),
            P("seq"),
            P("seq"),
            P("seq"),
            P("samp", "seq", None),
            P(),
            P(),
            P(),
            P(),
            P(),
        ),
        out_specs=(
            P("samp", "seq", None),
            P(("seq", "samp"), None, None, None),
            P(),
            P(),
            P(),
            P(),
            P(),
        ),
        check_vma=False,
    )
```

```python
from functools import partial

import jax
import jax.numpy as jnp
from jax import lax
from jax.experimental import pallas as pl
from jax.experimental.pallas import tpu as pltpu
from jax.sharding import PartitionSpec as P

HALO = 64
KWIN = 128
QBLK = 32
HEADS = 4
EPSILON = 1e-05
F32 = jnp.float32
BF16 = jnp.bfloat16
DIMS = (4, 4, 2, 4, 2)
WORLD = ("seq", "samp")


def moves(part, step):
    pairs = []
    for source in range(256):
        place, rest = [], source
        for size in reversed(DIMS):
            place.append(rest % size)
            rest //= size
        place.reverse()
        place[part] = (place[part] + step) % DIMS[part]
        target = 0
        for size, value in zip(DIMS, place):
            target = target * size + value
        pairs.append((source, target))
    return pairs


def hop(value, part, step):
    return lax.ppermute(value, WORLD, moves(part, step))


def swapped(near, far):
    length = lax.axis_size("seq")
    chip = [(i, i ^ 1) for i in range(length)]
    across = [(i, i - 1 + 2 * (i % 2)) for i in range(length)]
    across = [(i, j) for i, j in across if 0 <= j < length]
    far = lax.ppermute(far, "seq", across)
    return lax.ppermute(near, "seq", chip), far


def pair_up(own, got):
    if len(got) == 1:
        return own + got[0]
    return (own + got[1]) + (got[0] + got[2])


def everyone(value, part):
    got = [hop(value, part, k).astype(F32) for k in range(1, DIMS[part])]
    return pair_up(value.astype(F32), got).astype(BF16)


def run(body, outs, args, smem=(), hbm=(), scratch=(), vmem=24, flops=10**8, nbytes=10**6):
    spaces = [pltpu.VMEM] * len(args)
    for i in smem:
        spaces[i] = pltpu.SMEM
    for i in hbm:
        spaces[i] = pltpu.HBM
    specs = [pl.BlockSpec(memory_space=space) for space in spaces]
    return pl.pallas_call(
        body,
        out_shape=[jax.ShapeDtypeStruct(s, d) for s, d in outs],
        in_specs=specs,
        out_specs=[pl.BlockSpec(memory_space=pltpu.VMEM) for _ in outs],
        scratch_shapes=list(scratch),
        compiler_params=pltpu.CompilerParams(vmem_limit_bytes=int(vmem * 2**20)),
        cost_estimate=pl.CostEstimate(flops=flops, bytes_accessed=nbytes, transcendentals=0),
    )(*args)


def nn(a, b):
    return jnp.dot(a, b, preferred_element_type=F32)


def nt(a, b):
    return lax.dot_general(a, b, (((1,), (1,)), ((), ())), preferred_element_type=F32)


def tn(a, b):
    return lax.dot_general(a, b, (((0,), (0,)), ((), ())), preferred_element_type=F32)


def stats(state):
    centred = state - jnp.mean(state, -1, keepdims=True)
    scale = lax.rsqrt(jnp.mean(centred * centred, -1, keepdims=True) + EPSILON)
    return centred * scale, scale


def sigmoid(value):
    return 1.0 / (1.0 + jnp.exp(-value))


def head_mask(rows):
    row = lax.broadcasted_iota(jnp.int32, (rows, 128), 0) // QBLK
    lane = lax.broadcasted_iota(jnp.int32, (rows, 128), 1) // 32
    return row == lane


def stacked(block, mask):
    return jnp.where(mask, jnp.concatenate([block.astype(F32)] * HEADS, 0), 0.0).astype(BF16)


def picked(wide, mask):
    wide = jnp.where(mask, wide, 0.0)
    return (wide[0:32] + wide[32:64]) + (wide[64:96] + wide[96:128])


def odd_core():
    return lax.rem(lax.axis_index("seq"), 2) == 1


def from_before(near, far):
    return jnp.where(odd_core(), near.astype(F32), far.astype(F32))


def from_after(near, far):
    return jnp.where(odd_core(), far.astype(F32), near.astype(F32))


def count_rows(counts):
    size = counts.shape[1]
    row = lax.broadcasted_iota(jnp.int32, (size, size), 0)
    lane = lax.broadcasted_iota(jnp.int32, (size, size), 1)
    column = jnp.sum(jnp.where(row == lane, counts.astype(F32), 0.0), -1, keepdims=True)
    return jnp.broadcast_to(column, (size, 128))


FIRST_VMEM = 62
PAIR_ROWS = 1024
ATOM_ROWS = PAIR_ROWS + 2 * HALO
MESSAGE = ATOM_ROWS + 16


def message_kernel(
    shift_far, pair, atoms, grad_far, counts_far, near, far, shift_row, shift, grad, counts, sems
):
    blocks, rows = pair.shape[0], atoms.shape[0]
    odd = odd_core()
    copies = [
        pltpu.make_async_copy(a, b, sems.at[i])
        for i, (a, b) in enumerate(((shift_far, shift), (grad_far, grad), (counts_far, counts)))
    ]
    bases = (jnp.where(odd, 0, blocks - 2), jnp.where(odd, blocks - 2, 0))
    for n, ref in enumerate((near, far)):
        for m in range(2):
            copies.append(
                pltpu.make_async_copy(
                    pair.at[bases[n] + m], ref.at[pl.ds(m * 512, 512)], sems.at[3 + n * 3 + m]
                )
            )
        first = pl.multiple_of(bases[n] * QBLK // (rows // 2) * (rows // 2), 128)
        copies.append(
            pltpu.make_async_copy(
                atoms.at[pl.ds(first, 2 * HALO)],
                ref.at[pl.ds(PAIR_ROWS, 2 * HALO)],
                sems.at[3 + n * 3 + 2],
            )
        )
    for copy in copies:
        copy.start()
    for copy in copies[:3]:
        copy.wait()
    size = counts.shape[1]
    lanes = lax.broadcasted_iota(jnp.int32, (1, size), 1)
    many = jnp.where(lanes == size - 1, counts[...].astype(F32), 0.0)
    many = jnp.sum(many, -1, keepdims=True)
    last = grad[16:32, :].astype(F32)[15:16, :]
    row = lax.broadcasted_iota(jnp.int32, (16, 128), 0)
    lane = lax.broadcasted_iota(jnp.int32, (16, 128), 1)
    group = jnp.where(row == 3, jnp.broadcast_to(many, (16, 128)), 0.0)
    for k in range(3):
        piece = jnp.broadcast_to(last[:, k * 128 : (k + 1) * 128], (16, 128))
        group = jnp.where(row == k, piece, group)
    for n, ref in enumerate((near, far)):
        value = group
        for m in range(2):
            place = jnp.logical_and(row == 4, lane == m)
            value = jnp.where(place, shift[bases[n] + m].astype(F32), value)
        ref[ATOM_ROWS:MESSAGE, :] = value.astype(BF16)
    lane = lax.broadcasted_iota(jnp.int32, (1, 128), 1)
    shifts = jnp.zeros((1, 128), jnp.int32)
    for j in range(blocks):
        shifts = jnp.where(lane == j, shift[j], shifts)
    shift_row[...] = shifts
    for copy in copies[3:]:
        copy.wait()


def first_kernel(atoms, gain, weight, normed, q, kv, gate):
    unit, _ = stats(atoms[...].astype(F32))
    normed[...] = (unit * gain[0:1, :]).astype(BF16)
    projected = nn(normed[...], weight[0])
    q[...] = projected[:, 0:128].astype(BF16)
    kv[...] = projected[:, 128:384].astype(BF16)
    gate[...] = sigmoid(projected[:, 384:512])


def block_bias(weight, layers, part):
    totals = [[None] * HEADS for _ in layers]
    for c in range(16):
        value = part(c)
        for n, layer in enumerate(layers):
            for h in range(HEADS):
                term = value * weight[layer, h, c]
                totals[n][h] = term if c == 0 else totals[n][h] + term
    return totals


def bias_kernel(weight, pair, first, later):
    def block(j, carry):
        totals = block_bias(
            weight, (0, 1), lambda c: pair[j, c * 32 : (c + 1) * 32, :].astype(F32)
        )
        for ref, total in zip((first, later), totals):
            for h in range(HEADS):
                ref[j, h * 32 : (h + 1) * 32, :] = total[h]
        return carry

    lax.fori_loop(0, pair.shape[0], block, 0)


def load_window(kv, keys, values):
    keys[...] = kv[:, 0:128].astype(F32)
    values[...] = kv[:, 128:256].astype(F32)


def windows(shifts, q, keys, values, margin):
    mask = head_mask(128)
    spans = [pl.ds(j * QBLK + shift + margin, KWIN) for j, shift in enumerate(shifts)]
    wide = [stacked(q[j * QBLK : (j + 1) * QBLK, :], mask) for j in range(len(spans))]
    key = [keys[span, :].astype(BF16) for span in spans]
    value = [values[span, :].astype(BF16) for span in spans]
    return spans, wide, key, value


def attention_forward(shifts, found, bias, first, atom_total):
    _, wide, key, value = found
    count = len(wide)
    mask = head_mask(128)
    lane = lax.broadcasted_iota(jnp.int32, (1, KWIN), 1)
    scores = [nt(wide[j], key[j]) for j in range(count)]
    chances = []
    for j in range(count):
        place = first + (j * QBLK + shifts[j]) + lane
        inside = jnp.logical_and(place >= 0, place < atom_total)
        weights = jnp.where(inside, jnp.exp(scores[j] * (32.0**-0.5) + bias[j]), 0.0)
        chances.append(weights * (1.0 / jnp.sum(weights, -1, keepdims=True)))
    out = [nn(chances[j].astype(BF16), value[j]) for j in range(count)]
    return chances, jnp.concatenate([picked(v, mask) for v in out], 0).astype(BF16)


def attention_backward(found, chances, grad_att, grad_q, grad_keys, grad_values, score_grad):
    spans, wide, key, value = found
    count = len(wide)
    mask = head_mask(128)
    out = [stacked(grad_att[j * QBLK : (j + 1) * QBLK, :], mask) for j in range(count)]
    rising = [nt(out[j], value[j]) for j in range(count)]
    value_back = [tn(chances[j].astype(BF16), out[j]) for j in range(count)]
    scaled = []
    for j in range(count):
        term = chances[j] * rising[j].astype(BF16).astype(F32)
        grad_score = term - chances[j] * jnp.sum(term, -1, keepdims=True)
        score_grad[j] = grad_score.astype(BF16)
        scaled.append((grad_score * (32.0**-0.5)).astype(BF16))
    query_back = [nn(scaled[j], key[j]) for j in range(count)]
    key_back = [tn(scaled[j], wide[j]) for j in range(count)]
    for j in range(count):
        grad_q[j * QBLK : (j + 1) * QBLK, :] = picked(query_back[j], mask).astype(BF16)
    grad_keys[...] = jnp.zeros_like(grad_keys)
    grad_values[...] = jnp.zeros_like(grad_values)
    for j in range(count):
        grad_keys[spans[j], :] += key_back[j].astype(BF16).astype(F32)
        grad_values[spans[j], :] += value_back[j].astype(BF16).astype(F32)


def share_scores(scores, parts):
    y = lax.axis_index("samp") // 2
    for k, ref in enumerate(parts):
        for n, score in enumerate(scores):
            ref[n * 2 : n * 2 + 2] = score[pl.ds(lax.rem(y + k, 4) * 2, 2)]


def forward_kernel(
    atom_total,
    shift,
    channel_weight,
    q,
    kv,
    near,
    far,
    bias,
    gate,
    atoms,
    weight_out,
    gain,
    weight_in,
    state,
    chances,
    att,
    kv_all,
    normed,
    q_next,
    kv_next,
    gate_next,
    keys,
    values,
):
    blocks, rows = bias.shape[0], q.shape[0]
    edge = HALO // QBLK
    first = lax.axis_index("seq") * rows
    there = slice(PAIR_ROWS, ATOM_ROWS)
    before, after = from_before(near[there], far[there]), from_after(near[there], far[there])
    beside = jnp.concatenate([before, after], 0)
    unit, _ = stats(beside)
    projected = nn((unit * gain[0:1, :]).astype(BF16), weight_in[0])
    for ref, at in ((keys, 128), (values, 256)):
        ref[0 : 2 * HALO, :] = projected[0 : 2 * HALO, at : at + 128].astype(BF16).astype(F32)
        ref[2 * HALO : 2 * HALO + rows, :] = kv[:, at - 128 : at].astype(F32)
        ref[2 * HALO + rows :, :] = projected[2 * HALO :, at : at + 128].astype(BF16).astype(F32)
    kv_all[:, 0:128] = keys[HALO : 3 * HALO + rows, :].astype(BF16)
    kv_all[:, 128:256] = values[HALO : 3 * HALO + rows, :].astype(BF16)
    ends = slice(HALO, 2 * HALO), slice(2 * HALO, 3 * HALO)
    queries = [projected[end, 0:128].astype(BF16) for end in ends]
    queries = jnp.concatenate([queries[0], q[...], queries[1]], 0)
    gates = [sigmoid(projected[end, 384:512]) for end in ends]
    gates = jnp.concatenate([gates[0], gate[...], gates[1]], 0)
    began = jnp.concatenate([beside[ends[0]], atoms[...].astype(F32), beside[ends[1]]], 0)
    biases, shifts = [], []
    tail = slice(ATOM_ROWS, MESSAGE)
    row = lax.broadcasted_iota(jnp.int32, (16, 128), 0)
    lane = lax.broadcasted_iota(jnp.int32, (16, 128), 1)
    for pick in (from_before, from_after):
        group = pick(near[tail], far[tail])
        for m in range(edge):
            chosen = jnp.where(jnp.logical_and(row == 4, lane == m), group, 0.0)
            value = jnp.sum(chosen).astype(jnp.int32)
            shifts.append(jnp.clip(value, -HALO, QBLK + HALO - KWIN))

            def part(c):
                span = slice(m * 512 + c * 32, m * 512 + (c + 1) * 32)
                return pick(near[span], far[span])

            (total,) = block_bias(channel_weight, (0,), part)
            biases.append(jnp.concatenate(total, 0))
    biases = biases[:edge] + [bias[j] for j in range(blocks)] + biases[edge:]
    shifts = shifts[:edge] + [shift[0, j] for j in range(blocks)] + shifts[edge:]
    found = windows(shifts, queries, keys, values, 2 * HALO - HALO)
    kept, attended = attention_forward(shifts, found, biases, first - HALO, atom_total)
    for j in range(blocks):
        chances[j] = kept[j + edge]
    att[...] = attended[HALO : HALO + rows]
    done = began + gates * nn(attended, weight_out[0])
    state[...] = done[HALO : HALO + rows]
    unit, _ = stats(done)
    normed_all = (unit * gain[1:2, :]).astype(BF16)
    normed[...] = normed_all[HALO : HALO + rows]
    projected = nn(normed_all, weight_in[1])
    place = first - HALO + lax.broadcasted_iota(jnp.int32, (rows + 2 * HALO, 1), 0)
    inside = jnp.logical_and(place >= 0, place < atom_total)
    kv_next[...] = jnp.where(inside, projected[:, 128:384], 0.0).astype(BF16)
    q_next[...] = projected[HALO : HALO + rows, 0:128].astype(BF16)
    gate_next[...] = sigmoid(projected[HALO : HALO + rows, 384:512])


def layer_back(
    grad_state, gate, att, weight_out, layer, grad_gate, grad_update, grad_att, update=None
):
    if update is None:
        update = nn(att[...], weight_out[layer])
    gates = gate[...]
    grad_gate[...] = (grad_state * update * gates * (1.0 - gates)).astype(BF16)
    change = (grad_state * gates).astype(BF16)
    grad_update[...] = change
    grad_att[...] = nt(change, weight_out[layer]).astype(BF16)


def send_halo(grad_keys, grad_values, center, near, far):
    rows = center.shape[0]
    odd = odd_core()
    for ref, at in ((grad_keys, 0), (grad_values, 128)):
        before, after = ref[0:HALO, :], ref[HALO + rows : HALO + rows + HALO, :]
        near[:, at : at + 128] = jnp.where(odd, before, after).astype(BF16)
        far[:, at : at + 128] = jnp.where(odd, after, before).astype(BF16)
        center[:, at : at + 128] = ref[HALO : HALO + rows, :]


def middle_kernel(
    atom_total,
    shift,
    q,
    kv,
    bias,
    gate,
    state,
    weight_out,
    weight_token,
    grad,
    counts,
    atom_token,
    near_first,
    far_first,
    att,
    grad_update,
    narrow_state,
    grad_hidden,
    grad_state,
    grad_gate,
    grad_q,
    center,
    grad_near,
    grad_far,
    score_grad,
    keys,
    values,
    grad_att,
    grad_keys,
    grad_values,
):
    load_window(kv, keys, values)
    shifts = [shift[0, j] for j in range(bias.shape[0])]
    found = windows(shifts, q, keys, values, HALO)
    first = lax.axis_index("seq") * q.shape[0]
    chances, attended = attention_forward(
        shifts, found, [bias[j] for j in range(bias.shape[0])], first, atom_total
    )
    att[...] = attended
    update = nn(attended, weight_out[1])
    after = (state[...] + gate[...] * update).astype(BF16)
    narrow_state[...] = after
    tokens = grad.shape[0]
    atoms = q.shape[0]
    place = atom_token[...] - lax.axis_index("seq") * tokens
    place = jnp.where(place < 0, tokens + 15, place)
    chosen = lax.broadcasted_iota(jnp.int32, (tokens + 16, atoms), 0) == place
    chosen = jnp.where(chosen, 1.0, 0.0).astype(BF16)
    own = jnp.concatenate([grad[...], count_rows(counts[...]).astype(BF16)], 1)
    group = from_before(near_first[ATOM_ROWS:MESSAGE, :], far_first[ATOM_ROWS:MESSAGE, :])
    before = [jnp.broadcast_to(group[k : k + 1], (16, 128)) for k in range(4)]
    before = jnp.concatenate(before, 1).astype(BF16)
    taken = tn(chosen, jnp.concatenate([own, before], 0))
    many = taken[:, 384:512]
    cotangent = taken[:, 0:384] / jnp.concatenate([many] * 3, 1)
    hidden = nn(after, weight_token[...])
    open_ = sigmoid(hidden)
    back = (cotangent * (open_ * (1.0 + hidden * (1.0 - open_)))).astype(BF16)
    grad_hidden[...] = back
    rising = nt(back, weight_token[...]).astype(BF16).astype(F32)
    grad_state[...] = rising
    layer_back(rising, gate, att, weight_out, 1, grad_gate, grad_update, grad_att, update)
    attention_backward(found, chances, grad_att, grad_q, grad_keys, grad_values, score_grad)
    send_halo(grad_keys, grad_values, center, grad_near, grad_far)


def pair_weight_grad(pair, scores, out):
    left = [pair[block] for block, _ in scores]
    product = nt(jnp.concatenate(left, 1), jnp.concatenate([piece for _, piece in scores], 1))
    row = lax.rem(lax.broadcasted_iota(jnp.int32, product.shape, 0), QBLK)
    lane = lax.rem(lax.broadcasted_iota(jnp.int32, product.shape, 1), QBLK)
    product = jnp.where(row == lane, product, 0.0)
    for c in range(16):
        out[c : c + 1, :] = jnp.sum(product[c * 32 : (c + 1) * 32], 0, keepdims=True)


def middle_weights_kernel(
    pair, scores, narrow_state, grad_hidden, att, grad_update, token, out, bias
):
    pair_weight_grad(pair, [(j, scores[j]) for j in range(pair.shape[0])], bias)
    product = tn(narrow_state[...], grad_hidden[...])
    for m in range(3):
        token[m * 128 : (m + 1) * 128, :] = product[:, m * 128 : (m + 1) * 128]
    out[...] = tn(att[...], grad_update[...])


def join_projected(grad_q, center, near, far, grad_gate, joined):
    rows = center.shape[0]
    joined[:, 0:128] = grad_q[...]
    joined[:, 384:512] = grad_gate[...]
    below, above = from_before(near[...], far[...]), from_after(near[...], far[...])
    joined[0:HALO, 128:384] = (center[0:HALO, :] + below).astype(BF16)
    joined[HALO : rows - HALO, 128:384] = center[HALO : rows - HALO, :].astype(BF16)
    joined[rows - HALO : rows, 128:384] = (center[rows - HALO : rows, :] + above).astype(BF16)


def norm_back(grad_normed, state, gain):
    unit, scale = stats(state)
    grad_gain = jnp.sum(grad_normed * unit, 0, keepdims=True)
    back = grad_normed * gain
    back = scale * (
        back - jnp.mean(back, -1, keepdims=True) - unit * jnp.mean(back * unit, -1, keepdims=True)
    )
    return back, grad_gain


def backward_kernel(
    shift,
    grad_q_later,
    center_later,
    near_later,
    far_later,
    grad_gate_later,
    state,
    gain,
    weight_in,
    grad_state_later,
    q,
    kv,
    gate,
    att,
    weight_out,
    chances,
    joined,
    grad_gain,
    grad_update,
    grad_state,
    grad_gate,
    grad_q,
    center,
    grad_near,
    grad_far,
    score_grad,
    keys,
    values,
    grad_att,
    grad_keys,
    grad_values,
):
    load_window(kv, keys, values)
    shifts = [shift[0, j] for j in range(chances.shape[0])]
    found = windows(shifts, q, keys, values, HALO)
    join_projected(grad_q_later, center_later, near_later, far_later, grad_gate_later, joined)
    grad_normed = nt(joined[...], weight_in[1]).astype(BF16).astype(F32)
    back, gained = norm_back(grad_normed, state[...], gain[1:2, :])
    grad_gain[...] = gained
    rising = grad_state_later[...] + back
    grad_state[...] = rising
    layer_back(rising, gate, att, weight_out, 0, grad_gate, grad_update, grad_att)
    kept = [chances[j] for j in range(chances.shape[0])]
    attention_backward(found, kept, grad_att, grad_q, grad_keys, grad_values, score_grad)
    send_halo(grad_keys, grad_values, center, grad_near, grad_far)


EARLY = 144
EXTRA = 160
SPAN = 224


def backward_weights_kernel(
    pair,
    scores,
    normed,
    joined,
    att,
    grad_update,
    token,
    out_later,
    bias_later,
    gain_later,
    scores_later,
    keep,
    send,
    own,
    one,
    two,
    three,
    whole,
):
    share_scores((scores, scores_later), (own, one, two, three))

    def put(row, value):
        whole[row // EARLY, row % EARLY : row % EARLY + 16, :] = value

    for r in range(0, 384, 16):
        put(r, token[r : r + 16, :])
    for r in range(0, 128, 16):
        put(384 + r, out_later[r : r + 16, :])
    inner = tn(normed[...], joined[...])
    for m in range(4):
        for r in range(0, 128, 16):
            put(512 + m * 128 + r, inner[r : r + 16, m * 128 : (m + 1) * 128])
    out = tn(att[...], grad_update[...])
    for r in range(0, 128, 16):
        put(1024 + r, out[r : r + 16, :])
    for m in range(2, 8):
        whole[m, EARLY:EXTRA, :] = jnp.zeros((16, 128), F32)
    pair_weight_grad(
        pair, [(j, scores[j]) for j in range(pair.shape[0])], whole.at[0, EARLY:EXTRA]
    )
    whole[1, EARLY:EXTRA, :] = bias_later[...]
    whole[3, EARLY : EARLY + 1, :] = gain_later[...]
    core = lax.rem(lax.axis_index("seq"), 2)
    keep[...] = whole[pl.ds(core * 4, 4)]
    send[...] = whole[pl.ds((1 - core) * 4, 4)]


def last_kernel(
    grad_q,
    center,
    near,
    far,
    grad_gate,
    atoms,
    gain,
    weight_in,
    grad_state,
    normed,
    keep_early,
    send_early,
    grad_atoms,
    keep,
    send,
    joined,
    late,
):
    join_projected(grad_q, center, near, far, grad_gate, joined)
    grad_normed = nt(joined[...], weight_in[0]).astype(BF16).astype(F32)
    product = tn(normed[...], joined[...])
    back, gained = norm_back(grad_normed, atoms[...].astype(F32), gain[0:1, :])
    grad_atoms[...] = (grad_state[...] + back).astype(BF16)
    for m in range(8):
        late[m, 0:16, :] = jnp.zeros((16, 128), F32)
        half = (m % 2) * 64
        late[m, 16:80, :] = product[half : half + 64, (m // 2) * 128 : (m // 2 + 1) * 128]
    late[2, 0:1, :] = gained
    core = lax.rem(lax.axis_index("seq"), 2)
    for ref, early, at in ((keep, keep_early, core), (send, send_early, 1 - core)):
        piece = late[pl.ds(at * 4, 4)]
        ref[:, 0:EARLY, :] = early[:, 0:EARLY, :].astype(ref.dtype)
        ref[:, EARLY:EXTRA, :] = (early[:, EARLY:EXTRA, :] + piece[:, 0:16]).astype(ref.dtype)
        ref[:, EXTRA:SPAN, :] = piece[:, 16:80].astype(ref.dtype)


def core_kernel(keep, got, own, one, two, three, whole):
    whole[...] = keep[...] + got[...].astype(F32)
    y = lax.axis_index("samp") // 2
    own[...] = whole[y]
    for k, ref in enumerate((one, two, three)):
        ref[...] = whole[lax.rem(y + k + 1, 4)].astype(BF16)


def far_kernel(own, one, two, three, score, score_one, score_two, score_three, message, kept, both):
    got = [ref[...].astype(F32) for ref in (one, two, three)]
    message[0:SPAN, :] = pair_up(own[...], got).astype(BF16)
    for n in range(2):
        for m in range(2):
            got = [v[n * 2 + m].astype(F32) for v in (score_one, score_two, score_three)]
            both[m, n] = pair_up(score[n * 2 + m].astype(F32), got)
    side = lax.rem(lax.axis_index("samp"), 2)
    kept[...] = both[side]
    away = both[1 - side].astype(BF16)
    for n in range(2):
        message[SPAN + n * 128 : SPAN + (n + 1) * 128, :] = away[n]


def quarter_kernel(own, one, two, three, half):
    y = lax.axis_index("samp") // 2
    half[y] = own[...]
    for k, ref in enumerate((one, two, three)):
        half[lax.rem(y + 3 - k, 4)] = ref[...]


def finish_kernel(half, got, grad_gain, inner, out, bias, token):
    def finish(lower, upper):
        def chunk(m):
            return (lower if m < 4 else upper).at[m % 4]

        def rows(row):
            return chunk(row // EARLY)[row % EARLY : row % EARLY + 16, :].astype(F32)

        def take(ref, base, blocks):
            for m in range(blocks):
                for r in range(0, 128, 16):
                    ref[r : r + 16, m * 128 : (m + 1) * 128] = rows(base + m * 128 + r)

        take(token, 0, 3)
        take(out.at[1], 384, 1)
        take(inner.at[1], 512, 4)
        take(out.at[0], 1024, 1)
        for m in range(8):
            half_rows = (m % 2) * 64
            inner[0, half_rows : half_rows + 64, (m // 2) * 128 : (m // 2 + 1) * 128] = chunk(m)[
                EXTRA:SPAN, :
            ].astype(F32)
        for layer in range(2):
            grad_gain[layer : layer + 1, :] = chunk(2 + layer)[EARLY:EXTRA, :].astype(F32)[0:1]
            head = lax.broadcasted_iota(jnp.int32, (HEADS, 128), 0)
            lane = lax.broadcasted_iota(jnp.int32, (HEADS, 128), 1) // QBLK
            choose = jnp.where(head == lane, 1.0, 0.0).astype(BF16)
            bias[layer] = nt(choose, chunk(layer)[EARLY:EXTRA, :])

    odd = odd_core()

    @pl.when(jnp.logical_not(odd))
    def _():
        finish(half, got)

    @pl.when(odd)
    def _():
        finish(got, half)


def expand_kernel(weight, kept, got, pair):
    first = kept[0] + got[SPAN : SPAN + 128, :].astype(F32)
    later = kept[1] + got[SPAN + 128 : SPAN + 256, :].astype(F32)
    for c in range(16):
        value = None
        for layer, ref in enumerate((first, later)):
            for h in range(HEADS):
                term = ref[h * 32 : (h + 1) * 32] * weight[layer, h, c]
                value = term if value is None else value + term
        pair[c * 32 : (c + 1) * 32, :] = value.astype(BF16)


def body(
    atoms_in,
    pair_feats,
    window_shift,
    atom_token,
    token_counts,
    token_grad,
    norm_gain,
    weight_in,
    weight_out,
    weight_bias,
    weight_token,
):
    rows = atoms_in.shape[1]
    blocks = pair_feats.shape[0]
    atom_total = rows * lax.axis_size("seq")
    atoms = atoms_in[0]
    grad = token_grad[0]
    pair = pair_feats.reshape(blocks, 512, 128)
    counts = token_counts.reshape(1, -1)
    token_row = atom_token.reshape(1, -1)
    ext = rows + 2 * HALO
    window = [pltpu.VMEM((ext, 128), F32), pltpu.VMEM((ext, 128), F32)]
    square = ((blocks, 128, 128), F32)
    wide = ((rows, 128), BF16)
    full = ((rows, 128), F32)
    kv_shape = ((rows, 256), BF16)
    rim = ((HALO, 256), BF16)
    scores_shape = ((blocks, 128, 128), BF16)
    channel_weight = weight_bias.transpose(0, 2, 1)

    begun = ((MESSAGE, 128), BF16)
    *rims0, shift_row = run(
        message_kernel,
        [begun, begun, ((1, 128), jnp.int32)],
        (window_shift, pair, atoms, grad, counts),
        hbm=range(5),
        scratch=[
            pltpu.SMEM(window_shift.shape, window_shift.dtype),
            pltpu.VMEM(grad.shape, grad.dtype),
            pltpu.VMEM(counts.shape, counts.dtype),
            pltpu.SemaphoreType.DMA((9,)),
        ],
        vmem=FIRST_VMEM,
    )
    rims0 = swapped(*rims0)
    normed0, q0, kv0, gate0 = run(
        first_kernel, [wide, wide, kv_shape, full], (atoms, norm_gain, weight_in)
    )
    bias0, bias1 = run(bias_kernel, [square, square], (channel_weight, pair), smem=(0,))
    ext_kv = ((ext, 256), BF16)
    state1, chances0, att0, kv0, normed1, q1, kv1, gate1 = run(
        partial(forward_kernel, atom_total),
        [full, square, wide, ext_kv, wide, wide, ext_kv, full],
        (
            shift_row,
            channel_weight,
            q0,
            kv0,
            *rims0,
            bias0,
            gate0,
            atoms,
            weight_out,
            norm_gain,
            weight_in,
        ),
        smem=(0, 1),
        scratch=[pltpu.VMEM((rows + 4 * HALO, 128), F32)] * 2,
    )
    back_scratch = [
        pltpu.VMEM((rows, 128), BF16),
        pltpu.VMEM((ext, 128), F32),
        pltpu.VMEM((ext, 128), F32),
    ]
    (
        att1,
        grad_update1,
        narrow_state,
        grad_hidden,
        grad_state2,
        grad_gate1,
        grad_q1,
        center1,
        near1,
        far1,
        scores1,
    ) = run(
        partial(middle_kernel, atom_total),
        [
            wide,
            wide,
            wide,
            ((rows, 384), BF16),
            full,
            wide,
            wide,
            ((rows, 256), F32),
            rim,
            rim,
            scores_shape,
        ],
        (
            shift_row,
            q1,
            kv1,
            bias1,
            gate1,
            state1,
            weight_out,
            weight_token,
            grad,
            counts,
            token_row,
            *rims0,
        ),
        smem=(0,),
        scratch=window + back_scratch,
    )
    rims1 = swapped(near1, far1)
    grad_token, grad_out1, grad_bias1 = run(
        middle_weights_kernel,
        [((384, 128), F32), ((128, 128), F32), ((16, 128), F32)],
        (pair, scores1, narrow_state, grad_hidden, att1, grad_update1),
    )
    rims1, grad_token = lax.optimization_barrier((rims1, grad_token))
    (
        joined1,
        grad_gain1,
        grad_update0,
        grad_state1,
        grad_gate0,
        grad_q0,
        center0,
        near0,
        far0,
        scores0,
    ) = run(
        backward_kernel,
        [
            ((rows, 512), BF16),
            ((1, 128), F32),
            wide,
            full,
            wide,
            wide,
            ((rows, 256), F32),
            rim,
            rim,
            ((blocks, 128, 128), BF16),
        ],
        (
            shift_row,
            grad_q1,
            center1,
            *rims1,
            grad_gate1,
            state1,
            norm_gain,
            weight_in,
            grad_state2,
            q0,
            kv0,
            gate0,
            att0,
            weight_out,
            chances0,
        ),
        smem=(0,),
        scratch=window + back_scratch,
    )
    last_rims = swapped(near0, far0)
    keep, send, *score_parts = run(
        backward_weights_kernel,
        [((4, EXTRA, 128), F32), ((4, EXTRA, 128), F32)] + [((4, 128, 128), BF16)] * 4,
        (
            pair,
            scores0,
            normed1,
            joined1,
            att0,
            grad_update0,
            grad_token,
            grad_out1,
            grad_bias1,
            grad_gain1,
            scores1,
        ),
        scratch=[pltpu.VMEM((8, EXTRA, 128), F32)],
    )
    grad_atoms, keep, send = run(
        last_kernel,
        [wide, ((4, SPAN, 128), F32), ((4, SPAN, 128), BF16)],
        (
            grad_q0,
            center0,
            *last_rims,
            grad_gate0,
            atoms,
            norm_gain,
            weight_in,
            grad_state1,
            normed0,
            keep,
            send,
        ),
        scratch=[pltpu.VMEM((rows, 512), BF16), pltpu.VMEM((8, 80, 128), F32)],
    )
    chunk = ((SPAN, 128), BF16)
    own, *pieces = run(
        core_kernel,
        [((SPAN, 128), F32), chunk, chunk, chunk],
        (keep, hop(send, 2, 1)),
        scratch=[pltpu.VMEM((4, SPAN, 128), F32)],
    )
    score_got = [hop(score_parts[k], 3, k) for k in range(1, 4)]
    message, kept = run(
        far_kernel,
        [((SPAN + 256, 128), BF16), ((2, 128, 128), F32)],
        (own, *[hop(v, 3, k + 1) for k, v in enumerate(pieces)], score_parts[0], *score_got),
        scratch=[pltpu.VMEM((2, 2, 128, 128), F32)],
    )
    far_got = hop(message, 4, 1)
    total = (message[0:SPAN].astype(F32) + far_got[0:SPAN].astype(F32)).astype(BF16)
    total = everyone(total, 0)
    (pair_sum,) = run(
        expand_kernel, [((512, 128), BF16)], (channel_weight, kept, far_got), smem=(0,)
    )
    total, pair_sum = lax.optimization_barrier((total, pair_sum))
    total = everyone(total, 1)
    (half,) = run(
        quarter_kernel,
        [((4, SPAN, 128), BF16)],
        (total, *[hop(total, 3, k) for k in range(1, 4)]),
    )
    grad_gain, grad_in, grad_out, grad_bias, grad_token = run(
        finish_kernel,
        [
            ((2, 128), F32),
            ((2, 128, 512), F32),
            ((2, 128, 128), F32),
            ((2, 4, 16), F32),
            ((128, 384), F32),
        ],
        (half, hop(half, 2, 1)),
    )
    return (
        grad_atoms[None],
        pair_sum.reshape(1, 16, 32, 128),
        grad_gain,
        grad_in,
        grad_out,
        grad_bias.transpose(0, 2, 1),
        grad_token,
    )


def solution(mesh):
    return jax.shard_map(
        body,
        mesh=mesh,
        in_specs=(
            P("samp", "seq", None),
            P("seq", None, None, None),
            P("seq"),
            P("seq"),
            P("seq"),
            P("samp", "seq", None),
            P(),
            P(),
            P(),
            P(),
            P(),
        ),
        out_specs=(
            P("samp", "seq", None),
            P(("seq", "samp"), None, None, None),
            P(),
            P(),
            P(),
            P(),
            P(),
        ),
        check_vma=False,
    )
```

```python
from functools import partial

import jax
import jax.numpy as jnp
from jax import lax
from jax.experimental import pallas as pl
from jax.experimental.pallas import tpu as pltpu
from jax.sharding import PartitionSpec as P

HALO = 64
KWIN = 128
QBLK = 32
HEADS = 4
EPSILON = 1e-05
F32 = jnp.float32
BF16 = jnp.bfloat16
DIMS = (4, 4, 2, 4, 2)
WORLD = ("seq", "samp")


def moves(part, step):
    pairs = []
    for source in range(256):
        place, rest = [], source
        for size in reversed(DIMS):
            place.append(rest % size)
            rest //= size
        place.reverse()
        place[part] = (place[part] + step) % DIMS[part]
        target = 0
        for size, value in zip(DIMS, place):
            target = target * size + value
        pairs.append((source, target))
    return pairs


def hop(value, part, step):
    return lax.ppermute(value, WORLD, moves(part, step))


def swapped(near, far):
    length = lax.axis_size("seq")
    chip = [(i, i ^ 1) for i in range(length)]
    across = [(i, i - 1 + 2 * (i % 2)) for i in range(length)]
    across = [(i, j) for i, j in across if 0 <= j < length]
    far = lax.ppermute(far, "seq", across)
    return lax.ppermute(near, "seq", chip), far


def pair_up(own, got):
    if len(got) == 1:
        return own + got[0]
    return (own + got[1]) + (got[0] + got[2])


def everyone(value, part):
    got = [hop(value, part, k).astype(F32) for k in range(1, DIMS[part])]
    return pair_up(value.astype(F32), got).astype(BF16)


def run(body, outs, args, smem=(), hbm=(), scratch=(), vmem=24, flops=10**8, nbytes=10**6):
    spaces = [pltpu.VMEM] * len(args)
    for i in smem:
        spaces[i] = pltpu.SMEM
    for i in hbm:
        spaces[i] = pltpu.HBM
    specs = [pl.BlockSpec(memory_space=space) for space in spaces]
    return pl.pallas_call(
        body,
        out_shape=[jax.ShapeDtypeStruct(s, d) for s, d in outs],
        in_specs=specs,
        out_specs=[pl.BlockSpec(memory_space=pltpu.VMEM) for _ in outs],
        scratch_shapes=list(scratch),
        compiler_params=pltpu.CompilerParams(vmem_limit_bytes=int(vmem * 2**20)),
        cost_estimate=pl.CostEstimate(flops=flops, bytes_accessed=nbytes, transcendentals=0),
    )(*args)


def nn(a, b):
    return jnp.dot(a, b, preferred_element_type=F32)


def nt(a, b):
    return lax.dot_general(a, b, (((1,), (1,)), ((), ())), preferred_element_type=F32)


def tn(a, b):
    return lax.dot_general(a, b, (((0,), (0,)), ((), ())), preferred_element_type=F32)


def stats(state):
    centred = state - jnp.mean(state, -1, keepdims=True)
    scale = lax.rsqrt(jnp.mean(centred * centred, -1, keepdims=True) + EPSILON)
    return centred * scale, scale


def sigmoid(value):
    return 1.0 / (1.0 + jnp.exp(-value))


def head_mask(rows):
    row = lax.broadcasted_iota(jnp.int32, (rows, 128), 0) // QBLK
    lane = lax.broadcasted_iota(jnp.int32, (rows, 128), 1) // 32
    return row == lane


def stacked(block, mask):
    return jnp.where(mask, jnp.concatenate([block.astype(F32)] * HEADS, 0), 0.0).astype(BF16)


def picked(wide, mask):
    wide = jnp.where(mask, wide, 0.0)
    return (wide[0:32] + wide[32:64]) + (wide[64:96] + wide[96:128])


def odd_core():
    return lax.rem(lax.axis_index("seq"), 2) == 1


def from_before(near, far):
    return jnp.where(odd_core(), near.astype(F32), far.astype(F32))


def from_after(near, far):
    return jnp.where(odd_core(), far.astype(F32), near.astype(F32))


def count_rows(counts):
    size = counts.shape[1]
    row = lax.broadcasted_iota(jnp.int32, (size, size), 0)
    lane = lax.broadcasted_iota(jnp.int32, (size, size), 1)
    column = jnp.sum(jnp.where(row == lane, counts.astype(F32), 0.0), -1, keepdims=True)
    return jnp.broadcast_to(column, (size, 128))


FIRST_VMEM = 62
PAIR_ROWS = 1024
ATOM_ROWS = PAIR_ROWS + 2 * HALO
MESSAGE = ATOM_ROWS + 16


def message_kernel(
    shift_far, pair, atoms, grad_far, counts_far, near, far, shift_row, shift, grad, counts, sems
):
    blocks, rows = pair.shape[0], atoms.shape[0]
    odd = odd_core()
    copies = [
        pltpu.make_async_copy(a, b, sems.at[i])
        for i, (a, b) in enumerate(((shift_far, shift), (grad_far, grad), (counts_far, counts)))
    ]
    bases = (jnp.where(odd, 0, blocks - 2), jnp.where(odd, blocks - 2, 0))
    for n, ref in enumerate((near, far)):
        for m in range(2):
            copies.append(
                pltpu.make_async_copy(
                    pair.at[bases[n] + m], ref.at[pl.ds(m * 512, 512)], sems.at[3 + n * 3 + m]
                )
            )
        first = pl.multiple_of(bases[n] * QBLK // (rows // 2) * (rows // 2), 128)
        copies.append(
            pltpu.make_async_copy(
                atoms.at[pl.ds(first, 2 * HALO)],
                ref.at[pl.ds(PAIR_ROWS, 2 * HALO)],
                sems.at[3 + n * 3 + 2],
            )
        )
    for copy in copies:
        copy.start()
    for copy in copies[:3]:
        copy.wait()
    size = counts.shape[1]
    lanes = lax.broadcasted_iota(jnp.int32, (1, size), 1)
    many = jnp.where(lanes == size - 1, counts[...].astype(F32), 0.0)
    many = jnp.sum(many, -1, keepdims=True)
    last = grad[16:32, :].astype(F32)[15:16, :]
    row = lax.broadcasted_iota(jnp.int32, (16, 128), 0)
    lane = lax.broadcasted_iota(jnp.int32, (16, 128), 1)
    group = jnp.where(row == 3, jnp.broadcast_to(many, (16, 128)), 0.0)
    for k in range(3):
        piece = jnp.broadcast_to(last[:, k * 128 : (k + 1) * 128], (16, 128))
        group = jnp.where(row == k, piece, group)
    for n, ref in enumerate((near, far)):
        value = group
        for m in range(2):
            place = jnp.logical_and(row == 4, lane == m)
            value = jnp.where(place, shift[bases[n] + m].astype(F32), value)
        ref[ATOM_ROWS:MESSAGE, :] = value.astype(BF16)
    lane = lax.broadcasted_iota(jnp.int32, (1, 128), 1)
    shifts = jnp.zeros((1, 128), jnp.int32)
    for j in range(blocks):
        shifts = jnp.where(lane == j, shift[j], shifts)
    shift_row[...] = shifts
    for copy in copies[3:]:
        copy.wait()


def first_kernel(atoms, gain, weight, normed, q, kv, gate):
    unit, _ = stats(atoms[...].astype(F32))
    normed[...] = (unit * gain[0:1, :]).astype(BF16)
    projected = nn(normed[...], weight[0])
    q[...] = projected[:, 0:128].astype(BF16)
    kv[...] = projected[:, 128:384].astype(BF16)
    gate[...] = sigmoid(projected[:, 384:512])


def block_bias(weight, layers, part):
    totals = [[None] * HEADS for _ in layers]
    for c in range(16):
        value = part(c)
        for n, layer in enumerate(layers):
            for h in range(HEADS):
                term = value * weight[layer, h, c]
                totals[n][h] = term if c == 0 else totals[n][h] + term
    return totals


def bias_kernel(weight, pair, first, later):
    def block(j, carry):
        totals = block_bias(
            weight, (0, 1), lambda c: pair[j, c * 32 : (c + 1) * 32, :].astype(F32)
        )
        for ref, total in zip((first, later), totals):
            for h in range(HEADS):
                ref[j, h * 32 : (h + 1) * 32, :] = total[h]
        return carry

    lax.fori_loop(0, pair.shape[0], block, 0)


def load_window(kv, keys, values):
    keys[...] = kv[:, 0:128].astype(F32)
    values[...] = kv[:, 128:256].astype(F32)


def windows(shifts, q, keys, values, margin):
    mask = head_mask(128)
    spans = [pl.ds(j * QBLK + shift + margin, KWIN) for j, shift in enumerate(shifts)]
    wide = [stacked(q[j * QBLK : (j + 1) * QBLK, :], mask) for j in range(len(spans))]
    key = [keys[span, :].astype(BF16) for span in spans]
    value = [values[span, :].astype(BF16) for span in spans]
    return spans, wide, key, value


def attention_forward(shifts, found, bias, first, atom_total):
    _, wide, key, value = found
    count = len(wide)
    mask = head_mask(128)
    lane = lax.broadcasted_iota(jnp.int32, (1, KWIN), 1)
    scores = [nt(wide[j], key[j]) for j in range(count)]
    chances = []
    for j in range(count):
        place = first + (j * QBLK + shifts[j]) + lane
        inside = jnp.logical_and(place >= 0, place < atom_total)
        weights = jnp.where(inside, jnp.exp(scores[j] * (32.0**-0.5) + bias[j]), 0.0)
        query = first + j * QBLK
        real = jnp.logical_and(query >= 0, query < atom_total)
        size = jnp.where(real, jnp.sum(weights, -1, keepdims=True), 1.0)
        chances.append(weights * (1.0 / size))
    out = [nn(chances[j].astype(BF16), value[j]) for j in range(count)]
    return chances, jnp.concatenate([picked(v, mask) for v in out], 0).astype(BF16)


def attention_backward(
    found, chances, grad_att, edge, grad_q, grad_keys, grad_values, score_grad
):
    spans, wide, key, value = found
    count = len(wide)
    own = range(edge, count - edge)
    mask = head_mask(128)
    out = [stacked(grad_att[j * QBLK : (j + 1) * QBLK, :], mask) for j in range(count)]
    rising = [nt(out[j], value[j]) for j in range(count)]
    value_back = [tn(chances[j].astype(BF16), out[j]) for j in range(count)]
    scaled = []
    for j in range(count):
        term = chances[j] * rising[j].astype(BF16).astype(F32)
        grad_score = term - chances[j] * jnp.sum(term, -1, keepdims=True)
        if j in own:
            score_grad[j - edge] = grad_score.astype(BF16)
        scaled.append((grad_score * (32.0**-0.5)).astype(BF16))
    query_back = [nn(scaled[j], key[j]) for j in own]
    key_back = [tn(scaled[j], wide[j]) for j in range(count)]
    for n, value in enumerate(query_back):
        grad_q[n * QBLK : (n + 1) * QBLK, 0:128] = picked(value, mask).astype(BF16)
    grad_keys[...] = jnp.zeros_like(grad_keys)
    grad_values[...] = jnp.zeros_like(grad_values)
    for j in range(count):
        grad_keys[spans[j], :] += key_back[j].astype(BF16).astype(F32)
        grad_values[spans[j], :] += value_back[j].astype(BF16).astype(F32)


def share_scores(scores, parts):
    y = lax.axis_index("samp") // 2
    for k, ref in enumerate(parts):
        for n, score in enumerate(scores):
            ref[n * 2 : n * 2 + 2] = score[pl.ds(lax.rem(y + k, 4) * 2, 2)]


def forward_kernel(
    atom_total,
    shift,
    channel_weight,
    q,
    kv,
    near,
    far,
    bias,
    gate,
    atoms,
    weight_out,
    gain,
    weight_in,
    state,
    chances,
    att,
    kv_all,
    q_all,
    gate_all,
    shift_all,
    normed,
    q_next,
    kv_next,
    gate_next,
    keys,
    values,
):
    blocks, rows = bias.shape[0], q.shape[0]
    edge = HALO // QBLK
    first = lax.axis_index("seq") * rows
    there = slice(PAIR_ROWS, ATOM_ROWS)
    before, after = from_before(near[there], far[there]), from_after(near[there], far[there])
    beside = jnp.concatenate([before, after], 0)
    unit, _ = stats(beside)
    projected = nn((unit * gain[0:1, :]).astype(BF16), weight_in[0])
    for ref, at in ((keys, 128), (values, 256)):
        ref[0 : 2 * HALO, :] = projected[0 : 2 * HALO, at : at + 128].astype(BF16).astype(F32)
        ref[2 * HALO : 2 * HALO + rows, :] = kv[:, at - 128 : at].astype(F32)
        ref[2 * HALO + rows :, :] = projected[2 * HALO :, at : at + 128].astype(BF16).astype(F32)
    kv_all[:, 0:128] = keys[...].astype(BF16)
    kv_all[:, 128:256] = values[...].astype(BF16)
    ends = slice(HALO, 2 * HALO), slice(2 * HALO, 3 * HALO)
    queries = [projected[end, 0:128].astype(BF16) for end in ends]
    queries = jnp.concatenate([queries[0], q[...], queries[1]], 0)
    gates = [sigmoid(projected[end, 384:512]) for end in ends]
    gates = jnp.concatenate([gates[0], gate[...], gates[1]], 0)
    q_all[...] = queries
    gate_all[...] = gates
    began = jnp.concatenate([beside[ends[0]], atoms[...].astype(F32), beside[ends[1]]], 0)
    biases, shifts = [], []
    tail = slice(ATOM_ROWS, MESSAGE)
    row = lax.broadcasted_iota(jnp.int32, (16, 128), 0)
    lane = lax.broadcasted_iota(jnp.int32, (16, 128), 1)
    for pick in (from_before, from_after):
        group = pick(near[tail], far[tail])
        for m in range(edge):
            chosen = jnp.where(jnp.logical_and(row == 4, lane == m), group, 0.0)
            value = jnp.sum(chosen).astype(jnp.int32)
            shifts.append(jnp.clip(value, -HALO, QBLK + HALO - KWIN))

            def part(c):
                span = slice(m * 512 + c * 32, m * 512 + (c + 1) * 32)
                return pick(near[span], far[span])

            (total,) = block_bias(channel_weight, (0,), part)
            biases.append(jnp.concatenate(total, 0))
    biases = biases[:edge] + [bias[j] for j in range(blocks)] + biases[edge:]
    shifts = shifts[:edge] + [shift[0, j] for j in range(blocks)] + shifts[edge:]
    lanes = lax.broadcasted_iota(jnp.int32, (1, 128), 1)
    row_of = jnp.zeros((1, 128), jnp.int32)
    for j, value in enumerate(shifts):
        row_of = jnp.where(lanes == j, value, row_of)
    shift_all[...] = row_of
    found = windows(shifts, queries, keys, values, 2 * HALO - HALO)
    kept, attended = attention_forward(shifts, found, biases, first - HALO, atom_total)
    for j, chance in enumerate(kept):
        chances[j] = chance
    att[...] = attended
    done = began + gates * nn(attended, weight_out[0])
    state[...] = done
    unit, _ = stats(done)
    normed_all = (unit * gain[1:2, :]).astype(BF16)
    normed[...] = normed_all[HALO : HALO + rows]
    projected = nn(normed_all, weight_in[1])
    place = first - HALO + lax.broadcasted_iota(jnp.int32, (rows + 2 * HALO, 1), 0)
    inside = jnp.logical_and(place >= 0, place < atom_total)
    kv_next[...] = jnp.where(inside, projected[:, 128:384], 0.0).astype(BF16)
    q_next[...] = projected[HALO : HALO + rows, 0:128].astype(BF16)
    gate_next[...] = sigmoid(projected[HALO : HALO + rows, 384:512])


def send_halo(grad_keys, grad_values, grad_q, grad_gate, grad_state, center, outgoing, near, far):
    rows = center.shape[0]
    ends = []
    for own, other in ((slice(0, HALO), 0), (slice(rows - HALO, rows), HALO + rows)):
        there = slice(other, other + HALO)
        here = slice(HALO + own.start, HALO + own.stop)
        parts = [grad_keys[there, :], grad_values[there, :], grad_keys[here, :]]
        parts += [grad_values[here, :], grad_q[own, :].astype(F32), grad_gate[own, :].astype(F32)]
        ends.append(jnp.concatenate([*parts, grad_state[own, :]], 1))
    near[...] = jnp.where(odd_core(), ends[0], ends[1]).astype(BF16)
    far[...] = jnp.where(odd_core(), ends[1], ends[0]).astype(BF16)
    outgoing[0:HALO, :] = ends[0][:, 0:256].astype(BF16)
    outgoing[HALO:, :] = ends[1][:, 0:256].astype(BF16)
    for ref, at in ((grad_keys, 0), (grad_values, 128)):
        center[:, at : at + 128] = ref[HALO : HALO + rows, :]


def middle_kernel(
    atom_total,
    shift,
    q,
    kv,
    bias,
    gate,
    state,
    weight_out,
    weight_token,
    grad,
    counts,
    atom_token,
    near_first,
    far_first,
    att,
    grad_update,
    narrow_state,
    grad_hidden,
    grad_state,
    grad_gate,
    grad_q,
    center,
    outgoing,
    grad_near,
    grad_far,
    score_grad,
    keys,
    values,
    grad_keys,
    grad_values,
):
    load_window(kv, keys, values)
    shifts = [shift[0, j + HALO // QBLK] for j in range(bias.shape[0])]
    found = windows(shifts, q, keys, values, HALO)
    first = lax.axis_index("seq") * q.shape[0]
    chances, attended = attention_forward(
        shifts, found, [bias[j] for j in range(bias.shape[0])], first, atom_total
    )
    att[...] = attended
    update = nn(attended, weight_out[1])
    after = (state[HALO : HALO + q.shape[0], :] + gate[...] * update).astype(BF16)
    narrow_state[...] = after
    tokens = grad.shape[0]
    atoms = q.shape[0]
    place = atom_token[...] - lax.axis_index("seq") * tokens
    place = jnp.where(place < 0, tokens + 15, place)
    chosen = lax.broadcasted_iota(jnp.int32, (tokens + 16, atoms), 0) == place
    chosen = jnp.where(chosen, 1.0, 0.0).astype(BF16)
    own = jnp.concatenate([grad[...], count_rows(counts[...]).astype(BF16)], 1)
    group = from_before(near_first[ATOM_ROWS:MESSAGE, :], far_first[ATOM_ROWS:MESSAGE, :])
    before = [jnp.broadcast_to(group[k : k + 1], (16, 128)) for k in range(4)]
    before = jnp.concatenate(before, 1).astype(BF16)
    taken = tn(chosen, jnp.concatenate([own, before], 0))
    many = taken[:, 384:512]
    cotangent = taken[:, 0:384] / jnp.concatenate([many] * 3, 1)
    hidden = nn(after, weight_token[...])
    open_ = sigmoid(hidden)
    back = (cotangent * (open_ * (1.0 + hidden * (1.0 - open_)))).astype(BF16)
    grad_hidden[...] = back
    rising = nt(back, weight_token[...]).astype(BF16).astype(F32)
    grad_state[...] = rising
    gates = gate[...]
    grad_gate[...] = (rising * update * gates * (1.0 - gates)).astype(BF16)
    change = (rising * gates).astype(BF16)
    grad_update[...] = change
    grad_att = nt(change, weight_out[1]).astype(BF16)
    attention_backward(found, chances, grad_att, 0, grad_q, grad_keys, grad_values, score_grad)
    send_halo(
        grad_keys,
        grad_values,
        grad_q,
        grad_gate,
        grad_state,
        center,
        outgoing,
        grad_near,
        grad_far,
    )


def pair_weight_grad(pair, scores, out):
    left = [pair[block] for block, _ in scores]
    product = nt(jnp.concatenate(left, 1), jnp.concatenate([piece for _, piece in scores], 1))
    row = lax.rem(lax.broadcasted_iota(jnp.int32, product.shape, 0), QBLK)
    lane = lax.rem(lax.broadcasted_iota(jnp.int32, product.shape, 1), QBLK)
    product = jnp.where(row == lane, product, 0.0)
    for c in range(16):
        out[c : c + 1, :] = jnp.sum(product[c * 32 : (c + 1) * 32], 0, keepdims=True)


def middle_weights_kernel(
    pair, scores, narrow_state, grad_hidden, att, grad_update, token, out, bias
):
    pair_weight_grad(pair, [(j, scores[j]) for j in range(pair.shape[0])], bias)
    product = tn(narrow_state[...], grad_hidden[...])
    for m in range(3):
        token[m * 128 : (m + 1) * 128, :] = product[:, m * 128 : (m + 1) * 128]
    out[...] = tn(att[...], grad_update[...])


def norm_back(grad_normed, state, gain):
    unit, scale = stats(state)
    back = grad_normed * gain
    back = scale * (
        back - jnp.mean(back, -1, keepdims=True) - unit * jnp.mean(back * unit, -1, keepdims=True)
    )
    return back, grad_normed * unit


def backward_kernel(
    shift,
    grad_q_later,
    center_later,
    outgoing,
    near,
    far,
    grad_gate_later,
    state,
    gain,
    weight_in,
    grad_state_later,
    q,
    kv,
    gate,
    att,
    weight_out,
    chances,
    atoms,
    joined_later,
    joined,
    grad_gain,
    grad_update,
    score_grad,
    grad_atoms,
    joined_all,
    keys,
    values,
    grad_keys,
    grad_values,
):
    rows = center_later.shape[0]
    edge = HALO // QBLK
    own = slice(HALO, HALO + rows)
    load_window(kv, keys, values)
    before, after = from_before(near[...], far[...]), from_after(near[...], far[...])
    for place, part, other in ((0, before, 0), (HALO + rows, after, HALO)):
        there = slice(place, place + HALO)
        joined_all[there, 0:128] = part[:, 512:640].astype(BF16)
        shares = part[:, 256:512] + outgoing[other : other + HALO, :].astype(F32)
        joined_all[there, 128:384] = shares.astype(BF16)
        joined_all[there, 384:512] = part[:, 640:768].astype(BF16)
    received = jnp.concatenate(
        [before[:, 0:256], jnp.zeros((rows - 2 * HALO, 256), F32), after[:, 0:256]], 0
    )
    joined_all[own, 0:128] = grad_q_later[...]
    joined_all[own, 128:384] = (center_later[...] + received).astype(BF16)
    joined_all[own, 384:512] = grad_gate_later[...]
    joined_later[...] = joined_all[own, :]
    grad_normed = nt(joined_all[...], weight_in[1]).astype(BF16).astype(F32)
    back, gained = norm_back(grad_normed, state[...], gain[1:2, :])
    grad_gain[1:2, :] = jnp.sum(gained[own], 0, keepdims=True)
    rising = [before[:, 768:896], grad_state_later[...], after[:, 768:896]]
    rising = jnp.concatenate(rising, 0) + back
    change = (rising * gate[...]).astype(BF16)
    grad_update[...] = change[own]
    grad_att = nt(change, weight_out[0]).astype(BF16)
    gates = gate[own, :]
    update = nn(att[own, :], weight_out[0])
    joined[:, 384:512] = (rising[own] * update * gates * (1.0 - gates)).astype(BF16)
    shifts = [shift[0, j] for j in range(chances.shape[0])]
    found = windows(shifts, q, keys, values, HALO)
    kept = [chances[j] for j in range(chances.shape[0])]
    attention_backward(found, kept, grad_att, edge, joined, grad_keys, grad_values, score_grad)
    inner = slice(2 * HALO, 2 * HALO + rows)
    joined[:, 128:256] = grad_keys[inner, :].astype(BF16)
    joined[:, 256:384] = grad_values[inner, :].astype(BF16)
    grad_normed = nt(joined[...], weight_in[0]).astype(BF16).astype(F32)
    back, gained = norm_back(grad_normed, atoms[...].astype(F32), gain[0:1, :])
    grad_gain[0:1, :] = jnp.sum(gained, 0, keepdims=True)
    grad_atoms[...] = (rising[own] + back).astype(BF16)


EARLY = 144
EXTRA = 160
SPAN = 224


def backward_weights_kernel(
    pair,
    scores,
    normed_first,
    joined_first,
    normed,
    joined,
    att,
    grad_update,
    token,
    out_later,
    bias_later,
    grad_gain,
    scores_later,
    keep,
    send,
    own,
    one,
    two,
    three,
    whole,
):
    share_scores((scores, scores_later), (own, one, two, three))

    def put(row, value):
        whole[row // EARLY, row % EARLY : row % EARLY + 16, :] = value

    for r in range(0, 384, 16):
        put(r, token[r : r + 16, :])
    for r in range(0, 128, 16):
        put(384 + r, out_later[r : r + 16, :])
    inner = tn(normed[...], joined[...])
    for m in range(4):
        for r in range(0, 128, 16):
            put(512 + m * 128 + r, inner[r : r + 16, m * 128 : (m + 1) * 128])
    out = tn(att[HALO : HALO + joined.shape[0], :], grad_update[...])
    for r in range(0, 128, 16):
        put(1024 + r, out[r : r + 16, :])
    for m in range(2, 8):
        whole[m, EARLY:EXTRA, :] = jnp.zeros((16, 128), F32)
    pair_weight_grad(
        pair, [(j, scores[j]) for j in range(pair.shape[0])], whole.at[0, EARLY:EXTRA]
    )
    whole[1, EARLY:EXTRA, :] = bias_later[...]
    whole[2, EARLY : EARLY + 1, :] = grad_gain[0:1, :]
    whole[3, EARLY : EARLY + 1, :] = grad_gain[1:2, :]
    inner = tn(normed_first[...], joined_first[...])
    for m in range(8):
        half = (m % 2) * 64
        whole[m, EXTRA:SPAN, :] = inner[half : half + 64, (m // 2) * 128 : (m // 2 + 1) * 128]
    core = lax.rem(lax.axis_index("seq"), 2)
    keep[...] = whole[pl.ds(core * 4, 4)]
    send[...] = whole[pl.ds((1 - core) * 4, 4)].astype(BF16)


def core_kernel(keep, got, own, one, two, three, whole):
    whole[...] = keep[...] + got[...].astype(F32)
    y = lax.axis_index("samp") // 2
    own[...] = whole[y]
    for k, ref in enumerate((one, two, three)):
        ref[...] = whole[lax.rem(y + k + 1, 4)].astype(BF16)


def far_kernel(own, one, two, three, score, score_one, score_two, score_three, message, kept, both):
    got = [ref[...].astype(F32) for ref in (one, two, three)]
    message[0:SPAN, :] = pair_up(own[...], got).astype(BF16)
    for n in range(2):
        for m in range(2):
            got = [v[n * 2 + m].astype(F32) for v in (score_one, score_two, score_three)]
            both[m, n] = pair_up(score[n * 2 + m].astype(F32), got)
    side = lax.rem(lax.axis_index("samp"), 2)
    kept[...] = both[side]
    away = both[1 - side].astype(BF16)
    for n in range(2):
        message[SPAN + n * 128 : SPAN + (n + 1) * 128, :] = away[n]


def quarter_kernel(own, one, two, three, half):
    y = lax.axis_index("samp") // 2
    half[y] = own[...]
    for k, ref in enumerate((one, two, three)):
        half[lax.rem(y + 3 - k, 4)] = ref[...]


def finish_kernel(half, got, grad_gain, inner, out, bias, token):
    def finish(lower, upper):
        def chunk(m):
            return (lower if m < 4 else upper).at[m % 4]

        def rows(row):
            return chunk(row // EARLY)[row % EARLY : row % EARLY + 16, :].astype(F32)

        def take(ref, base, blocks):
            for m in range(blocks):
                for r in range(0, 128, 16):
                    ref[r : r + 16, m * 128 : (m + 1) * 128] = rows(base + m * 128 + r)

        take(token, 0, 3)
        take(out.at[1], 384, 1)
        take(inner.at[1], 512, 4)
        take(out.at[0], 1024, 1)
        for m in range(8):
            half_rows = (m % 2) * 64
            inner[0, half_rows : half_rows + 64, (m // 2) * 128 : (m // 2 + 1) * 128] = chunk(m)[
                EXTRA:SPAN, :
            ].astype(F32)
        for layer in range(2):
            grad_gain[layer : layer + 1, :] = chunk(2 + layer)[EARLY:EXTRA, :].astype(F32)[0:1]
            head = lax.broadcasted_iota(jnp.int32, (HEADS, 128), 0)
            lane = lax.broadcasted_iota(jnp.int32, (HEADS, 128), 1) // QBLK
            choose = jnp.where(head == lane, 1.0, 0.0).astype(BF16)
            bias[layer] = nt(choose, chunk(layer)[EARLY:EXTRA, :])

    odd = odd_core()

    @pl.when(jnp.logical_not(odd))
    def _():
        finish(half, got)

    @pl.when(odd)
    def _():
        finish(got, half)


def expand_kernel(weight, kept, got, pair):
    first = kept[0] + got[SPAN : SPAN + 128, :].astype(F32)
    later = kept[1] + got[SPAN + 128 : SPAN + 256, :].astype(F32)
    for c in range(16):
        value = None
        for layer, ref in enumerate((first, later)):
            for h in range(HEADS):
                term = ref[h * 32 : (h + 1) * 32] * weight[layer, h, c]
                value = term if value is None else value + term
        pair[c * 32 : (c + 1) * 32, :] = value.astype(BF16)


def body(
    atoms_in,
    pair_feats,
    window_shift,
    atom_token,
    token_counts,
    token_grad,
    norm_gain,
    weight_in,
    weight_out,
    weight_bias,
    weight_token,
):
    rows = atoms_in.shape[1]
    blocks = pair_feats.shape[0]
    atom_total = rows * lax.axis_size("seq")
    atoms = atoms_in[0]
    grad = token_grad[0]
    pair = pair_feats.reshape(blocks, 512, 128)
    counts = token_counts.reshape(1, -1)
    token_row = atom_token.reshape(1, -1)
    ext = rows + 2 * HALO
    window = [pltpu.VMEM((ext, 128), F32), pltpu.VMEM((ext, 128), F32)]
    square = ((blocks, 128, 128), F32)
    wide = ((rows, 128), BF16)
    full = ((rows, 128), F32)
    kv_shape = ((rows, 256), BF16)
    rim = ((HALO, 896), BF16)
    scores_shape = ((blocks, 128, 128), BF16)
    channel_weight = weight_bias.transpose(0, 2, 1)

    begun = ((MESSAGE, 128), BF16)
    *rims0, shift_row = run(
        message_kernel,
        [begun, begun, ((1, 128), jnp.int32)],
        (window_shift, pair, atoms, grad, counts),
        hbm=range(5),
        scratch=[
            pltpu.SMEM(window_shift.shape, window_shift.dtype),
            pltpu.VMEM(grad.shape, grad.dtype),
            pltpu.VMEM(counts.shape, counts.dtype),
            pltpu.SemaphoreType.DMA((9,)),
        ],
        vmem=FIRST_VMEM,
    )
    rims0 = swapped(*rims0)
    normed0, q0, kv0, gate0 = run(
        first_kernel, [wide, wide, kv_shape, full], (atoms, norm_gain, weight_in)
    )
    bias0, bias1 = run(bias_kernel, [square, square], (channel_weight, pair), smem=(0,))
    ext_kv = ((ext, 256), BF16)
    more = blocks + 2 * HALO // QBLK
    broad = ext + 2 * HALO
    state1, chances0, att0, kv0, q0, gate0, shift_row, normed1, q1, kv1, gate1 = run(
        partial(forward_kernel, atom_total),
        [
            ((ext, 128), F32),
            ((more, 128, 128), F32),
            ((ext, 128), BF16),
            ((broad, 256), BF16),
            ((ext, 128), BF16),
            ((ext, 128), F32),
            ((1, 128), jnp.int32),
            wide,
            wide,
            ext_kv,
            full,
        ],
        (
            shift_row,
            channel_weight,
            q0,
            kv0,
            *rims0,
            bias0,
            gate0,
            atoms,
            weight_out,
            norm_gain,
            weight_in,
        ),
        smem=(0, 1),
        scratch=[pltpu.VMEM((rows + 4 * HALO, 128), F32)] * 2,
    )
    (
        att1,
        grad_update1,
        narrow_state,
        grad_hidden,
        grad_state2,
        grad_gate1,
        grad_q1,
        center1,
        outgoing,
        near1,
        far1,
        scores1,
    ) = run(
        partial(middle_kernel, atom_total),
        [
            wide,
            wide,
            wide,
            ((rows, 384), BF16),
            full,
            wide,
            wide,
            ((rows, 256), F32),
            ((2 * HALO, 256), BF16),
            rim,
            rim,
            scores_shape,
        ],
        (
            shift_row,
            q1,
            kv1,
            bias1,
            gate1,
            state1,
            weight_out,
            weight_token,
            grad,
            counts,
            token_row,
            *rims0,
        ),
        smem=(0,),
        scratch=window + window,
    )
    rims1 = swapped(near1, far1)
    grad_token, grad_out1, grad_bias1 = run(
        middle_weights_kernel,
        [((384, 128), F32), ((128, 128), F32), ((16, 128), F32)],
        (pair, scores1, narrow_state, grad_hidden, att1, grad_update1),
    )
    rims1, grad_token = lax.optimization_barrier((rims1, grad_token))
    joined1, joined0, gains, grad_update0, scores0, grad_atoms = run(
        backward_kernel,
        [((rows, 512), BF16), ((rows, 512), BF16), ((2, 128), F32), wide, scores_shape, wide],
        (
            shift_row,
            grad_q1,
            center1,
            outgoing,
            *rims1,
            grad_gate1,
            state1,
            norm_gain,
            weight_in,
            grad_state2,
            q0,
            kv0,
            gate0,
            att0,
            weight_out,
            chances0,
            atoms,
        ),
        smem=(0,),
        scratch=[pltpu.VMEM((ext, 512), BF16)] + [pltpu.VMEM((broad, 128), F32)] * 4,
    )
    keep, send, *score_parts = run(
        backward_weights_kernel,
        [((4, SPAN, 128), F32), ((4, SPAN, 128), BF16)] + [((4, 128, 128), BF16)] * 4,
        (
            pair,
            scores0,
            normed0,
            joined0,
            normed1,
            joined1,
            att0,
            grad_update0,
            grad_token,
            grad_out1,
            grad_bias1,
            gains,
            scores1,
        ),
        scratch=[pltpu.VMEM((8, SPAN, 128), F32)],
    )
    chunk = ((SPAN, 128), BF16)
    own, *pieces = run(
        core_kernel,
        [((SPAN, 128), F32), chunk, chunk, chunk],
        (keep, hop(send, 2, 1)),
        scratch=[pltpu.VMEM((4, SPAN, 128), F32)],
    )
    score_got = [hop(score_parts[k], 3, k) for k in range(1, 4)]
    message, kept = run(
        far_kernel,
        [((SPAN + 256, 128), BF16), ((2, 128, 128), F32)],
        (own, *[hop(v, 3, k + 1) for k, v in enumerate(pieces)], score_parts[0], *score_got),
        scratch=[pltpu.VMEM((2, 2, 128, 128), F32)],
    )
    far_got = hop(message, 4, 1)
    total = (message[0:SPAN].astype(F32) + far_got[0:SPAN].astype(F32)).astype(BF16)
    total = everyone(total, 0)
    (pair_sum,) = run(
        expand_kernel, [((512, 128), BF16)], (channel_weight, kept, far_got), smem=(0,)
    )
    total, pair_sum = lax.optimization_barrier((total, pair_sum))
    total = everyone(total, 1)
    (half,) = run(
        quarter_kernel,
        [((4, SPAN, 128), BF16)],
        (total, *[hop(total, 3, k) for k in range(1, 4)]),
    )
    grad_gain, grad_in, grad_out, grad_bias, grad_token = run(
        finish_kernel,
        [
            ((2, 128), F32),
            ((2, 128, 512), F32),
            ((2, 128, 128), F32),
            ((2, 4, 16), F32),
            ((128, 384), F32),
        ],
        (half, hop(half, 2, 1)),
    )
    return (
        grad_atoms[None],
        pair_sum.reshape(1, 16, 32, 128),
        grad_gain,
        grad_in,
        grad_out,
        grad_bias.transpose(0, 2, 1),
        grad_token,
    )


def solution(mesh):
    return jax.shard_map(
        body,
        mesh=mesh,
        in_specs=(
            P("samp", "seq", None),
            P("seq", None, None, None),
            P("seq"),
            P("seq"),
            P("seq"),
            P("samp", "seq", None),
            P(),
            P(),
            P(),
            P(),
            P(),
        ),
        out_specs=(
            P("samp", "seq", None),
            P(("seq", "samp"), None, None, None),
            P(),
            P(),
            P(),
            P(),
            P(),
        ),
        check_vma=False,
    )
```

```python
from functools import partial

import jax
import jax.numpy as jnp
from jax import lax
from jax.experimental import pallas as pl
from jax.experimental.pallas import tpu as pltpu
from jax.sharding import PartitionSpec as P

HALO = 64
KWIN = 128
QBLK = 32
HEADS = 4
EPSILON = 1e-05
F32 = jnp.float32
BF16 = jnp.bfloat16
DIMS = (4, 4, 2, 4, 2)
WORLD = ("seq", "samp")


def moves(part, step):
    pairs = []
    for source in range(256):
        place, rest = [], source
        for size in reversed(DIMS):
            place.append(rest % size)
            rest //= size
        place.reverse()
        place[part] = (place[part] + step) % DIMS[part]
        target = 0
        for size, value in zip(DIMS, place):
            target = target * size + value
        pairs.append((source, target))
    return pairs


def hop(value, part, step):
    return lax.ppermute(value, WORLD, moves(part, step))


def swapped(near, far):
    length = lax.axis_size("seq")
    chip = [(i, i ^ 1) for i in range(length)]
    across = [(i, i - 1 + 2 * (i % 2)) for i in range(length)]
    across = [(i, j) for i, j in across if 0 <= j < length]
    far = lax.ppermute(far, "seq", across)
    return lax.ppermute(near, "seq", chip), far


def pair_up(own, got):
    if len(got) == 1:
        return own + got[0]
    return (own + got[1]) + (got[0] + got[2])


def everyone(value, part):
    got = [hop(value, part, k).astype(F32) for k in range(1, DIMS[part])]
    return pair_up(value.astype(F32), got).astype(BF16)


def run(body, outs, args, smem=(), hbm=(), scratch=(), vmem=24, flops=10**8, nbytes=10**6):
    spaces = [pltpu.VMEM] * len(args)
    for i in smem:
        spaces[i] = pltpu.SMEM
    for i in hbm:
        spaces[i] = pltpu.HBM
    specs = [pl.BlockSpec(memory_space=space) for space in spaces]
    return pl.pallas_call(
        body,
        out_shape=[jax.ShapeDtypeStruct(s, d) for s, d in outs],
        in_specs=specs,
        out_specs=[pl.BlockSpec(memory_space=pltpu.VMEM) for _ in outs],
        scratch_shapes=list(scratch),
        compiler_params=pltpu.CompilerParams(vmem_limit_bytes=int(vmem * 2**20)),
        cost_estimate=pl.CostEstimate(flops=flops, bytes_accessed=nbytes, transcendentals=0),
    )(*args)


def nn(a, b):
    return jnp.dot(a, b, preferred_element_type=F32)


def nt(a, b):
    return lax.dot_general(a, b, (((1,), (1,)), ((), ())), preferred_element_type=F32)


def tn(a, b):
    return lax.dot_general(a, b, (((0,), (0,)), ((), ())), preferred_element_type=F32)


def stats(state):
    centred = state - jnp.mean(state, -1, keepdims=True)
    scale = lax.rsqrt(jnp.mean(centred * centred, -1, keepdims=True) + EPSILON)
    return centred * scale, scale


def sigmoid(value):
    return 1.0 / (1.0 + jnp.exp(-value))


def head_mask(rows):
    row = lax.broadcasted_iota(jnp.int32, (rows, 128), 0) // QBLK
    lane = lax.broadcasted_iota(jnp.int32, (rows, 128), 1) // 32
    return row == lane


def stacked(block, mask):
    return jnp.where(mask, jnp.concatenate([block.astype(F32)] * HEADS, 0), 0.0).astype(BF16)


def picked(wide, mask):
    wide = jnp.where(mask, wide, 0.0)
    return (wide[0:32] + wide[32:64]) + (wide[64:96] + wide[96:128])


def odd_core():
    return lax.rem(lax.axis_index("seq"), 2) == 1


def from_before(near, far):
    return jnp.where(odd_core(), near.astype(F32), far.astype(F32))


def from_after(near, far):
    return jnp.where(odd_core(), far.astype(F32), near.astype(F32))


def count_rows(counts):
    size = counts.shape[1]
    row = lax.broadcasted_iota(jnp.int32, (size, size), 0)
    lane = lax.broadcasted_iota(jnp.int32, (size, size), 1)
    column = jnp.sum(jnp.where(row == lane, counts.astype(F32), 0.0), -1, keepdims=True)
    return jnp.broadcast_to(column, (size, 128))


FIRST_VMEM = 62
PAIR_ROWS = 1024
ATOM_ROWS = PAIR_ROWS + 2 * HALO
MESSAGE = ATOM_ROWS + 16


def message_kernel(
    shift_far, pair, atoms, grad_far, counts_far, near, far, shift_row, shift, grad, counts, sems
):
    blocks, rows = pair.shape[0], atoms.shape[0]
    odd = odd_core()
    copies = [
        pltpu.make_async_copy(a, b, sems.at[i])
        for i, (a, b) in enumerate(((shift_far, shift), (grad_far, grad), (counts_far, counts)))
    ]
    bases = (jnp.where(odd, 0, blocks - 2), jnp.where(odd, blocks - 2, 0))
    for n, ref in enumerate((near, far)):
        for m in range(2):
            copies.append(
                pltpu.make_async_copy(
                    pair.at[bases[n] + m], ref.at[pl.ds(m * 512, 512)], sems.at[3 + n * 3 + m]
                )
            )
        first = pl.multiple_of(bases[n] * QBLK // (rows // 2) * (rows // 2), 128)
        copies.append(
            pltpu.make_async_copy(
                atoms.at[pl.ds(first, 2 * HALO)],
                ref.at[pl.ds(PAIR_ROWS, 2 * HALO)],
                sems.at[3 + n * 3 + 2],
            )
        )
    for copy in copies:
        copy.start()
    for copy in copies[:3]:
        copy.wait()
    size = counts.shape[1]
    lanes = lax.broadcasted_iota(jnp.int32, (1, size), 1)
    many = jnp.where(lanes == size - 1, counts[...].astype(F32), 0.0)
    many = jnp.sum(many, -1, keepdims=True)
    last = grad[16:32, :].astype(F32)[15:16, :]
    row = lax.broadcasted_iota(jnp.int32, (16, 128), 0)
    lane = lax.broadcasted_iota(jnp.int32, (16, 128), 1)
    group = jnp.where(row == 3, jnp.broadcast_to(many, (16, 128)), 0.0)
    for k in range(3):
        piece = jnp.broadcast_to(last[:, k * 128 : (k + 1) * 128], (16, 128))
        group = jnp.where(row == k, piece, group)
    for n, ref in enumerate((near, far)):
        value = group
        for m in range(2):
            place = jnp.logical_and(row == 4, lane == m)
            value = jnp.where(place, shift[bases[n] + m].astype(F32), value)
        ref[ATOM_ROWS:MESSAGE, :] = value.astype(BF16)
    lane = lax.broadcasted_iota(jnp.int32, (1, 128), 1)
    shifts = jnp.zeros((1, 128), jnp.int32)
    for j in range(blocks):
        shifts = jnp.where(lane == j, shift[j], shifts)
    shift_row[...] = shifts
    for copy in copies[3:]:
        copy.wait()


def first_kernel(
    atoms, gain, weight, shift, token, counts, normed, q, kv, gate, shift_here, token_here, counts_here
):
    shift_here[...] = shift[...]
    token_here[...] = token[...]
    counts_here[...] = counts[...]
    unit, _ = stats(atoms[...].astype(F32))
    normed[...] = (unit * gain[0:1, :]).astype(BF16)
    projected = nn(normed[...], weight[0])
    q[...] = projected[:, 0:128].astype(BF16)
    kv[...] = projected[:, 128:384].astype(BF16)
    gate[...] = sigmoid(projected[:, 384:512])


def block_bias(weight, layers, part):
    totals = [[None] * HEADS for _ in layers]
    for c in range(16):
        value = part(c)
        for n, layer in enumerate(layers):
            for h in range(HEADS):
                term = value * weight[layer, h, c]
                totals[n][h] = term if c == 0 else totals[n][h] + term
    return totals


def bias_kernel(weight, pair, first, later):
    def block(j, carry):
        totals = block_bias(
            weight, (0, 1), lambda c: pair[j, c * 32 : (c + 1) * 32, :].astype(F32)
        )
        for ref, total in zip((first, later), totals):
            for h in range(HEADS):
                ref[j, h * 32 : (h + 1) * 32, :] = total[h]
        return carry

    lax.fori_loop(0, pair.shape[0], block, 0)


def load_window(kv, keys, values):
    keys[...] = kv[:, 0:128].astype(F32)
    values[...] = kv[:, 128:256].astype(F32)


def windows(at, shifts, q, keys, values, margin):
    mask = head_mask(128)
    spans = [pl.ds(j * QBLK + shift + margin, KWIN) for j, shift in zip(at, shifts)]
    wide = [stacked(block, mask) for block in q]
    key = [keys[span, :].astype(BF16) for span in spans]
    value = [values[span, :].astype(BF16) for span in spans]
    return spans, wide, key, value


def blocks_of(array, at):
    return [array[j * QBLK : (j + 1) * QBLK, :] for j in at]


def attention_forward(at, shifts, found, bias, first, atom_total):
    _, wide, key, value = found
    count = len(wide)
    mask = head_mask(128)
    lane = lax.broadcasted_iota(jnp.int32, (1, KWIN), 1)
    scores = [nt(wide[n], key[n]) for n in range(count)]
    chances = []
    for n in range(count):
        query = first + at[n] * QBLK
        place = query + shifts[n] + lane
        inside = jnp.logical_and(place >= 0, place < atom_total)
        weights = jnp.where(inside, jnp.exp(scores[n] * (32.0**-0.5) + bias[n]), 0.0)
        real = jnp.logical_and(query >= 0, query < atom_total)
        size = jnp.where(real, jnp.sum(weights, -1, keepdims=True), 1.0)
        chances.append(weights * (1.0 / size))
    out = [nn(chances[n].astype(BF16), value[n]) for n in range(count)]
    return chances, [picked(v, mask).astype(BF16) for v in out]


def attention_backward(found, chances, grad_att, own, grad_q, grad_keys, grad_values, score_grad):
    spans, wide, key, value = found
    count = len(wide)
    mask = head_mask(128)
    out = [stacked(block, mask) for block in blocks_of(grad_att, range(count))]
    rising = [nt(out[n], value[n]) for n in range(count)]
    value_back = [tn(chances[n].astype(BF16), out[n]) for n in range(count)]
    scaled = []
    for n in range(count):
        term = chances[n] * rising[n].astype(BF16).astype(F32)
        grad_score = term - chances[n] * jnp.sum(term, -1, keepdims=True)
        if own[n] is not None:
            score_grad[own[n]] = grad_score.astype(BF16)
        scaled.append((grad_score * (32.0**-0.5)).astype(BF16))
    query_back = [None if own[n] is None else nn(scaled[n], key[n]) for n in range(count)]
    key_back = [tn(scaled[n], wide[n]) for n in range(count)]
    for n in range(count):
        if own[n] is not None:
            rows = slice(own[n] * QBLK, (own[n] + 1) * QBLK)
            grad_q[rows, 0:128] = picked(query_back[n], mask).astype(BF16)
    for n in range(count):
        grad_keys[spans[n], :] += key_back[n].astype(BF16).astype(F32)
        grad_values[spans[n], :] += value_back[n].astype(BF16).astype(F32)


INNER = (2, 3, 4, 5)


def inner_kernel(atom_total, shift, q, kv, bias, chances, att, keys, values):
    load_window(kv, keys, values)
    shifts = [shift[0, j] for j in INNER]
    found = windows(INNER, shifts, blocks_of(q, INNER), keys, values, 0)
    first = lax.axis_index("seq") * q.shape[0]
    kept, attended = attention_forward(
        INNER, shifts, found, [bias[j] for j in INNER], first, atom_total
    )
    for n, chance in enumerate(kept):
        chances[n] = chance
    att[...] = jnp.concatenate(attended, 0)


def share_scores(scores, parts):
    y = lax.axis_index("samp") // 2
    for k, ref in enumerate(parts):
        for n, score in enumerate(scores):
            ref[n * 2 : n * 2 + 2] = score[pl.ds(lax.rem(y + k, 4) * 2, 2)]


def forward_kernel(
    atom_total,
    shift,
    channel_weight,
    q,
    kv,
    near,
    far,
    bias,
    gate,
    atoms,
    weight_out,
    gain,
    weight_in,
    att_inner,
    state,
    chances,
    att,
    kv_all,
    q_all,
    gate_all,
    shift_all,
    normed,
    q_next,
    kv_next,
    gate_next,
    keys,
    values,
):
    blocks, rows = bias.shape[0], q.shape[0]
    edge = HALO // QBLK
    first = lax.axis_index("seq") * rows
    there = slice(PAIR_ROWS, ATOM_ROWS)
    before, after = from_before(near[there], far[there]), from_after(near[there], far[there])
    beside = jnp.concatenate([before, after], 0)
    unit, _ = stats(beside)
    projected = nn((unit * gain[0:1, :]).astype(BF16), weight_in[0])
    for ref, at in ((keys, 128), (values, 256)):
        ref[0 : 2 * HALO, :] = projected[0 : 2 * HALO, at : at + 128].astype(BF16).astype(F32)
        ref[2 * HALO : 2 * HALO + rows, :] = kv[:, at - 128 : at].astype(F32)
        ref[2 * HALO + rows :, :] = projected[2 * HALO :, at : at + 128].astype(BF16).astype(F32)
    kv_all[:, 0:128] = keys[...].astype(BF16)
    kv_all[:, 128:256] = values[...].astype(BF16)
    ends = slice(HALO, 2 * HALO), slice(2 * HALO, 3 * HALO)
    queries = [projected[end, 0:128].astype(BF16) for end in ends]
    queries = jnp.concatenate([queries[0], q[...], queries[1]], 0)
    gates = [sigmoid(projected[end, 384:512]) for end in ends]
    gates = jnp.concatenate([gates[0], gate[...], gates[1]], 0)
    q_all[...] = queries
    gate_all[...] = gates
    began = jnp.concatenate([beside[ends[0]], atoms[...].astype(F32), beside[ends[1]]], 0)
    biases, shifts = [], []
    tail = slice(ATOM_ROWS, MESSAGE)
    row = lax.broadcasted_iota(jnp.int32, (16, 128), 0)
    lane = lax.broadcasted_iota(jnp.int32, (16, 128), 1)
    for pick in (from_before, from_after):
        group = pick(near[tail], far[tail])
        for m in range(edge):
            chosen = jnp.where(jnp.logical_and(row == 4, lane == m), group, 0.0)
            value = jnp.sum(chosen).astype(jnp.int32)
            shifts.append(jnp.clip(value, -HALO, QBLK + HALO - KWIN))

            def part(c):
                span = slice(m * 512 + c * 32, m * 512 + (c + 1) * 32)
                return pick(near[span], far[span])

            (total,) = block_bias(channel_weight, (0,), part)
            biases.append(jnp.concatenate(total, 0))
    biases = biases[:edge] + [bias[j] for j in range(blocks)] + biases[edge:]
    shifts = shifts[:edge] + [shift[0, j] for j in range(blocks)] + shifts[edge:]
    lanes = lax.broadcasted_iota(jnp.int32, (1, 128), 1)
    row_of = jnp.zeros((1, 128), jnp.int32)
    for j, value in enumerate(shifts):
        row_of = jnp.where(lanes == j, value, row_of)
    shift_all[...] = row_of
    outer = [j for j in range(len(shifts)) if j - edge not in INNER]
    near_shifts = [shifts[j] for j in outer]
    found = windows(outer, near_shifts, blocks_of(queries, outer), keys, values, HALO)
    kept, attended = attention_forward(
        outer, near_shifts, found, [biases[j] for j in outer], first - HALO, atom_total
    )
    for n, chance in enumerate(kept):
        chances[n] = chance
    half = len(attended) // 2
    attended = jnp.concatenate([*attended[:half], att_inner[...], *attended[half:]], 0)
    att[...] = attended
    done = began + gates * nn(attended, weight_out[0])
    state[...] = done
    unit, _ = stats(done)
    normed_all = (unit * gain[1:2, :]).astype(BF16)
    normed[...] = normed_all[HALO : HALO + rows]
    projected = nn(normed_all, weight_in[1])
    place = first - HALO + lax.broadcasted_iota(jnp.int32, (rows + 2 * HALO, 1), 0)
    inside = jnp.logical_and(place >= 0, place < atom_total)
    kv_next[...] = jnp.where(inside, projected[:, 128:384], 0.0).astype(BF16)
    q_next[...] = projected[HALO : HALO + rows, 0:128].astype(BF16)
    gate_next[...] = sigmoid(projected[HALO : HALO + rows, 384:512])


def send_halo(grad_keys, grad_values, grad_q, grad_gate, grad_state, center, outgoing, near, far):
    rows = center.shape[0]
    ends = []
    for own, other in ((slice(0, HALO), 0), (slice(rows - HALO, rows), HALO + rows)):
        there = slice(other, other + HALO)
        here = slice(HALO + own.start, HALO + own.stop)
        parts = [grad_keys[there, :], grad_values[there, :], grad_keys[here, :]]
        parts += [grad_values[here, :], grad_q[own, :].astype(F32), grad_gate[own, :].astype(F32)]
        ends.append(jnp.concatenate([*parts, grad_state[own, :]], 1))
    near[...] = jnp.where(odd_core(), ends[0], ends[1]).astype(BF16)
    far[...] = jnp.where(odd_core(), ends[1], ends[0]).astype(BF16)
    outgoing[0:HALO, :] = ends[0][:, 0:256].astype(BF16)
    outgoing[HALO:, :] = ends[1][:, 0:256].astype(BF16)
    for ref, at in ((grad_keys, 0), (grad_values, 128)):
        center[:, at : at + 128] = ref[HALO : HALO + rows, :]


def middle_kernel(
    atom_total,
    shift,
    q,
    kv,
    bias,
    gate,
    state,
    weight_out,
    weight_token,
    grad,
    counts,
    atom_token,
    near_first,
    far_first,
    att,
    grad_update,
    narrow_state,
    grad_hidden,
    grad_state,
    grad_gate,
    grad_q,
    center,
    outgoing,
    grad_near,
    grad_far,
    score_grad,
    keys,
    values,
    grad_keys,
    grad_values,
):
    load_window(kv, keys, values)
    shifts = [shift[0, j + HALO // QBLK] for j in range(bias.shape[0])]
    at = range(bias.shape[0])
    found = windows(at, shifts, blocks_of(q, at), keys, values, HALO)
    first = lax.axis_index("seq") * q.shape[0]
    chances, attended = attention_forward(
        at, shifts, found, [bias[j] for j in at], first, atom_total
    )
    attended = jnp.concatenate(attended, 0)
    att[...] = attended
    update = nn(attended, weight_out[1])
    after = (state[HALO : HALO + q.shape[0], :] + gate[...] * update).astype(BF16)
    narrow_state[...] = after
    tokens = grad.shape[0]
    atoms = q.shape[0]
    place = atom_token[...] - lax.axis_index("seq") * tokens
    place = jnp.where(place < 0, tokens + 15, place)
    chosen = lax.broadcasted_iota(jnp.int32, (tokens + 16, atoms), 0) == place
    chosen = jnp.where(chosen, 1.0, 0.0).astype(BF16)
    own = jnp.concatenate([grad[...], count_rows(counts[...]).astype(BF16)], 1)
    group = from_before(near_first[ATOM_ROWS:MESSAGE, :], far_first[ATOM_ROWS:MESSAGE, :])
    before = [jnp.broadcast_to(group[k : k + 1], (16, 128)) for k in range(4)]
    before = jnp.concatenate(before, 1).astype(BF16)
    taken = tn(chosen, jnp.concatenate([own, before], 0))
    many = taken[:, 384:512]
    cotangent = taken[:, 0:384] / jnp.concatenate([many] * 3, 1)
    hidden = nn(after, weight_token[...])
    open_ = sigmoid(hidden)
    back = (cotangent * (open_ * (1.0 + hidden * (1.0 - open_)))).astype(BF16)
    grad_hidden[...] = back
    rising = nt(back, weight_token[...]).astype(BF16).astype(F32)
    grad_state[...] = rising
    gates = gate[...]
    grad_gate[...] = (rising * update * gates * (1.0 - gates)).astype(BF16)
    change = (rising * gates).astype(BF16)
    grad_update[...] = change
    grad_att = nt(change, weight_out[1]).astype(BF16)
    grad_keys[...] = jnp.zeros_like(grad_keys)
    grad_values[...] = jnp.zeros_like(grad_values)
    attention_backward(found, chances, grad_att, at, grad_q, grad_keys, grad_values, score_grad)
    send_halo(
        grad_keys,
        grad_values,
        grad_q,
        grad_gate,
        grad_state,
        center,
        outgoing,
        grad_near,
        grad_far,
    )


def pair_weight_grad(pair, scores, out):
    left = [pair[block] for block, _ in scores]
    product = nt(jnp.concatenate(left, 1), jnp.concatenate([piece for _, piece in scores], 1))
    row = lax.rem(lax.broadcasted_iota(jnp.int32, product.shape, 0), QBLK)
    lane = lax.rem(lax.broadcasted_iota(jnp.int32, product.shape, 1), QBLK)
    product = jnp.where(row == lane, product, 0.0)
    for c in range(16):
        out[c : c + 1, :] = jnp.sum(product[c * 32 : (c + 1) * 32], 0, keepdims=True)


def middle_weights_kernel(
    pair, scores, narrow_state, grad_hidden, att, grad_update, token, out, bias
):
    pair_weight_grad(pair, [(j, scores[j]) for j in range(pair.shape[0])], bias)
    product = tn(narrow_state[...], grad_hidden[...])
    for m in range(3):
        token[m * 128 : (m + 1) * 128, :] = product[:, m * 128 : (m + 1) * 128]
    out[...] = tn(att[...], grad_update[...])


def norm_back(grad_normed, state, gain):
    unit, scale = stats(state)
    back = grad_normed * gain
    back = scale * (
        back - jnp.mean(back, -1, keepdims=True) - unit * jnp.mean(back * unit, -1, keepdims=True)
    )
    return back, grad_normed * unit


def inner_back_kernel(
    shift,
    grad_q_later,
    center_later,
    grad_gate_later,
    state,
    gain,
    weight_in,
    grad_state_later,
    q,
    kv,
    gate,
    weight_out,
    chances,
    grad_gain,
    rising_inner,
    grad_q,
    score_grad,
    grad_keys,
    grad_values,
    keys,
    values,
):
    rows = center_later.shape[0]
    edge = HALO // QBLK
    inner = slice(HALO, rows - HALO)
    wide = slice(2 * HALO, rows)
    load_window(kv[2 * HALO : 2 * HALO + rows, :], keys, values)
    parts = [grad_q_later[inner, :], center_later[inner, :].astype(BF16), grad_gate_later[inner, :]]
    joined = jnp.concatenate(parts, 1)
    grad_normed = nt(joined, weight_in[1]).astype(BF16).astype(F32)
    back, gained = norm_back(grad_normed, state[wide, :], gain[1:2, :])
    grad_gain[...] = jnp.sum(gained, 0, keepdims=True)
    rising = grad_state_later[inner, :] + back
    rising_inner[...] = rising
    grad_att = nt((rising * gate[wide, :]).astype(BF16), weight_out[0]).astype(BF16)
    shifts = [shift[0, j + edge] for j in INNER]
    queries = blocks_of(q, [j + edge for j in INNER])
    found = windows(INNER, shifts, queries, keys, values, 0)
    grad_keys[...] = jnp.zeros_like(grad_keys)
    grad_values[...] = jnp.zeros_like(grad_values)
    kept = [chances[n] for n in range(len(INNER))]
    own = range(len(INNER))
    attention_backward(found, kept, grad_att, own, grad_q, grad_keys, grad_values, score_grad)


def backward_kernel(
    shift,
    grad_q_later,
    center_later,
    outgoing,
    near,
    far,
    grad_gate_later,
    state,
    gain,
    weight_in,
    grad_state_later,
    q,
    kv,
    gate,
    att,
    weight_out,
    chances,
    atoms,
    gain_inner,
    rising_inner,
    grad_q_inner,
    score_inner,
    keys_inner,
    values_inner,
    joined_later,
    joined,
    grad_gain,
    grad_update,
    score_grad,
    grad_atoms,
    joined_all,
    keys,
    values,
    grad_keys,
    grad_values,
):
    rows = center_later.shape[0]
    edge = HALO // QBLK
    own = slice(HALO, HALO + rows)
    load_window(kv, keys, values)
    before, after = from_before(near[...], far[...]), from_after(near[...], far[...])
    for place, part, other in ((0, before, 0), (HALO + rows, after, HALO)):
        there = slice(place, place + HALO)
        joined_all[there, 0:128] = part[:, 512:640].astype(BF16)
        shares = part[:, 256:512] + outgoing[other : other + HALO, :].astype(F32)
        joined_all[there, 128:384] = shares.astype(BF16)
        joined_all[there, 384:512] = part[:, 640:768].astype(BF16)
    received = jnp.concatenate(
        [before[:, 0:256], jnp.zeros((rows - 2 * HALO, 256), F32), after[:, 0:256]], 0
    )
    joined_all[own, 0:128] = grad_q_later[...]
    joined_all[own, 128:384] = (center_later[...] + received).astype(BF16)
    joined_all[own, 384:512] = grad_gate_later[...]
    joined_later[...] = joined_all[own, :]
    ends = slice(0, 2 * HALO), slice(rows, rows + 2 * HALO)

    def outer_of(array):
        return jnp.concatenate([array[end, :] for end in ends], 0)

    grad_normed = nt(outer_of(joined_all), weight_in[1]).astype(BF16).astype(F32)
    back, gained = norm_back(grad_normed, outer_of(state), gain[1:2, :])
    gained = jnp.sum(gained[HALO : 3 * HALO], 0, keepdims=True)
    grad_gain[1:2, :] = gained + gain_inner[...]
    rising = [before[:, 768:896], grad_state_later[0:HALO, :]]
    rising += [grad_state_later[rows - HALO : rows, :], after[:, 768:896]]
    rising = jnp.concatenate(rising, 0) + back
    grad_att = nt((rising * outer_of(gate)).astype(BF16), weight_out[0]).astype(BF16)
    rising = jnp.concatenate(
        [rising[HALO : 2 * HALO], rising_inner[...], rising[2 * HALO : 3 * HALO]], 0
    )
    gates = gate[own, :]
    grad_update[...] = (rising * gates).astype(BF16)
    update = nn(att[own, :], weight_out[0])
    joined[:, 384:512] = (rising * update * gates * (1.0 - gates)).astype(BF16)
    count = rows // QBLK
    outer = [j for j in range(count + 2 * edge) if j - edge not in INNER]
    shifts = [shift[0, j] for j in outer]
    found = windows(outer, shifts, blocks_of(q, outer), keys, values, HALO)
    kept = [chances[n] for n in range(len(outer))]
    mine = [j - edge if 0 <= j - edge < count else None for j in outer]
    for ref, first in ((grad_keys, keys_inner), (grad_values, values_inner)):
        ref[0 : 2 * HALO, :] = jnp.zeros((2 * HALO, 128), F32)
        ref[2 * HALO : 2 * HALO + rows, :] = first[...]
        ref[2 * HALO + rows :, :] = jnp.zeros((2 * HALO, 128), F32)
    attention_backward(found, kept, grad_att, mine, joined, grad_keys, grad_values, score_grad)
    joined[HALO : rows - HALO, 0:128] = grad_q_inner[...]
    for n, j in enumerate(INNER):
        score_grad[j] = score_inner[n]
    inner = slice(2 * HALO, 2 * HALO + rows)
    joined[:, 128:256] = grad_keys[inner, :].astype(BF16)
    joined[:, 256:384] = grad_values[inner, :].astype(BF16)
    grad_normed = nt(joined[...], weight_in[0]).astype(BF16).astype(F32)
    back, gained = norm_back(grad_normed, atoms[...].astype(F32), gain[0:1, :])
    grad_gain[0:1, :] = jnp.sum(gained, 0, keepdims=True)
    grad_atoms[...] = (rising + back).astype(BF16)


EARLY = 144
EXTRA = 160
SPAN = 224


def backward_weights_kernel(
    pair,
    scores,
    normed_first,
    joined_first,
    normed,
    joined,
    att,
    grad_update,
    token,
    out_later,
    bias_later,
    grad_gain,
    scores_later,
    keep,
    send,
    own,
    one,
    two,
    three,
    whole,
):
    share_scores((scores, scores_later), (own, one, two, three))

    def put(row, value):
        whole[row // EARLY, row % EARLY : row % EARLY + 16, :] = value

    for r in range(0, 384, 16):
        put(r, token[r : r + 16, :])
    for r in range(0, 128, 16):
        put(384 + r, out_later[r : r + 16, :])
    inner = tn(normed[...], joined[...])
    for m in range(4):
        for r in range(0, 128, 16):
            put(512 + m * 128 + r, inner[r : r + 16, m * 128 : (m + 1) * 128])
    out = tn(att[HALO : HALO + joined.shape[0], :], grad_update[...])
    for r in range(0, 128, 16):
        put(1024 + r, out[r : r + 16, :])
    for m in range(2, 8):
        whole[m, EARLY:EXTRA, :] = jnp.zeros((16, 128), F32)
    pair_weight_grad(
        pair, [(j, scores[j]) for j in range(pair.shape[0])], whole.at[0, EARLY:EXTRA]
    )
    whole[1, EARLY:EXTRA, :] = bias_later[...]
    whole[2, EARLY : EARLY + 1, :] = grad_gain[0:1, :]
    whole[3, EARLY : EARLY + 1, :] = grad_gain[1:2, :]
    inner = tn(normed_first[...], joined_first[...])
    for m in range(8):
        half = (m % 2) * 64
        whole[m, EXTRA:SPAN, :] = inner[half : half + 64, (m // 2) * 128 : (m // 2 + 1) * 128]
    core = lax.rem(lax.axis_index("seq"), 2)
    keep[...] = whole[pl.ds(core * 4, 4)]
    send[...] = whole[pl.ds((1 - core) * 4, 4)].astype(BF16)


def core_kernel(keep, got, own, one, two, three, whole):
    whole[...] = keep[...] + got[...].astype(F32)
    y = lax.axis_index("samp") // 2
    own[...] = whole[y]
    for k, ref in enumerate((one, two, three)):
        ref[...] = whole[lax.rem(y + k + 1, 4)].astype(BF16)


def far_kernel(own, one, two, three, score, score_one, score_two, score_three, message, kept, both):
    got = [ref[...].astype(F32) for ref in (one, two, three)]
    message[0:SPAN, :] = pair_up(own[...], got).astype(BF16)
    for n in range(2):
        for m in range(2):
            got = [v[n * 2 + m].astype(F32) for v in (score_one, score_two, score_three)]
            both[m, n] = pair_up(score[n * 2 + m].astype(F32), got)
    side = lax.rem(lax.axis_index("samp"), 2)
    kept[...] = both[side]
    away = both[1 - side].astype(BF16)
    for n in range(2):
        message[SPAN + n * 128 : SPAN + (n + 1) * 128, :] = away[n]


def quarter_kernel(own, one, two, three, half):
    y = lax.axis_index("samp") // 2
    half[y] = own[...]
    for k, ref in enumerate((one, two, three)):
        half[lax.rem(y + 3 - k, 4)] = ref[...]


def finish_kernel(half, got, grad_gain, inner, out, bias, token):
    def finish(lower, upper):
        def chunk(m):
            return (lower if m < 4 else upper).at[m % 4]

        def rows(row):
            return chunk(row // EARLY)[row % EARLY : row % EARLY + 16, :].astype(F32)

        def take(ref, base, blocks):
            for m in range(blocks):
                for r in range(0, 128, 16):
                    ref[r : r + 16, m * 128 : (m + 1) * 128] = rows(base + m * 128 + r)

        take(token, 0, 3)
        take(out.at[1], 384, 1)
        take(inner.at[1], 512, 4)
        take(out.at[0], 1024, 1)
        for m in range(8):
            half_rows = (m % 2) * 64
            inner[0, half_rows : half_rows + 64, (m // 2) * 128 : (m // 2 + 1) * 128] = chunk(m)[
                EXTRA:SPAN, :
            ].astype(F32)
        for layer in range(2):
            grad_gain[layer : layer + 1, :] = chunk(2 + layer)[EARLY:EXTRA, :].astype(F32)[0:1]
            head = lax.broadcasted_iota(jnp.int32, (HEADS, 128), 0)
            lane = lax.broadcasted_iota(jnp.int32, (HEADS, 128), 1) // QBLK
            choose = jnp.where(head == lane, 1.0, 0.0).astype(BF16)
            bias[layer] = nt(choose, chunk(layer)[EARLY:EXTRA, :])

    odd = odd_core()

    @pl.when(jnp.logical_not(odd))
    def _():
        finish(half, got)

    @pl.when(odd)
    def _():
        finish(got, half)


def expand_kernel(weight, kept, got, pair):
    first = kept[0] + got[SPAN : SPAN + 128, :].astype(F32)
    later = kept[1] + got[SPAN + 128 : SPAN + 256, :].astype(F32)
    for c in range(16):
        value = None
        for layer, ref in enumerate((first, later)):
            for h in range(HEADS):
                term = ref[h * 32 : (h + 1) * 32] * weight[layer, h, c]
                value = term if value is None else value + term
        pair[c * 32 : (c + 1) * 32, :] = value.astype(BF16)


def body(
    atoms_in,
    pair_feats,
    window_shift,
    atom_token,
    token_counts,
    token_grad,
    norm_gain,
    weight_in,
    weight_out,
    weight_bias,
    weight_token,
):
    rows = atoms_in.shape[1]
    blocks = pair_feats.shape[0]
    atom_total = rows * lax.axis_size("seq")
    atoms = atoms_in[0]
    grad = token_grad[0]
    pair = pair_feats.reshape(blocks, 512, 128)
    counts = token_counts.reshape(1, -1)
    token_row = atom_token.reshape(1, -1)
    ext = rows + 2 * HALO
    window = [pltpu.VMEM((ext, 128), F32), pltpu.VMEM((ext, 128), F32)]
    square = ((blocks, 128, 128), F32)
    wide = ((rows, 128), BF16)
    full = ((rows, 128), F32)
    kv_shape = ((rows, 256), BF16)
    rim = ((HALO, 896), BF16)
    scores_shape = ((blocks, 128, 128), BF16)
    channel_weight = weight_bias.transpose(0, 2, 1)

    begun = ((MESSAGE, 128), BF16)
    *rims0, shift_row = run(
        message_kernel,
        [begun, begun, ((1, 128), jnp.int32)],
        (window_shift, pair, atoms, grad, counts),
        hbm=range(5),
        scratch=[
            pltpu.SMEM(window_shift.shape, window_shift.dtype),
            pltpu.VMEM(grad.shape, grad.dtype),
            pltpu.VMEM(counts.shape, counts.dtype),
            pltpu.SemaphoreType.DMA((9,)),
        ],
        vmem=FIRST_VMEM,
    )
    rims0 = swapped(*rims0)
    normed0, q0, kv0, gate0, shift_row, token_row, counts = run(
        first_kernel,
        [wide, wide, kv_shape, full]
        + [((1, 128), jnp.int32), (token_row.shape, jnp.int32), (counts.shape, jnp.int32)],
        (atoms, norm_gain, weight_in, shift_row, token_row, counts),
    )
    bias0, bias1 = run(bias_kernel, [square, square], (channel_weight, pair), smem=(0,))
    inner_square = ((len(INNER), 128, 128), F32)
    inner_wide = ((len(INNER) * QBLK, 128), BF16)
    own_window = [pltpu.VMEM((rows, 128), F32)] * 2
    chances_inner, att_inner = run(
        partial(inner_kernel, atom_total),
        [inner_square, inner_wide],
        (shift_row, q0, kv0, bias0),
        smem=(0,),
        scratch=own_window,
    )
    ext_kv = ((ext, 256), BF16)
    more = blocks + 2 * HALO // QBLK - len(INNER)
    broad = ext + 2 * HALO
    state1, chances0, att0, kv0, q0, gate0, shift_row, normed1, q1, kv1, gate1 = run(
        partial(forward_kernel, atom_total),
        [
            ((ext, 128), F32),
            ((more, 128, 128), F32),
            ((ext, 128), BF16),
            ((broad, 256), BF16),
            ((ext, 128), BF16),
            ((ext, 128), F32),
            ((1, 128), jnp.int32),
            wide,
            wide,
            ext_kv,
            full,
        ],
        (
            shift_row,
            channel_weight,
            q0,
            kv0,
            *rims0,
            bias0,
            gate0,
            atoms,
            weight_out,
            norm_gain,
            weight_in,
            att_inner,
        ),
        smem=(0, 1),
        scratch=[pltpu.VMEM((rows + 4 * HALO, 128), F32)] * 2,
    )
    (
        att1,
        grad_update1,
        narrow_state,
        grad_hidden,
        grad_state2,
        grad_gate1,
        grad_q1,
        center1,
        outgoing,
        near1,
        far1,
        scores1,
    ) = run(
        partial(middle_kernel, atom_total),
        [
            wide,
            wide,
            wide,
            ((rows, 384), BF16),
            full,
            wide,
            wide,
            ((rows, 256), F32),
            ((2 * HALO, 256), BF16),
            rim,
            rim,
            scores_shape,
        ],
        (
            shift_row,
            q1,
            kv1,
            bias1,
            gate1,
            state1,
            weight_out,
            weight_token,
            grad,
            counts,
            token_row,
            *rims0,
        ),
        smem=(0,),
        scratch=window + window,
    )
    rims1 = swapped(near1, far1)
    grad_token, grad_out1, grad_bias1 = run(
        middle_weights_kernel,
        [((384, 128), F32), ((128, 128), F32), ((16, 128), F32)],
        (pair, scores1, narrow_state, grad_hidden, att1, grad_update1),
    )
    inner_back = run(
        inner_back_kernel,
        [
            ((1, 128), F32),
            ((len(INNER) * QBLK, 128), F32),
            inner_wide,
            ((len(INNER), 128, 128), BF16),
            full,
            full,
        ],
        (
            shift_row,
            grad_q1,
            center1,
            grad_gate1,
            state1,
            norm_gain,
            weight_in,
            grad_state2,
            q0,
            kv0,
            gate0,
            weight_out,
            chances_inner,
        ),
        smem=(0,),
        scratch=own_window,
    )
    rims1, grad_token = lax.optimization_barrier((rims1, grad_token))
    joined1, joined0, gains, grad_update0, scores0, grad_atoms = run(
        backward_kernel,
        [((rows, 512), BF16), ((rows, 512), BF16), ((2, 128), F32), wide, scores_shape, wide],
        (
            shift_row,
            grad_q1,
            center1,
            outgoing,
            *rims1,
            grad_gate1,
            state1,
            norm_gain,
            weight_in,
            grad_state2,
            q0,
            kv0,
            gate0,
            att0,
            weight_out,
            chances0,
            atoms,
            *inner_back,
        ),
        smem=(0,),
        scratch=[pltpu.VMEM((ext, 512), BF16)] + [pltpu.VMEM((broad, 128), F32)] * 4,
    )
    keep, send, *score_parts = run(
        backward_weights_kernel,
        [((4, SPAN, 128), F32), ((4, SPAN, 128), BF16)] + [((4, 128, 128), BF16)] * 4,
        (
            pair,
            scores0,
            normed0,
            joined0,
            normed1,
            joined1,
            att0,
            grad_update0,
            grad_token,
            grad_out1,
            grad_bias1,
            gains,
            scores1,
        ),
        scratch=[pltpu.VMEM((8, SPAN, 128), F32)],
    )
    chunk = ((SPAN, 128), BF16)
    own, *pieces = run(
        core_kernel,
        [((SPAN, 128), F32), chunk, chunk, chunk],
        (keep, hop(send, 2, 1)),
        scratch=[pltpu.VMEM((4, SPAN, 128), F32)],
    )
    score_got = [hop(score_parts[k], 3, k) for k in range(1, 4)]
    message, kept = run(
        far_kernel,
        [((SPAN + 256, 128), BF16), ((2, 128, 128), F32)],
        (own, *[hop(v, 3, k + 1) for k, v in enumerate(pieces)], score_parts[0], *score_got),
        scratch=[pltpu.VMEM((2, 2, 128, 128), F32)],
    )
    far_got = hop(message, 4, 1)
    total = (message[0:SPAN].astype(F32) + far_got[0:SPAN].astype(F32)).astype(BF16)
    total = everyone(total, 0)
    (pair_sum,) = run(
        expand_kernel, [((512, 128), BF16)], (channel_weight, kept, far_got), smem=(0,)
    )
    total, pair_sum = lax.optimization_barrier((total, pair_sum))
    total = everyone(total, 1)
    (half,) = run(
        quarter_kernel,
        [((4, SPAN, 128), BF16)],
        (total, *[hop(total, 3, k) for k in range(1, 4)]),
    )
    grad_gain, grad_in, grad_out, grad_bias, grad_token = run(
        finish_kernel,
        [
            ((2, 128), F32),
            ((2, 128, 512), F32),
            ((2, 128, 128), F32),
            ((2, 4, 16), F32),
            ((128, 384), F32),
        ],
        (half, hop(half, 2, 1)),
    )
    return (
        grad_atoms[None],
        pair_sum.reshape(1, 16, 32, 128),
        grad_gain,
        grad_in,
        grad_out,
        grad_bias.transpose(0, 2, 1),
        grad_token,
    )


def solution(mesh):
    return jax.shard_map(
        body,
        mesh=mesh,
        in_specs=(
            P("samp", "seq", None),
            P("seq", None, None, None),
            P("seq"),
            P("seq"),
            P("seq"),
            P("samp", "seq", None),
            P(),
            P(),
            P(),
            P(),
            P(),
        ),
        out_specs=(
            P("samp", "seq", None),
            P(("seq", "samp"), None, None, None),
            P(),
            P(),
            P(),
            P(),
            P(),
        ),
        check_vma=False,
    )
```

```python
from functools import partial

import jax
import jax.numpy as jnp
from jax import lax
from jax.experimental import pallas as pl
from jax.experimental.pallas import tpu as pltpu
from jax.sharding import PartitionSpec as P

HALO = 64
KWIN = 128
QBLK = 32
HEADS = 4
EPSILON = 1e-05
F32 = jnp.float32
BF16 = jnp.bfloat16
DIMS = (4, 4, 2, 4, 2)
WORLD = ("seq", "samp")


def moves(part, step):
    pairs = []
    for source in range(256):
        place, rest = [], source
        for size in reversed(DIMS):
            place.append(rest % size)
            rest //= size
        place.reverse()
        place[part] = (place[part] + step) % DIMS[part]
        target = 0
        for size, value in zip(DIMS, place):
            target = target * size + value
        pairs.append((source, target))
    return pairs


def hop(value, part, step):
    return lax.ppermute(value, WORLD, moves(part, step))


def swapped(near, far):
    length = lax.axis_size("seq")
    chip = [(i, i ^ 1) for i in range(length)]
    across = [(i, i - 1 + 2 * (i % 2)) for i in range(length)]
    across = [(i, j) for i, j in across if 0 <= j < length]
    far = lax.ppermute(far, "seq", across)
    return lax.ppermute(near, "seq", chip), far


def pair_up(own, got):
    if len(got) == 1:
        return own + got[0]
    return (own + got[1]) + (got[0] + got[2])


def everyone(value, part):
    got = [hop(value, part, k).astype(F32) for k in range(1, DIMS[part])]
    return pair_up(value.astype(F32), got).astype(BF16)


def run(body, outs, args, smem=(), hbm=(), scratch=(), vmem=24, flops=10**8, nbytes=10**6):
    spaces = [pltpu.VMEM] * len(args)
    for i in smem:
        spaces[i] = pltpu.SMEM
    for i in hbm:
        spaces[i] = pltpu.HBM
    specs = [pl.BlockSpec(memory_space=space) for space in spaces]
    return pl.pallas_call(
        body,
        out_shape=[jax.ShapeDtypeStruct(s, d) for s, d in outs],
        in_specs=specs,
        out_specs=[pl.BlockSpec(memory_space=pltpu.VMEM) for _ in outs],
        scratch_shapes=list(scratch),
        compiler_params=pltpu.CompilerParams(vmem_limit_bytes=int(vmem * 2**20)),
        cost_estimate=pl.CostEstimate(flops=flops, bytes_accessed=nbytes, transcendentals=0),
    )(*args)


def nn(a, b):
    return jnp.dot(a, b, preferred_element_type=F32)


def nt(a, b):
    return lax.dot_general(a, b, (((1,), (1,)), ((), ())), preferred_element_type=F32)


def tn(a, b):
    return lax.dot_general(a, b, (((0,), (0,)), ((), ())), preferred_element_type=F32)


def stats(state):
    centred = state - jnp.mean(state, -1, keepdims=True)
    scale = lax.rsqrt(jnp.mean(centred * centred, -1, keepdims=True) + EPSILON)
    return centred * scale, scale


def sigmoid(value):
    return 1.0 / (1.0 + jnp.exp(-value))


def head_mask(rows):
    row = lax.broadcasted_iota(jnp.int32, (rows, 128), 0) // QBLK
    lane = lax.broadcasted_iota(jnp.int32, (rows, 128), 1) // 32
    return row == lane


def stacked(block, mask):
    return jnp.where(mask, jnp.concatenate([block.astype(F32)] * HEADS, 0), 0.0).astype(BF16)


def picked(wide, mask):
    wide = jnp.where(mask, wide, 0.0)
    return (wide[0:32] + wide[32:64]) + (wide[64:96] + wide[96:128])


def odd_core():
    return lax.rem(lax.axis_index("seq"), 2) == 1


def from_before(near, far):
    return jnp.where(odd_core(), near.astype(F32), far.astype(F32))


def from_after(near, far):
    return jnp.where(odd_core(), far.astype(F32), near.astype(F32))


def count_rows(counts):
    size = counts.shape[1]
    row = lax.broadcasted_iota(jnp.int32, (size, size), 0)
    lane = lax.broadcasted_iota(jnp.int32, (size, size), 1)
    column = jnp.sum(jnp.where(row == lane, counts.astype(F32), 0.0), -1, keepdims=True)
    return jnp.broadcast_to(column, (size, 128))


FIRST_VMEM = 62
PAIR_ROWS = 1024
ATOM_ROWS = PAIR_ROWS + 2 * HALO
MESSAGE = ATOM_ROWS + 16


def message_kernel(
    shift_far, pair, atoms, grad_far, counts_far, near, far, shift_row, shift, grad, counts, sems
):
    blocks, rows = pair.shape[0], atoms.shape[0]
    odd = odd_core()
    copies = [
        pltpu.make_async_copy(a, b, sems.at[i])
        for i, (a, b) in enumerate(((shift_far, shift), (grad_far, grad), (counts_far, counts)))
    ]
    bases = (jnp.where(odd, 0, blocks - 2), jnp.where(odd, blocks - 2, 0))
    for n, ref in enumerate((near, far)):
        for m in range(2):
            copies.append(
                pltpu.make_async_copy(
                    pair.at[bases[n] + m], ref.at[pl.ds(m * 512, 512)], sems.at[3 + n * 3 + m]
                )
            )
        first = pl.multiple_of(bases[n] * QBLK // (rows // 2) * (rows // 2), 128)
        copies.append(
            pltpu.make_async_copy(
                atoms.at[pl.ds(first, 2 * HALO)],
                ref.at[pl.ds(PAIR_ROWS, 2 * HALO)],
                sems.at[3 + n * 3 + 2],
            )
        )
    for copy in copies:
        copy.start()
    for copy in copies[:3]:
        copy.wait()
    size = counts.shape[1]
    lanes = lax.broadcasted_iota(jnp.int32, (1, size), 1)
    many = jnp.where(lanes == size - 1, counts[...].astype(F32), 0.0)
    many = jnp.sum(many, -1, keepdims=True)
    last = grad[16:32, :].astype(F32)[15:16, :]
    row = lax.broadcasted_iota(jnp.int32, (16, 128), 0)
    lane = lax.broadcasted_iota(jnp.int32, (16, 128), 1)
    group = jnp.where(row == 3, jnp.broadcast_to(many, (16, 128)), 0.0)
    for k in range(3):
        piece = jnp.broadcast_to(last[:, k * 128 : (k + 1) * 128], (16, 128))
        group = jnp.where(row == k, piece, group)
    for n, ref in enumerate((near, far)):
        value = group
        for m in range(2):
            place = jnp.logical_and(row == 4, lane == m)
            value = jnp.where(place, shift[bases[n] + m].astype(F32), value)
        ref[ATOM_ROWS:MESSAGE, :] = value.astype(BF16)
    lane = lax.broadcasted_iota(jnp.int32, (1, 128), 1)
    shifts = jnp.zeros((1, 128), jnp.int32)
    for j in range(blocks):
        shifts = jnp.where(lane == j, shift[j], shifts)
    shift_row[...] = shifts
    for copy in copies[3:]:
        copy.wait()


def first_kernel(
    atoms, gain, weight, shift, token, counts, normed, q, kv, gate, shift_here, token_here, counts_here
):
    shift_here[...] = shift[...]
    token_here[...] = token[...]
    counts_here[...] = counts[...]
    unit, _ = stats(atoms[...].astype(F32))
    normed[...] = (unit * gain[0:1, :]).astype(BF16)
    projected = nn(normed[...], weight[0])
    q[...] = projected[:, 0:128].astype(BF16)
    kv[...] = projected[:, 128:384].astype(BF16)
    gate[...] = sigmoid(projected[:, 384:512])


def block_bias(weight, layers, part):
    totals = [[None] * HEADS for _ in layers]
    for c in range(16):
        value = part(c)
        for n, layer in enumerate(layers):
            for h in range(HEADS):
                term = value * weight[layer, h, c]
                totals[n][h] = term if c == 0 else totals[n][h] + term
    return totals


def bias_kernel(weight, pair, first, later):
    def block(j, carry):
        totals = block_bias(
            weight, (0, 1), lambda c: pair[j, c * 32 : (c + 1) * 32, :].astype(F32)
        )
        for ref, total in zip((first, later), totals):
            for h in range(HEADS):
                ref[j, h * 32 : (h + 1) * 32, :] = total[h]
        return carry

    lax.fori_loop(0, pair.shape[0], block, 0)


def load_window(kv, keys, values):
    keys[...] = kv[:, 0:128].astype(F32)
    values[...] = kv[:, 128:256].astype(F32)


def windows(at, shifts, q, keys, values, margin):
    mask = head_mask(128)
    spans = [pl.ds(j * QBLK + shift + margin, KWIN) for j, shift in zip(at, shifts)]
    wide = [stacked(block, mask) for block in q]
    key = [keys[span, :].astype(BF16) for span in spans]
    value = [values[span, :].astype(BF16) for span in spans]
    return spans, wide, key, value


def blocks_of(array, at):
    return [array[j * QBLK : (j + 1) * QBLK, :] for j in at]


def attention_forward(at, shifts, found, bias, first, atom_total):
    _, wide, key, value = found
    count = len(wide)
    mask = head_mask(128)
    lane = lax.broadcasted_iota(jnp.int32, (1, KWIN), 1)
    scores = [nt(wide[n], key[n]) for n in range(count)]
    chances = []
    for n in range(count):
        query = first + at[n] * QBLK
        place = query + shifts[n] + lane
        inside = jnp.logical_and(place >= 0, place < atom_total)
        weights = jnp.where(inside, jnp.exp(scores[n] * (32.0**-0.5) + bias[n]), 0.0)
        real = jnp.logical_and(query >= 0, query < atom_total)
        size = jnp.where(real, jnp.sum(weights, -1, keepdims=True), 1.0)
        chances.append(weights * (1.0 / size))
    out = [nn(chances[n].astype(BF16), value[n]) for n in range(count)]
    return chances, [picked(v, mask).astype(BF16) for v in out]


def attention_backward(found, chances, grad_att, own, grad_q, grad_keys, grad_values, score_grad):
    spans, wide, key, value = found
    count = len(wide)
    mask = head_mask(128)
    out = [stacked(block, mask) for block in blocks_of(grad_att, range(count))]
    rising = [nt(out[n], value[n]) for n in range(count)]
    value_back = [tn(chances[n].astype(BF16), out[n]) for n in range(count)]
    scaled = []
    for n in range(count):
        term = chances[n] * rising[n].astype(BF16).astype(F32)
        grad_score = term - chances[n] * jnp.sum(term, -1, keepdims=True)
        if own[n] is not None:
            score_grad[own[n]] = grad_score.astype(BF16)
        scaled.append((grad_score * (32.0**-0.5)).astype(BF16))
    query_back = [None if own[n] is None else nn(scaled[n], key[n]) for n in range(count)]
    key_back = [tn(scaled[n], wide[n]) for n in range(count)]
    for n in range(count):
        if own[n] is not None:
            rows = slice(own[n] * QBLK, (own[n] + 1) * QBLK)
            grad_q[rows, 0:128] = picked(query_back[n], mask).astype(BF16)
    for n in range(count):
        grad_keys[spans[n], :] += key_back[n].astype(BF16).astype(F32)
        grad_values[spans[n], :] += value_back[n].astype(BF16).astype(F32)


INNER = (2, 3, 4, 5)


def inner_kernel(atom_total, shift, q, kv, bias, chances, att, keys, values):
    load_window(kv, keys, values)
    shifts = [shift[0, j] for j in INNER]
    found = windows(INNER, shifts, blocks_of(q, INNER), keys, values, 0)
    first = lax.axis_index("seq") * q.shape[0]
    kept, attended = attention_forward(
        INNER, shifts, found, [bias[j] for j in INNER], first, atom_total
    )
    for n, chance in enumerate(kept):
        chances[n] = chance
    att[...] = jnp.concatenate(attended, 0)


def share_scores(scores, parts):
    y = lax.axis_index("samp") // 2
    for k, ref in enumerate(parts):
        for n, score in enumerate(scores):
            ref[n * 2 : n * 2 + 2] = score[pl.ds(lax.rem(y + k, 4) * 2, 2)]


def forward_kernel(
    atom_total,
    shift,
    channel_weight,
    q,
    kv,
    near,
    far,
    bias,
    gate,
    atoms,
    weight_out,
    gain,
    weight_in,
    att_inner,
    state,
    chances,
    att,
    kv_all,
    q_all,
    gate_all,
    shift_all,
    normed,
    q_next,
    kv_next,
    gate_next,
    keys,
    values,
):
    blocks, rows = bias.shape[0], q.shape[0]
    edge = HALO // QBLK
    first = lax.axis_index("seq") * rows
    there = slice(PAIR_ROWS, ATOM_ROWS)
    before, after = from_before(near[there], far[there]), from_after(near[there], far[there])
    beside = jnp.concatenate([before, after], 0)
    unit, _ = stats(beside)
    projected = nn((unit * gain[0:1, :]).astype(BF16), weight_in[0])
    for ref, at in ((keys, 128), (values, 256)):
        ref[0 : 2 * HALO, :] = projected[0 : 2 * HALO, at : at + 128].astype(BF16).astype(F32)
        ref[2 * HALO : 2 * HALO + rows, :] = kv[:, at - 128 : at].astype(F32)
        ref[2 * HALO + rows :, :] = projected[2 * HALO :, at : at + 128].astype(BF16).astype(F32)
    kv_all[:, 0:128] = keys[...].astype(BF16)
    kv_all[:, 128:256] = values[...].astype(BF16)
    ends = slice(HALO, 2 * HALO), slice(2 * HALO, 3 * HALO)
    queries = [projected[end, 0:128].astype(BF16) for end in ends]
    queries = jnp.concatenate([queries[0], q[...], queries[1]], 0)
    gates = [sigmoid(projected[end, 384:512]) for end in ends]
    gates = jnp.concatenate([gates[0], gate[...], gates[1]], 0)
    q_all[...] = queries
    gate_all[...] = gates
    began = jnp.concatenate([beside[ends[0]], atoms[...].astype(F32), beside[ends[1]]], 0)
    biases, shifts = [], []
    tail = slice(ATOM_ROWS, MESSAGE)
    row = lax.broadcasted_iota(jnp.int32, (16, 128), 0)
    lane = lax.broadcasted_iota(jnp.int32, (16, 128), 1)
    for pick in (from_before, from_after):
        group = pick(near[tail], far[tail])
        for m in range(edge):
            chosen = jnp.where(jnp.logical_and(row == 4, lane == m), group, 0.0)
            value = jnp.sum(chosen).astype(jnp.int32)
            shifts.append(jnp.clip(value, -HALO, QBLK + HALO - KWIN))

            def part(c):
                span = slice(m * 512 + c * 32, m * 512 + (c + 1) * 32)
                return pick(near[span], far[span])

            (total,) = block_bias(channel_weight, (0,), part)
            biases.append(jnp.concatenate(total, 0))
    biases = biases[:edge] + [bias[j] for j in range(blocks)] + biases[edge:]
    shifts = shifts[:edge] + [shift[0, j] for j in range(blocks)] + shifts[edge:]
    lanes = lax.broadcasted_iota(jnp.int32, (1, 128), 1)
    row_of = jnp.zeros((1, 128), jnp.int32)
    for j, value in enumerate(shifts):
        row_of = jnp.where(lanes == j, value, row_of)
    shift_all[...] = row_of
    outer = [j for j in range(len(shifts)) if j - edge not in INNER]
    near_shifts = [shifts[j] for j in outer]
    found = windows(outer, near_shifts, blocks_of(queries, outer), keys, values, HALO)
    kept, attended = attention_forward(
        outer, near_shifts, found, [biases[j] for j in outer], first - HALO, atom_total
    )
    for n, chance in enumerate(kept):
        chances[n] = chance
    half = len(attended) // 2
    attended = jnp.concatenate([*attended[:half], att_inner[...], *attended[half:]], 0)
    att[...] = attended
    done = began + gates * nn(attended, weight_out[0])
    state[...] = done
    unit, _ = stats(done)
    normed_all = (unit * gain[1:2, :]).astype(BF16)
    normed[...] = normed_all[HALO : HALO + rows]
    projected = nn(normed_all, weight_in[1])
    place = first - HALO + lax.broadcasted_iota(jnp.int32, (rows + 2 * HALO, 1), 0)
    inside = jnp.logical_and(place >= 0, place < atom_total)
    kv_next[...] = jnp.where(inside, projected[:, 128:384], 0.0).astype(BF16)
    q_next[...] = projected[HALO : HALO + rows, 0:128].astype(BF16)
    gate_next[...] = sigmoid(projected[HALO : HALO + rows, 384:512])


def send_halo(grad_keys, grad_values, grad_q, grad_gate, grad_state, center, outgoing, near, far):
    rows = center.shape[0]
    ends = []
    for own, other in ((slice(0, HALO), 0), (slice(rows - HALO, rows), HALO + rows)):
        there = slice(other, other + HALO)
        here = slice(HALO + own.start, HALO + own.stop)
        parts = [grad_keys[there, :], grad_values[there, :], grad_keys[here, :]]
        parts += [grad_values[here, :], grad_q[own, :].astype(F32), grad_gate[own, :].astype(F32)]
        ends.append(jnp.concatenate([*parts, grad_state[own, :]], 1))
    near[...] = jnp.where(odd_core(), ends[0], ends[1]).astype(BF16)
    far[...] = jnp.where(odd_core(), ends[1], ends[0]).astype(BF16)
    outgoing[0:HALO, :] = ends[0][:, 0:256].astype(BF16)
    outgoing[HALO:, :] = ends[1][:, 0:256].astype(BF16)
    for ref, at in ((grad_keys, 0), (grad_values, 128)):
        center[:, at : at + 128] = ref[HALO : HALO + rows, :]


def middle_kernel(
    atom_total,
    shift,
    q,
    kv,
    bias,
    gate,
    state,
    weight_out,
    weight_token,
    grad,
    counts,
    atom_token,
    near_first,
    far_first,
    att,
    grad_update,
    narrow_state,
    grad_hidden,
    grad_state,
    grad_gate,
    grad_q,
    center,
    outgoing,
    grad_near,
    grad_far,
    score_grad,
    keys,
    values,
    grad_keys,
    grad_values,
):
    load_window(kv, keys, values)
    shifts = [shift[0, j + HALO // QBLK] for j in range(bias.shape[0])]
    at = range(bias.shape[0])
    found = windows(at, shifts, blocks_of(q, at), keys, values, HALO)
    first = lax.axis_index("seq") * q.shape[0]
    chances, attended = attention_forward(
        at, shifts, found, [bias[j] for j in at], first, atom_total
    )
    attended = jnp.concatenate(attended, 0)
    att[...] = attended
    update = nn(attended, weight_out[1])
    after = (state[HALO : HALO + q.shape[0], :] + gate[...] * update).astype(BF16)
    narrow_state[...] = after
    tokens = grad.shape[0]
    atoms = q.shape[0]
    place = atom_token[...] - lax.axis_index("seq") * tokens
    place = jnp.where(place < 0, tokens + 15, place)
    chosen = lax.broadcasted_iota(jnp.int32, (tokens + 16, atoms), 0) == place
    chosen = jnp.where(chosen, 1.0, 0.0).astype(BF16)
    own = jnp.concatenate([grad[...], count_rows(counts[...]).astype(BF16)], 1)
    group = from_before(near_first[ATOM_ROWS:MESSAGE, :], far_first[ATOM_ROWS:MESSAGE, :])
    before = [jnp.broadcast_to(group[k : k + 1], (16, 128)) for k in range(4)]
    before = jnp.concatenate(before, 1).astype(BF16)
    taken = tn(chosen, jnp.concatenate([own, before], 0))
    many = taken[:, 384:512]
    cotangent = taken[:, 0:384] / jnp.concatenate([many] * 3, 1)
    hidden = nn(after, weight_token[...])
    open_ = sigmoid(hidden)
    back = (cotangent * (open_ * (1.0 + hidden * (1.0 - open_)))).astype(BF16)
    grad_hidden[...] = back
    rising = nt(back, weight_token[...]).astype(BF16).astype(F32)
    grad_state[...] = rising
    gates = gate[...]
    grad_gate[...] = (rising * update * gates * (1.0 - gates)).astype(BF16)
    change = (rising * gates).astype(BF16)
    grad_update[...] = change
    grad_att = nt(change, weight_out[1]).astype(BF16)
    grad_keys[...] = jnp.zeros_like(grad_keys)
    grad_values[...] = jnp.zeros_like(grad_values)
    attention_backward(found, chances, grad_att, at, grad_q, grad_keys, grad_values, score_grad)
    send_halo(
        grad_keys,
        grad_values,
        grad_q,
        grad_gate,
        grad_state,
        center,
        outgoing,
        grad_near,
        grad_far,
    )


def pair_weight_grad(pair, scores, out):
    left = [pair[block] for block, _ in scores]
    product = nt(jnp.concatenate(left, 1), jnp.concatenate([piece for _, piece in scores], 1))
    row = lax.rem(lax.broadcasted_iota(jnp.int32, product.shape, 0), QBLK)
    lane = lax.rem(lax.broadcasted_iota(jnp.int32, product.shape, 1), QBLK)
    product = jnp.where(row == lane, product, 0.0)
    for c in range(16):
        out[c : c + 1, :] = jnp.sum(product[c * 32 : (c + 1) * 32], 0, keepdims=True)


def middle_weights_kernel(
    pair, scores, narrow_state, grad_hidden, att, grad_update, token, out, bias
):
    pair_weight_grad(pair, [(j, scores[j]) for j in range(pair.shape[0])], bias)
    product = tn(narrow_state[...], grad_hidden[...])
    for m in range(3):
        token[m * 128 : (m + 1) * 128, :] = product[:, m * 128 : (m + 1) * 128]
    out[...] = tn(att[...], grad_update[...])


def norm_back(grad_normed, state, gain):
    unit, scale = stats(state)
    back = grad_normed * gain
    back = scale * (
        back - jnp.mean(back, -1, keepdims=True) - unit * jnp.mean(back * unit, -1, keepdims=True)
    )
    return back, grad_normed * unit


def inner_back_kernel(
    shift,
    grad_q_later,
    center_later,
    grad_gate_later,
    state,
    gain,
    weight_in,
    grad_state_later,
    q,
    kv,
    gate,
    weight_out,
    chances,
    grad_gain,
    rising_inner,
    grad_q,
    score_grad,
    grad_keys,
    grad_values,
    keys,
    values,
):
    rows = center_later.shape[0]
    edge = HALO // QBLK
    inner = slice(HALO, rows - HALO)
    wide = slice(2 * HALO, rows)
    load_window(kv[2 * HALO : 2 * HALO + rows, :], keys, values)
    parts = [grad_q_later[inner, :], center_later[inner, :].astype(BF16), grad_gate_later[inner, :]]
    joined = jnp.concatenate(parts, 1)
    grad_normed = nt(joined, weight_in[1]).astype(BF16).astype(F32)
    back, gained = norm_back(grad_normed, state[wide, :], gain[1:2, :])
    grad_gain[...] = jnp.sum(gained, 0, keepdims=True)
    rising = grad_state_later[inner, :] + back
    rising_inner[...] = rising
    grad_att = nt((rising * gate[wide, :]).astype(BF16), weight_out[0]).astype(BF16)
    shifts = [shift[0, j + edge] for j in INNER]
    queries = blocks_of(q, [j + edge for j in INNER])
    found = windows(INNER, shifts, queries, keys, values, 0)
    grad_keys[...] = jnp.zeros_like(grad_keys)
    grad_values[...] = jnp.zeros_like(grad_values)
    kept = [chances[n] for n in range(len(INNER))]
    own = range(len(INNER))
    attention_backward(found, kept, grad_att, own, grad_q, grad_keys, grad_values, score_grad)


def backward_kernel(
    shift,
    grad_q_later,
    center_later,
    outgoing,
    near,
    far,
    grad_gate_later,
    state,
    gain,
    weight_in,
    grad_state_later,
    q,
    kv,
    gate,
    att,
    weight_out,
    chances,
    atoms,
    gain_inner,
    rising_inner,
    grad_q_inner,
    score_inner,
    keys_inner,
    values_inner,
    joined_later,
    joined,
    grad_gain,
    grad_update,
    score_grad,
    grad_atoms,
    joined_all,
    keys,
    values,
    grad_keys,
    grad_values,
):
    rows = center_later.shape[0]
    edge = HALO // QBLK
    own = slice(HALO, HALO + rows)
    load_window(kv, keys, values)
    before, after = from_before(near[...], far[...]), from_after(near[...], far[...])
    for place, part, other in ((0, before, 0), (HALO + rows, after, HALO)):
        there = slice(place, place + HALO)
        joined_all[there, 0:128] = part[:, 512:640].astype(BF16)
        shares = part[:, 256:512] + outgoing[other : other + HALO, :].astype(F32)
        joined_all[there, 128:384] = shares.astype(BF16)
        joined_all[there, 384:512] = part[:, 640:768].astype(BF16)
    received = jnp.concatenate(
        [before[:, 0:256], jnp.zeros((rows - 2 * HALO, 256), F32), after[:, 0:256]], 0
    )
    joined_all[own, 0:128] = grad_q_later[...]
    joined_all[own, 128:384] = (center_later[...] + received).astype(BF16)
    joined_all[own, 384:512] = grad_gate_later[...]
    joined_later[...] = joined_all[own, :]
    ends = slice(0, 2 * HALO), slice(rows, rows + 2 * HALO)

    def outer_of(array):
        return jnp.concatenate([array[end, :] for end in ends], 0)

    grad_normed = nt(outer_of(joined_all), weight_in[1]).astype(BF16).astype(F32)
    back, gained = norm_back(grad_normed, outer_of(state), gain[1:2, :])
    gained = jnp.sum(gained[HALO : 3 * HALO], 0, keepdims=True)
    grad_gain[1:2, :] = gained + gain_inner[...]
    rising = [before[:, 768:896], grad_state_later[0:HALO, :]]
    rising += [grad_state_later[rows - HALO : rows, :], after[:, 768:896]]
    rising = jnp.concatenate(rising, 0) + back
    grad_att = nt((rising * outer_of(gate)).astype(BF16), weight_out[0]).astype(BF16)
    rising = jnp.concatenate(
        [rising[HALO : 2 * HALO], rising_inner[...], rising[2 * HALO : 3 * HALO]], 0
    )
    gates = gate[own, :]
    grad_update[...] = (rising * gates).astype(BF16)
    update = nn(att[own, :], weight_out[0])
    joined[:, 384:512] = (rising * update * gates * (1.0 - gates)).astype(BF16)
    count = rows // QBLK
    outer = [j for j in range(count + 2 * edge) if j - edge not in INNER]
    shifts = [shift[0, j] for j in outer]
    found = windows(outer, shifts, blocks_of(q, outer), keys, values, HALO)
    kept = [chances[n] for n in range(len(outer))]
    mine = [j - edge if 0 <= j - edge < count else None for j in outer]
    for ref, first in ((grad_keys, keys_inner), (grad_values, values_inner)):
        ref[0 : 2 * HALO, :] = jnp.zeros((2 * HALO, 128), F32)
        ref[2 * HALO : 2 * HALO + rows, :] = first[...]
        ref[2 * HALO + rows :, :] = jnp.zeros((2 * HALO, 128), F32)
    attention_backward(found, kept, grad_att, mine, joined, grad_keys, grad_values, score_grad)
    joined[HALO : rows - HALO, 0:128] = grad_q_inner[...]
    for n, j in enumerate(INNER):
        score_grad[j] = score_inner[n]
    inner = slice(2 * HALO, 2 * HALO + rows)
    joined[:, 128:256] = grad_keys[inner, :].astype(BF16)
    joined[:, 256:384] = grad_values[inner, :].astype(BF16)
    grad_normed = nt(joined[...], weight_in[0]).astype(BF16).astype(F32)
    back, gained = norm_back(grad_normed, atoms[...].astype(F32), gain[0:1, :])
    grad_gain[0:1, :] = jnp.sum(gained, 0, keepdims=True)
    grad_atoms[...] = (rising + back).astype(BF16)


EARLY = 144
EXTRA = 160
SPAN = 224


def backward_weights_kernel(
    pair,
    scores,
    normed_first,
    joined_first,
    normed,
    joined,
    att,
    grad_update,
    token,
    out_later,
    bias_later,
    grad_gain,
    scores_later,
    keep,
    send,
    own,
    one,
    two,
    three,
    whole,
):
    share_scores((scores, scores_later), (own, one, two, three))

    def put(row, value):
        whole[row // EARLY, row % EARLY : row % EARLY + 16, :] = value

    for r in range(0, 384, 16):
        put(r, token[r : r + 16, :])
    for r in range(0, 128, 16):
        put(384 + r, out_later[r : r + 16, :])
    inner = tn(normed[...], joined[...])
    for m in range(4):
        for r in range(0, 128, 16):
            put(512 + m * 128 + r, inner[r : r + 16, m * 128 : (m + 1) * 128])
    out = tn(att[HALO : HALO + joined.shape[0], :], grad_update[...])
    for r in range(0, 128, 16):
        put(1024 + r, out[r : r + 16, :])
    for m in range(2, 8):
        whole[m, EARLY:EXTRA, :] = jnp.zeros((16, 128), F32)
    pair_weight_grad(
        pair, [(j, scores[j]) for j in range(pair.shape[0])], whole.at[0, EARLY:EXTRA]
    )
    whole[1, EARLY:EXTRA, :] = bias_later[...]
    whole[2, EARLY : EARLY + 1, :] = grad_gain[0:1, :]
    whole[3, EARLY : EARLY + 1, :] = grad_gain[1:2, :]
    inner = tn(normed_first[...], joined_first[...])
    for m in range(8):
        half = (m % 2) * 64
        whole[m, EXTRA:SPAN, :] = inner[half : half + 64, (m // 2) * 128 : (m // 2 + 1) * 128]
    core = lax.rem(lax.axis_index("seq"), 2)
    keep[...] = whole[pl.ds(core * 4, 4)]
    send[...] = whole[pl.ds((1 - core) * 4, 4)].astype(BF16)


def core_kernel(keep, got, own, one, two, three, whole):
    whole[...] = keep[...] + got[...].astype(F32)
    y = lax.axis_index("samp") // 2
    own[...] = whole[y]
    for k, ref in enumerate((one, two, three)):
        ref[...] = whole[lax.rem(y + k + 1, 4)].astype(BF16)


def far_kernel(own, one, two, three, score, score_one, score_two, score_three, message, kept, both):
    got = [ref[...].astype(F32) for ref in (one, two, three)]
    message[0:SPAN, :] = pair_up(own[...], got).astype(BF16)
    for n in range(2):
        for m in range(2):
            got = [v[n * 2 + m].astype(F32) for v in (score_one, score_two, score_three)]
            both[m, n] = pair_up(score[n * 2 + m].astype(F32), got)
    side = lax.rem(lax.axis_index("samp"), 2)
    kept[...] = both[side]
    away = both[1 - side].astype(BF16)
    for n in range(2):
        message[SPAN + n * 128 : SPAN + (n + 1) * 128, :] = away[n]


def finish_kernel(own, one, two, three, grad_gain, inner, out, bias, token, whole):
    y = lax.axis_index("samp") // 2
    for k, ref in enumerate((own, one, two, three)):
        at = lax.rem(y + 4 - k, 4)
        for core in range(2):
            whole[core * 4 + at] = ref[core]

    def finish():
        def chunk(m):
            return whole.at[m]

        def rows(row):
            return chunk(row // EARLY)[row % EARLY : row % EARLY + 16, :].astype(F32)

        def take(ref, base, blocks):
            for m in range(blocks):
                for r in range(0, 128, 16):
                    ref[r : r + 16, m * 128 : (m + 1) * 128] = rows(base + m * 128 + r)

        take(token, 0, 3)
        take(out.at[1], 384, 1)
        take(inner.at[1], 512, 4)
        take(out.at[0], 1024, 1)
        for m in range(8):
            half_rows = (m % 2) * 64
            inner[0, half_rows : half_rows + 64, (m // 2) * 128 : (m // 2 + 1) * 128] = chunk(m)[
                EXTRA:SPAN, :
            ].astype(F32)
        for layer in range(2):
            grad_gain[layer : layer + 1, :] = chunk(2 + layer)[EARLY:EXTRA, :].astype(F32)[0:1]
            head = lax.broadcasted_iota(jnp.int32, (HEADS, 128), 0)
            lane = lax.broadcasted_iota(jnp.int32, (HEADS, 128), 1) // QBLK
            choose = jnp.where(head == lane, 1.0, 0.0).astype(BF16)
            bias[layer] = nt(choose, chunk(layer)[EARLY:EXTRA, :])

    finish()


def expand_kernel(weight, kept, got, pair):
    first = kept[0] + got[SPAN : SPAN + 128, :].astype(F32)
    later = kept[1] + got[SPAN + 128 : SPAN + 256, :].astype(F32)
    for c in range(16):
        value = None
        for layer, ref in enumerate((first, later)):
            for h in range(HEADS):
                term = ref[h * 32 : (h + 1) * 32] * weight[layer, h, c]
                value = term if value is None else value + term
        pair[c * 32 : (c + 1) * 32, :] = value.astype(BF16)


def body(
    atoms_in,
    pair_feats,
    window_shift,
    atom_token,
    token_counts,
    token_grad,
    norm_gain,
    weight_in,
    weight_out,
    weight_bias,
    weight_token,
):
    rows = atoms_in.shape[1]
    blocks = pair_feats.shape[0]
    atom_total = rows * lax.axis_size("seq")
    atoms = atoms_in[0]
    grad = token_grad[0]
    pair = pair_feats.reshape(blocks, 512, 128)
    counts = token_counts.reshape(1, -1)
    token_row = atom_token.reshape(1, -1)
    ext = rows + 2 * HALO
    window = [pltpu.VMEM((ext, 128), F32), pltpu.VMEM((ext, 128), F32)]
    square = ((blocks, 128, 128), F32)
    wide = ((rows, 128), BF16)
    full = ((rows, 128), F32)
    kv_shape = ((rows, 256), BF16)
    rim = ((HALO, 896), BF16)
    scores_shape = ((blocks, 128, 128), BF16)
    channel_weight = weight_bias.transpose(0, 2, 1)

    begun = ((MESSAGE, 128), BF16)
    *rims0, shift_row = run(
        message_kernel,
        [begun, begun, ((1, 128), jnp.int32)],
        (window_shift, pair, atoms, grad, counts),
        hbm=range(5),
        scratch=[
            pltpu.SMEM(window_shift.shape, window_shift.dtype),
            pltpu.VMEM(grad.shape, grad.dtype),
            pltpu.VMEM(counts.shape, counts.dtype),
            pltpu.SemaphoreType.DMA((9,)),
        ],
        vmem=FIRST_VMEM,
    )
    rims0 = swapped(*rims0)
    normed0, q0, kv0, gate0, shift_row, token_row, counts = run(
        first_kernel,
        [wide, wide, kv_shape, full]
        + [((1, 128), jnp.int32), (token_row.shape, jnp.int32), (counts.shape, jnp.int32)],
        (atoms, norm_gain, weight_in, shift_row, token_row, counts),
    )
    bias0, bias1 = run(bias_kernel, [square, square], (channel_weight, pair), smem=(0,))
    inner_square = ((len(INNER), 128, 128), F32)
    inner_wide = ((len(INNER) * QBLK, 128), BF16)
    own_window = [pltpu.VMEM((rows, 128), F32)] * 2
    chances_inner, att_inner = run(
        partial(inner_kernel, atom_total),
        [inner_square, inner_wide],
        (shift_row, q0, kv0, bias0),
        smem=(0,),
        scratch=own_window,
    )
    ext_kv = ((ext, 256), BF16)
    more = blocks + 2 * HALO // QBLK - len(INNER)
    broad = ext + 2 * HALO
    state1, chances0, att0, kv0, q0, gate0, shift_row, normed1, q1, kv1, gate1 = run(
        partial(forward_kernel, atom_total),
        [
            ((ext, 128), F32),
            ((more, 128, 128), F32),
            ((ext, 128), BF16),
            ((broad, 256), BF16),
            ((ext, 128), BF16),
            ((ext, 128), F32),
            ((1, 128), jnp.int32),
            wide,
            wide,
            ext_kv,
            full,
        ],
        (
            shift_row,
            channel_weight,
            q0,
            kv0,
            *rims0,
            bias0,
            gate0,
            atoms,
            weight_out,
            norm_gain,
            weight_in,
            att_inner,
        ),
        smem=(0, 1),
        scratch=[pltpu.VMEM((rows + 4 * HALO, 128), F32)] * 2,
    )
    (
        att1,
        grad_update1,
        narrow_state,
        grad_hidden,
        grad_state2,
        grad_gate1,
        grad_q1,
        center1,
        outgoing,
        near1,
        far1,
        scores1,
    ) = run(
        partial(middle_kernel, atom_total),
        [
            wide,
            wide,
            wide,
            ((rows, 384), BF16),
            full,
            wide,
            wide,
            ((rows, 256), F32),
            ((2 * HALO, 256), BF16),
            rim,
            rim,
            scores_shape,
        ],
        (
            shift_row,
            q1,
            kv1,
            bias1,
            gate1,
            state1,
            weight_out,
            weight_token,
            grad,
            counts,
            token_row,
            *rims0,
        ),
        smem=(0,),
        scratch=window + window,
    )
    rims1 = swapped(near1, far1)
    grad_token, grad_out1, grad_bias1 = run(
        middle_weights_kernel,
        [((384, 128), F32), ((128, 128), F32), ((16, 128), F32)],
        (pair, scores1, narrow_state, grad_hidden, att1, grad_update1),
    )
    inner_back = run(
        inner_back_kernel,
        [
            ((1, 128), F32),
            ((len(INNER) * QBLK, 128), F32),
            inner_wide,
            ((len(INNER), 128, 128), BF16),
            full,
            full,
        ],
        (
            shift_row,
            grad_q1,
            center1,
            grad_gate1,
            state1,
            norm_gain,
            weight_in,
            grad_state2,
            q0,
            kv0,
            gate0,
            weight_out,
            chances_inner,
        ),
        smem=(0,),
        scratch=own_window,
    )
    rims1, grad_token = lax.optimization_barrier((rims1, grad_token))
    joined1, joined0, gains, grad_update0, scores0, grad_atoms = run(
        backward_kernel,
        [((rows, 512), BF16), ((rows, 512), BF16), ((2, 128), F32), wide, scores_shape, wide],
        (
            shift_row,
            grad_q1,
            center1,
            outgoing,
            *rims1,
            grad_gate1,
            state1,
            norm_gain,
            weight_in,
            grad_state2,
            q0,
            kv0,
            gate0,
            att0,
            weight_out,
            chances0,
            atoms,
            *inner_back,
        ),
        smem=(0,),
        scratch=[pltpu.VMEM((ext, 512), BF16)] + [pltpu.VMEM((broad, 128), F32)] * 4,
    )
    keep, send, *score_parts = run(
        backward_weights_kernel,
        [((4, SPAN, 128), F32), ((4, SPAN, 128), BF16)] + [((4, 128, 128), BF16)] * 4,
        (
            pair,
            scores0,
            normed0,
            joined0,
            normed1,
            joined1,
            att0,
            grad_update0,
            grad_token,
            grad_out1,
            grad_bias1,
            gains,
            scores1,
        ),
        scratch=[pltpu.VMEM((8, SPAN, 128), F32)],
    )
    chunk = ((SPAN, 128), BF16)
    own, *pieces = run(
        core_kernel,
        [((SPAN, 128), F32), chunk, chunk, chunk],
        (keep, hop(send, 2, 1)),
        scratch=[pltpu.VMEM((4, SPAN, 128), F32)],
    )
    score_got = [hop(score_parts[k], 3, k) for k in range(1, 4)]
    message, kept = run(
        far_kernel,
        [((SPAN + 256, 128), BF16), ((2, 128, 128), F32)],
        (own, *[hop(v, 3, k + 1) for k, v in enumerate(pieces)], score_parts[0], *score_got),
        scratch=[pltpu.VMEM((2, 2, 128, 128), F32)],
    )
    far_got = hop(message, 4, 1)
    total = (message[0:SPAN].astype(F32) + far_got[0:SPAN].astype(F32)).astype(BF16)
    total = everyone(total, 0)
    (pair_sum,) = run(
        expand_kernel, [((512, 128), BF16)], (channel_weight, kept, far_got), smem=(0,)
    )
    total, pair_sum = lax.optimization_barrier((total, pair_sum))
    total = everyone(total, 1)
    other = hop(total, 2, 1)
    odd = odd_core()
    both = jnp.stack([jnp.where(odd, other, total), jnp.where(odd, total, other)])
    grad_gain, grad_in, grad_out, grad_bias, grad_token = run(
        finish_kernel,
        [
            ((2, 128), F32),
            ((2, 128, 512), F32),
            ((2, 128, 128), F32),
            ((2, 4, 16), F32),
            ((128, 384), F32),
        ],
        (both, *[hop(both, 3, k) for k in range(1, 4)]),
        scratch=[pltpu.VMEM((8, SPAN, 128), BF16)],
    )
    return (
        grad_atoms[None],
        pair_sum.reshape(1, 16, 32, 128),
        grad_gain,
        grad_in,
        grad_out,
        grad_bias.transpose(0, 2, 1),
        grad_token,
    )


def solution(mesh):
    return jax.shard_map(
        body,
        mesh=mesh,
        in_specs=(
            P("samp", "seq", None),
            P("seq", None, None, None),
            P("seq"),
            P("seq"),
            P("seq"),
            P("samp", "seq", None),
            P(),
            P(),
            P(),
            P(),
            P(),
        ),
        out_specs=(
            P("samp", "seq", None),
            P(("seq", "samp"), None, None, None),
            P(),
            P(),
            P(),
            P(),
            P(),
        ),
        check_vma=False,
    )
```
